32 devices in a mesh: section: 4 (over z), dp: 2 (over x), mp: 4 (over y, core).
Axes of the slice: x: 2, y: 2, z: 4, core: 2. Of those that a mesh axis runs over, the one named last changes fastest.
Arguments:
- lengths: int32 [16], P(('section', 'dp')), may hold values from 1 to 128
- final_hidden: bfloat16 [16, 3584], P(('section', 'dp')), may hold values from -6 to 6
- score_gain: bfloat16 [3584], replicated, may hold values from 0.5 to 1.5
- score_head: bfloat16 [3584], replicated, may hold values from -0.09375 to 0.09375
- policy_input: bfloat16 [2048, 8192], P(('section', 'dp'), 'mp')
- block_order: int32 [8, 2], P(('section', 'dp')), may hold values from 0 to 1, each once within a row
- norm_gain: bfloat16 [8192], P('mp'), may hold values from 0.5 to 1.5
- key_weight: bfloat16 [8192, 1024], P('mp'), may hold values from -0.0625 to 0.0625
- key_cotangent: bfloat16 [2048, 1024], P(('section', 'dp'), 'mp'), may hold values from -6 to 6
Outputs:
- keys: bfloat16 [2048, 1024], P(('section', 'dp'), 'mp')
- grad_weight: float32 [8192, 1024], P('mp')
- grad_gain: float32 [8192], P('mp')
The draws below stay inside these ranges and needn't reach their ends.
Inputs may be any that keep to these rules, and one draw needn't show every extreme that they name: `block_order`: each row lists every number from 0 to 1 once.
All inputs are finite; a program needn't handle non-finite values.
Results may differ from the reference program's by a relative error of at most 0.0062.
Values may be sent and summed in bfloat16 or wider, within the bound.
No kernel may reach another device: no remote copies, remote signals or barrier semaphores. Data moves between devices by JAX's collectives and lax.ppermute only.
A program may use at most 128 MiB of HBM per device.

```python
import math
import jax
import jax.numpy as jnp
from jax import lax

D = 8192
RD = 3584
BLK = 128
PAIR = 1
RB_DEV = 2
SHARDS = 8
BLOCKS = 16
TOKENS = 2048
KVD = 1024
N_SECTION = 4
N_DP = 2


def draw_policy_input(key, part):
    row_key, col_key, base_key = jax.random.split(key, 3)
    rows = jax.random.uniform(row_key, (TOKENS, 1), jnp.float32)
    cols = jax.random.uniform(col_key, (1, D), jnp.float32)
    ramp = lax.broadcasted_iota(jnp.float32, (1, D), 1) / D
    base = jnp.clip(jax.random.normal(base_key, (TOKENS, D), jnp.float32), -6.0, 6.0)
    scale = jnp.exp(math.log(10.0) * (0.7 * ramp + 0.3 * cols + rows))
    return (base * scale).astype(jnp.bfloat16)


def place_ends(values, key, least, top_value):
    longest = values.shape.index(max(values.shape))
    spots = []
    for shift in (0, 1):
        where = [jax.random.randint(jax.random.fold_in(key, axis), (), 0, length) for axis, length in enumerate(values.shape)]
        where[longest] = (where[longest] + shift) % values.shape[longest]
        spots.append(tuple(where))
    return values.at[spots[0]].set(least).at[spots[1]].set(top_value)


def levels(stream_key, dims, pieces, low, largest):
    def one(axis_at, parts):
        draws = jax.random.uniform(jax.random.fold_in(jax.random.fold_in(stream_key, 6), axis_at), (parts,), jnp.float32, low / len(pieces), largest / len(pieces))
        return jnp.repeat(jnp.exp(draws), dims[axis_at] // parts).reshape((-1,) + (1,) * (len(dims) - axis_at - 1))

    loudness = one(*pieces[0])
    for cut in pieces[1:]:
        loudness = loudness * one(*cut)
    return loudness


def gaussian(own_key, extent, width, limit, cuts=(), kind=jnp.bfloat16):
    result = jax.random.normal(own_key, extent, jnp.float32) * width
    if len(cuts) > 0:
        result = levels(own_key, extent, cuts, -0.22, 0.18) * result
    return jnp.clip(result, min=-limit, max=limit).astype(kind)


def setup_inputs(seed: int = 0) -> dict:
    streams_of = jax.random.split(jax.random.key(seed), 10)
    return {
        "lengths": place_ends(jax.random.randint(streams_of[0], (BLOCKS,), 1, BLK + 1), jax.random.fold_in(streams_of[0], 1), 1, BLK).astype(jnp.int32),
        "final_hidden": gaussian(streams_of[1], (BLOCKS, RD), 1.0, 6.0, ((0, 8),)),
        "score_gain": jnp.clip(1.0 + 0.1 * jax.random.normal(streams_of[2], (RD,), jnp.float32), 0.5, 1.5).astype(jnp.bfloat16),
        "score_head": gaussian(streams_of[3], (RD,), RD ** -0.5, 0.09375),
        "policy_input": draw_policy_input(jax.random.fold_in(streams_of[9], 71), 0),
        "block_order": jax.vmap(lambda own: jax.random.permutation(own, RB_DEV))(jax.random.split(streams_of[5], SHARDS)).reshape((SHARDS, RB_DEV)).astype(jnp.int32),
        "norm_gain": jnp.clip(1.0 + 0.1 * jax.random.normal(streams_of[6], (D,), jnp.float32), 0.5, 1.5).astype(jnp.bfloat16),
        "key_weight": gaussian(streams_of[7], (D, KVD), D ** -0.5, 0.0625, ((0, 4),)),
        "key_cotangent": gaussian(streams_of[8], (TOKENS, KVD), 1.0, 6.0, ((0, 8), (1, 4))),
    }


EPSILON = 1e-06

def reference(lengths, final_hidden, score_gain, score_head, policy_input, block_order, norm_gain, key_weight, key_cotangent):
    hidden_values = final_hidden.astype(jnp.float32)
    inverse_rms = lax.rsqrt(lax.optimization_barrier(jnp.mean(hidden_values * hidden_values, axis=1)) + EPSILON)
    coefficient = score_gain.astype(jnp.float32) * score_head.astype(jnp.float32)
    scores = lax.optimization_barrier(jnp.sum(hidden_values * coefficient[None, :], axis=1)) * inverse_rms
    position = jnp.arange(BLK, dtype=jnp.int32)
    token_weight = jnp.where(position[None, :] < lengths[:, None], scores[:, None], 0.0).astype(jnp.bfloat16)
    source_of = jnp.argsort(block_order, axis=1).astype(jnp.int32)
    section_ids = jnp.arange(N_SECTION, dtype=jnp.int32)[:, None, None, None]
    target = jnp.arange(N_DP, dtype=jnp.int32)[None, :, None, None]
    sender = jnp.arange(N_DP, dtype=jnp.int32)[None, None, :, None]
    within = jnp.arange(PAIR, dtype=jnp.int32)[None, None, None, :]
    shard = section_ids * N_DP + sender
    slot = target * PAIR + within
    block_ids = (shard * RB_DEV + source_of[shard, slot]).reshape(-1).astype(jnp.int32)
    per_shard = block_ids.reshape(SHARDS, RB_DEV)
    blocks_in = policy_input.reshape(BLOCKS, BLK, D)
    gain_values = norm_gain.astype(jnp.float32)

    def shard_step(carry, inputs):
        grad_weight, grad_gain = carry
        chosen, cotangent = inputs
        rows = jnp.take(blocks_in, chosen, axis=0).reshape(-1, D).astype(jnp.float32)
        row_weight = jnp.take(token_weight, chosen, axis=0).reshape(-1).astype(jnp.float32)
        inverse = lax.rsqrt(lax.optimization_barrier(jnp.mean(rows * rows, axis=1, keepdims=True)) + EPSILON)
        scaled = rows * inverse
        normed = (scaled * gain_values[None, :]).astype(jnp.bfloat16)
        projected = jnp.dot(normed, key_weight, preferred_element_type=jnp.float32).astype(jnp.bfloat16)
        key_grad = (cotangent.astype(jnp.float32) * row_weight[:, None]).astype(jnp.bfloat16)
        grad_weight = grad_weight + jnp.dot(normed.T, key_grad, preferred_element_type=jnp.float32)
        grad_normed = jnp.dot(key_grad, key_weight.T, preferred_element_type=jnp.float32)
        grad_gain = grad_gain + lax.optimization_barrier(jnp.sum(grad_normed * scaled, axis=0))
        return ((grad_weight, grad_gain), projected)
    cotangents = key_cotangent.reshape(SHARDS, RB_DEV * BLK, KVD)
    starting = (jnp.zeros((D, KVD), jnp.float32), jnp.zeros((D,), jnp.float32))
    (grad_weight, grad_gain), projected = lax.scan(shard_step, starting, (per_shard, cotangents))
    return (projected.reshape(TOKENS, KVD), grad_weight / SHARDS, grad_gain / SHARDS)
```

```python
import jax
import jax.numpy as jnp
from jax import lax
from jax.sharding import PartitionSpec as P

EPSILON = 1e-06
CHUNKS = 8


def swap(value, axis, bit):
    return lax.ppermute(value, axis, [(i, i ^ bit) for i in range(lax.axis_size(axis))])


def gather_pieces(piece, axis, dimension):
    index = lax.axis_index(axis)
    pieces = [piece]
    bit = lax.axis_size(axis) // 2
    while bit:
        sent = jnp.concatenate(pieces, axis=dimension) if len(pieces) > 1 else pieces[0]
        got = jnp.split(swap(sent, axis, bit), len(pieces), axis=dimension)
        low = (index & bit) == 0
        pieces = [
            value
            for mine, theirs in zip(pieces, got)
            for value in (jnp.where(low, mine, theirs), jnp.where(low, theirs, mine))
        ]
        bit //= 2
    return pieces


def to_bfloat16(value):
    return lax.reduce_precision(value, 8, 7).astype(jnp.bfloat16)


def add(left, right):
    return to_bfloat16(left.astype(jnp.float32) + right.astype(jnp.float32))


def line_sum(part, axis):
    size = lax.axis_size(axis)
    index = lax.axis_index(axis)
    half = size // 2
    for i in range(half - 1):
        part = add(part, lax.ppermute(part, axis, [(i, i + 1), (size - 1 - i, size - 2 - i)]))
    total = add(part, lax.ppermute(part, axis, [(half - 1, half), (half, half - 1)]))
    for i in reversed(range(half - 1)):
        got = lax.ppermute(total, axis, [(i + 1, i), (size - 2 - i, size - 1 - i)])
        total = jnp.where((index == i) | (index == size - 1 - i), got, total)
    return total


def body(
    lengths,
    final_hidden,
    score_gain,
    score_head,
    policy_input,
    block_order,
    norm_gain,
    key_weight,
    key_cotangent,
):
    n_section, n_dp, n_mp = (lax.axis_size(name) for name in ("section", "dp", "mp"))
    dp, mp = lax.axis_index("dp"), lax.axis_index("mp")
    block_count = lengths.shape[0]
    tokens, local_width = policy_input.shape
    block_len = tokens // block_count
    pair = block_count // n_dp
    columns = key_cotangent.shape[1]
    own_width = local_width // n_dp
    order = block_order[0]

    cotangent_rows = jnp.concatenate(gather_pieces(key_cotangent, "dp", 0), axis=0)
    cotangents = jnp.concatenate(gather_pieces(cotangent_rows, "mp", 1), axis=1)

    rows = []
    for j in range(n_dp):
        piece = lax.dynamic_slice_in_dim(policy_input, (dp ^ j) * own_width, own_width, 1)
        rows.append(piece if j == 0 else swap(piece, "dp", j))
    rows = jnp.concatenate(rows, axis=0)

    hidden_values = final_hidden.astype(jnp.float32)
    inverse_hidden = lax.rsqrt(jnp.mean(hidden_values * hidden_values, axis=1) + EPSILON)
    coefficient = score_gain.astype(jnp.float32) * score_head.astype(jnp.float32)
    scores = jnp.sum(hidden_values * coefficient[None, :], axis=1) * inverse_hidden
    squares = jnp.sum(jnp.square(policy_input.astype(jnp.float32)), axis=1)
    small = jnp.concatenate(
        [squares, scores, lengths.astype(jnp.float32), order.astype(jnp.float32)]
    )
    small = lax.all_gather(small, ("dp", "mp")).reshape(n_dp, n_mp, -1)
    squares = jnp.sum(small[:, :, :tokens], axis=1)
    small = small[:, 0, tokens:].reshape(n_dp, 3, block_count)
    inverse = lax.rsqrt(squares / (local_width * n_mp) + EPSILON)
    position = lax.broadcasted_iota(jnp.int32, (n_dp, block_count, block_len), 2)
    token_weight = jnp.where(
        position < small[:, 1, :, None].astype(jnp.int32), small[:, 0, :, None], 0.0
    ).astype(jnp.bfloat16)
    orders = small[:, 2].astype(jnp.int32)

    senders = dp ^ jnp.arange(n_dp)
    slots = orders[senders]
    learner_block = (slots // pair) * block_count + senders[:, None] * pair + slots % pair
    taken = jnp.take(
        cotangents.reshape(n_dp * block_count, block_len, -1), learner_block.reshape(-1), axis=0
    )
    taken_weight = token_weight[senders].reshape(-1, block_len, 1).astype(jnp.float32)
    taken_inverse = inverse[senders].reshape(-1, block_len, 1)
    key_grad = to_bfloat16(taken.astype(jnp.float32) * taken_weight)
    key_grad = (key_grad.astype(jnp.float32) * taken_inverse).astype(jnp.bfloat16)
    key_grad = key_grad.reshape(n_dp * tokens, -1)

    chunk = own_width // CHUNKS
    found = []
    for c in range(CHUNKS):
        part = lax.dot_general(
            rows[:, c * chunk : (c + 1) * chunk],
            key_grad,
            (((0,), (0,)), ((), ())),
            preferred_element_type=jnp.float32,
        )
        found.append(gather_pieces(line_sum(to_bfloat16(part), "section"), "dp", 0))
    shards = n_section * n_dp
    gain = norm_gain.astype(jnp.float32)
    grad_weight = jnp.zeros((local_width, n_mp * columns), jnp.float32)
    grad_gain = jnp.zeros((local_width,), jnp.float32)
    for c in range(CHUNKS):
        for e in range(n_dp):
            start = e * own_width + c * chunk
            value = found[c][e].astype(jnp.float32) / shards
            grad_weight = lax.dynamic_update_slice(
                grad_weight, value * gain[start : start + chunk, None], (start, 0)
            )
            weight = key_weight[start : start + chunk].astype(jnp.float32)
            grad_gain = lax.dynamic_update_slice(
                grad_gain, jnp.sum(value * weight, axis=1), (start,)
            )

    scaled = (policy_input.astype(jnp.float32) * gain[None, :]).astype(jnp.bfloat16)
    partial = jnp.dot(scaled, key_weight, preferred_element_type=jnp.float32)
    own_columns = lax.dynamic_slice_in_dim(partial, mp * columns, columns, 1)
    partial = partial.astype(jnp.bfloat16)
    for j in range(1, n_mp):
        piece = lax.dynamic_slice_in_dim(partial, (mp ^ j) * columns, columns, 1)
        own_columns = own_columns + swap(piece, "mp", j).astype(jnp.float32)
    own_inverse = inverse[dp][:, None]
    keys = jnp.where(own_inverse == 0.0, 0.0, own_columns * own_inverse).astype(jnp.bfloat16)
    block = jnp.arange(block_count)
    source = jnp.sum(jnp.where(order[None, :] == block[:, None], block[None, :], 0), axis=1)
    send = jnp.take(keys.reshape(block_count, block_len, columns), source, axis=0)
    arrived = []
    for j in range(n_dp):
        piece = lax.dynamic_slice_in_dim(send, (dp ^ j) * pair, pair, 0)
        arrived.append(piece if j == 0 else swap(piece, "dp", j))
    learner_keys = jnp.take(jnp.stack(arrived), senders, axis=0).reshape(tokens, columns)
    return learner_keys, grad_weight, grad_gain


def solution(mesh):
    placed = (
        P(("section", "dp")),
        P(("section", "dp"), None),
        P(),
        P(),
        P(("section", "dp"), "mp"),
        P(("section", "dp"), None),
        P("mp"),
        P("mp", None),
        P(("section", "dp"), "mp"),
    )
    return jax.shard_map(
        body,
        mesh=mesh,
        in_specs=placed,
        out_specs=(P(("section", "dp"), "mp"), P("mp", None), P("mp")),
        check_vma=False,
    )
```

```python
import jax
import jax.numpy as jnp
from jax import lax
from jax.sharding import PartitionSpec as P

EPSILON = 1e-06
FEATURE_BLOCKS = 8
LAG = 3


def swap(value, axis, bit):
    return lax.ppermute(value, axis, [(i, i ^ bit) for i in range(lax.axis_size(axis))])


def pick(values, index):
    chosen = values[0]
    for i in range(1, len(values)):
        chosen = jnp.where(index == i, values[i], chosen)
    return chosen


def to_bfloat16(value):
    return lax.reduce_precision(value, 8, 7).astype(jnp.bfloat16)


def add(left, right):
    return to_bfloat16(left.astype(jnp.float32) + right.astype(jnp.float32))


def line_sums(parts, axis):
    if lax.axis_size(axis) != 4:
        return [to_bfloat16(lax.psum(part.astype(jnp.float32), axis)) for part in parts]
    index = lax.axis_index(axis)
    inner = (index == 1) | (index == 2)
    count = len(parts)
    totals, results = [], []
    for k in range(count + LAG):
        if k < LAG:
            sent = parts[k]
        elif k < count:
            sent = jnp.where(inner, totals[k - LAG], parts[k])
        else:
            sent = totals[k - LAG]
        got = lax.ppermute(sent, axis, [(0, 1), (1, 0), (2, 3), (3, 2)])
        if k < count:
            half = add(parts[k], got)
            other = lax.ppermute(half, axis, [(1, 2), (2, 1), (0, 0), (3, 3)])
            totals.append(add(half, other))
        if k >= LAG:
            results.append(jnp.where(inner, totals[k - LAG], got))
    return results


def body(
    lengths,
    final_hidden,
    score_gain,
    score_head,
    policy_input,
    block_order,
    norm_gain,
    key_weight,
    key_cotangent,
):
    n_section, n_dp, n_mp = (lax.axis_size(name) for name in ("section", "dp", "mp"))
    dp, mp = lax.axis_index("dp"), lax.axis_index("mp")
    block_count = lengths.shape[0]
    tokens, local_width = policy_input.shape
    block_len = tokens // block_count
    pair = block_count // n_dp
    columns = key_cotangent.shape[1]
    own_width = local_width // n_dp
    chunk = own_width // FEATURE_BLOCKS
    n_far = n_mp // 2
    order = block_order[0]
    gain = norm_gain.astype(jnp.float32)

    cotangents = [key_cotangent] + [swap(key_cotangent, "dp", j) for j in range(1, n_dp)]

    def both_cores(values):
        other = [swap(value, "mp", 1) for value in values]
        low = mp % 2 == 0
        return jnp.concatenate(
            [
                jnp.concatenate([jnp.where(low, a, b), jnp.where(low, b, a)], axis=1)
                for a, b in zip(values, other)
            ],
            axis=0,
        )

    def features(part, f):
        start = part * own_width + f * chunk
        return policy_input[:, start : start + chunk]

    def piece_for(j, first, last):
        return pick(
            [
                policy_input[:, e * own_width + first * chunk : e * own_width + last * chunk]
                for e in range(n_dp)
            ],
            dp ^ j,
        )

    send_blocks = FEATURE_BLOCKS // 4
    rows = []
    for first in range(0, FEATURE_BLOCKS, send_blocks):
        last = first + send_blocks
        got = [piece_for(0, first, last)]
        got += [swap(piece_for(j, first, last), "dp", j) for j in range(1, n_dp)]
        got = jnp.concatenate(got, axis=0)
        rows += [got[:, i * chunk : (i + 1) * chunk] for i in range(send_blocks)]

    hidden_values = final_hidden.astype(jnp.float32)
    inverse_hidden = lax.rsqrt(jnp.mean(hidden_values * hidden_values, axis=1) + EPSILON)
    coefficient = score_gain.astype(jnp.float32) * score_head.astype(jnp.float32)
    scores = jnp.sum(hidden_values * coefficient[None, :], axis=1) * inverse_hidden
    position = lax.broadcasted_iota(jnp.int32, (block_count, block_len), 1)
    token_weight = jnp.where(position < lengths[:, None], scores[:, None], 0.0)
    squares = jnp.sum(jnp.square(policy_input.astype(jnp.float32)), axis=1)
    squares = squares.reshape(block_count, block_len)
    squares = squares + sum(swap(squares, "mp", j) for j in range(1, n_mp))
    inverse = lax.rsqrt(squares / (local_width * n_mp) + EPSILON)
    small = jnp.concatenate(
        [
            inverse,
            token_weight,
            jnp.broadcast_to(order.astype(jnp.float32)[:, None], (block_count, block_len)),
        ],
        axis=0,
    )
    small = [small] + [swap(small, "dp", j) for j in range(1, n_dp)]

    def key_gradient(cotangent):
        blocks = cotangent.reshape(n_dp, block_count, block_len, -1)
        found = []
        for j in range(n_dp):
            sender = dp ^ j
            for b in range(block_count):
                slot = small[j][2 * block_count + b, 0].astype(jnp.int32)
                candidates, where = [], []
                for e in range(n_dp):
                    for q in range(pair):
                        candidates.append(
                            lax.dynamic_index_in_dim(
                                blocks[e], sender * pair + q, 0, keepdims=False
                            )
                        )
                        where.append((dp ^ e) * pair + q)
                chosen = candidates[0]
                for value, at in zip(candidates[1:], where[1:]):
                    chosen = jnp.where(slot == at, value, chosen)
                weight = small[j][block_count + b].astype(jnp.bfloat16).astype(jnp.float32)
                key_grad = to_bfloat16(chosen.astype(jnp.float32) * weight[:, None])
                found.append(
                    (key_grad.astype(jnp.float32) * small[j][b][:, None]).astype(jnp.bfloat16)
                )
        return jnp.concatenate(found, axis=0)

    parts = []
    for g in range(n_far):
        near = cotangents if g == 0 else [swap(value, "mp", 2 * g) for value in cotangents]
        key_grad = key_gradient(both_cores(near))
        for f in range(FEATURE_BLOCKS):
            part = lax.dot_general(
                rows[f],
                key_grad,
                (((0,), (0,)), ((), ())),
                preferred_element_type=jnp.float32,
            )
            parts.append(to_bfloat16(part))
    totals = line_sums(parts, "section")
    shared = [[total] + [swap(total, "dp", j) for j in range(1, n_dp)] for total in totals]
    shards = n_section * n_dp
    grad_weight = jnp.zeros((local_width, n_mp * columns), jnp.float32)
    grad_gain = [None] * (n_dp * FEATURE_BLOCKS)
    for f in range(FEATURE_BLOCKS):
        groups = [shared[g * FEATURE_BLOCKS + f] for g in range(n_far)]
        for e in range(n_dp):
            start = e * own_width + f * chunk
            by_group = [pick(group, dp ^ e) for group in groups]
            value = jnp.concatenate([pick(by_group, (mp // 2) ^ g) for g in range(n_far)], axis=1)
            value = value.astype(jnp.float32) / shards
            grad_weight = lax.dynamic_update_slice(
                grad_weight, value * gain[start : start + chunk, None], (start, 0)
            )
            weight = key_weight[start : start + chunk].astype(jnp.float32)
            grad_gain[e * FEATURE_BLOCKS + f] = jnp.sum(value * weight, axis=1)
    grad_gain = jnp.concatenate(grad_gain)

    inverse, _ = lax.optimization_barrier((inverse, totals[0]))
    normed = policy_input.astype(jnp.float32) * inverse.reshape(-1, 1) * gain[None, :]
    normed = lax.optimization_barrier(normed.astype(jnp.bfloat16))
    partial = jnp.dot(normed, key_weight, preferred_element_type=jnp.float32)
    own_columns = pick([partial[:, i * columns : (i + 1) * columns] for i in range(n_mp)], mp)
    partial = partial.astype(jnp.bfloat16)
    for j in range(1, n_mp):
        piece = pick([partial[:, i * columns : (i + 1) * columns] for i in range(n_mp)], mp ^ j)
        own_columns = own_columns + swap(piece, "mp", j).astype(jnp.float32)
    keys = own_columns.astype(jnp.bfloat16).reshape(block_count, block_len, columns)
    by_slot = []
    for slot in range(block_count):
        chosen = keys[0]
        for b in range(1, block_count):
            chosen = jnp.where(order[b] == slot, keys[b], chosen)
        by_slot.append(chosen)
    by_target = [jnp.stack(by_slot[e * pair : (e + 1) * pair]) for e in range(n_dp)]
    arrived = [pick(by_target, dp)]
    arrived += [swap(pick(by_target, dp ^ j), "dp", j) for j in range(1, n_dp)]
    learner_keys = jnp.concatenate([pick(arrived, dp ^ a) for a in range(n_dp)], axis=0)
    return learner_keys.reshape(tokens, columns), grad_weight, grad_gain


def solution(mesh):
    placed = (
        P(("section", "dp")),
        P(("section", "dp"), None),
        P(),
        P(),
        P(("section", "dp"), "mp"),
        P(("section", "dp"), None),
        P("mp"),
        P("mp", None),
        P(("section", "dp"), "mp"),
    )
    return jax.shard_map(
        body,
        mesh=mesh,
        in_specs=placed,
        out_specs=(P(("section", "dp"), "mp"), P("mp", None), P("mp")),
        check_vma=False,
    )
```

```python
import functools

import jax
import jax.numpy as jnp
from jax import lax
from jax.experimental import pallas as pl
from jax.experimental.pallas import tpu as pltpu
from jax.sharding import PartitionSpec as P

EPSILON = 1e-06
CHUNK_ROWS = 128
LAG = 3
SHARE_LAG = 2


def swap(value, axis, bit):
    return lax.ppermute(value, axis, [(i, i ^ bit) for i in range(lax.axis_size(axis))])


def pick(values, index):
    chosen = values[0]
    for i in range(1, len(values)):
        chosen = jnp.where(index == i, values[i], chosen)
    return chosen


def to_bfloat16(value):
    return lax.reduce_precision(value, 8, 7).astype(jnp.bfloat16)


def add(left, right):
    return to_bfloat16(left.astype(jnp.float32) + right.astype(jnp.float32))


def summed(parts, shared_sum, emit):
    count = len(parts)
    if lax.axis_size("section") != 4:
        for k, part in enumerate(parts):
            emit(k, shared_sum(to_bfloat16(lax.psum(part.astype(jnp.float32), "section"))))
        return
    index = lax.axis_index("section")
    inner = (index == 1) | (index == 2)

    def outer_swap(value):
        return lax.ppermute(value, "section", [(0, 1), (1, 0), (2, 3), (3, 2)])

    def middle_swap(value):
        return lax.ppermute(value, "section", [(1, 2), (2, 1), (0, 0), (3, 3)])

    arriving = {k: outer_swap(parts[k]) for k in range(min(LAG, count))}
    halves, others, totals, shares = {}, {}, {}, {}
    for k in range(count + LAG + SHARE_LAG):
        waited = {}
        if k in arriving:
            waited["got"] = arriving[k]
        if k - 1 in others:
            waited["other"] = others[k - 1]
        if k - LAG - SHARE_LAG in shares:
            waited["share"] = shares[k - LAG - SHARE_LAG]
        waited = lax.optimization_barrier(waited)
        if k < count:
            halves[k] = add(parts[k], waited["got"])
            others[k] = middle_swap(halves[k])
        if "other" in waited:
            totals[k - 1] = add(halves[k - 1], waited["other"])
        following = k - 1 + LAG
        if LAG <= following < count + LAG:
            value = totals[following - LAG]
            if following < count:
                value = jnp.where(inner, value, parts[following])
            arriving[following] = outer_swap(value)
        if LAG <= k < count + LAG:
            shares[k - LAG] = shared_sum(jnp.where(inner, totals[k - LAG], waited["got"]))
        if "share" in waited:
            emit(k - LAG - SHARE_LAG, waited["share"])


def prepare(n_dp, block_len, send_width, lengths, order, hidden, gain, head, rows, squares, rest, *pieces):
    block_count = lengths.shape[0]
    dp = lax.axis_index("dp")
    own_width = rows.shape[1] // n_dp
    per_owner = own_width // send_width
    for j in range(n_dp):
        for e in range(n_dp):

            @pl.when((dp ^ j) == e)
            def _(j=j, e=e):
                for i in range(per_owner):
                    start = e * own_width + i * send_width
                    pieces[j * per_owner + i][...] = rows[:, start : start + send_width]

    lane = lax.broadcasted_iota(jnp.int32, (block_len, block_len), 1)
    diagonal = lane == lax.broadcasted_iota(jnp.int32, (block_len, block_len), 0)
    position = lax.broadcasted_iota(jnp.int32, (1, block_len), 1)
    values = hidden[...].astype(jnp.float32)
    coefficient = (gain[...].astype(jnp.float32) * head[...].astype(jnp.float32)).reshape(1, -1)
    inverse = lax.rsqrt(jnp.mean(values * values, axis=1, keepdims=True) + EPSILON)
    scores = jnp.sum(values * coefficient, axis=1, keepdims=True) * inverse
    for b in range(block_count):
        total = jnp.zeros((block_len, 128), jnp.float32)
        for start in range(0, rows.shape[1], 128):
            value = rows[b * block_len : (b + 1) * block_len, start : start + 128]
            value = value.astype(jnp.float32)
            total = total + value * value
        total = jnp.sum(total, axis=1, keepdims=True)
        squares[b : b + 1, :] = jnp.sum(jnp.where(diagonal, total, 0.0), axis=0, keepdims=True)
        weight = jnp.where(position < lengths[b], scores[b : b + 1], 0.0)
        rest[b : b + 1, :] = weight
        rest[block_count + b : block_count + b + 1, :] = jnp.full(
            (1, block_len), order[0, b].astype(jnp.float32)
        )


def body(
    lengths,
    final_hidden,
    score_gain,
    score_head,
    policy_input,
    block_order,
    norm_gain,
    key_weight,
    key_cotangent,
):
    n_section, n_dp, n_mp = (lax.axis_size(name) for name in ("section", "dp", "mp"))
    dp, mp = lax.axis_index("dp"), lax.axis_index("mp")
    block_count = lengths.shape[0]
    tokens, local_width = policy_input.shape
    block_len = tokens // block_count
    pair = block_count // n_dp
    columns = key_cotangent.shape[1]
    own_width = local_width // n_dp
    chunk = min(CHUNK_ROWS, own_width)
    feature_blocks = own_width // chunk
    n_far = n_mp // 2
    far, core = mp >> 1, mp & 1
    order = block_order[0]
    gain = norm_gain.astype(jnp.float32)

    cotangents = [key_cotangent] + [swap(key_cotangent, "dp", j) for j in range(1, n_dp)]
    cotangents = jnp.concatenate(cotangents, axis=0)

    send_width = min(2 * chunk, own_width)
    per_owner = own_width // send_width
    vmem, smem = pl.BlockSpec(memory_space=pltpu.VMEM), pl.BlockSpec(memory_space=pltpu.SMEM)
    squares, rest, *pieces = pl.pallas_call(
        functools.partial(prepare, n_dp, block_len, send_width),
        out_shape=[
            jax.ShapeDtypeStruct((block_count, block_len), jnp.float32),
            jax.ShapeDtypeStruct((2 * block_count, block_len), jnp.float32),
        ]
        + [jax.ShapeDtypeStruct((tokens, send_width), jnp.bfloat16)] * (n_dp * per_owner),
        in_specs=[smem, smem, vmem, vmem, vmem, vmem],
        out_specs=[vmem] * (2 + n_dp * per_owner),
        compiler_params=pltpu.CompilerParams(vmem_limit_bytes=32 * 2**20),
        name="prepare",
    )(lengths, block_order, final_hidden, score_gain, score_head, policy_input)
    squares = squares + sum(swap(squares, "mp", j) for j in range(1, n_mp))
    inverse = lax.rsqrt(squares / (local_width * n_mp) + EPSILON)
    small = jnp.concatenate([inverse, rest], axis=0)
    small = [small] + [swap(small, "dp", j) for j in range(1, n_dp)]
    rows = []
    for i in range(per_owner):
        got = [pieces[i]]
        for j in range(1, n_dp):
            piece = pieces[j * per_owner + i]
            if i:
                piece, _ = lax.optimization_barrier((piece, small[0]))
            got.append(swap(piece, "dp", j))
        got = jnp.concatenate(got, axis=0)
        rows += [got[:, c : c + chunk] for c in range(0, send_width, chunk)]

    def key_gradient(near):
        other = swap(near, "mp", 1)
        low = core == 0
        cotangent = jnp.concatenate(
            [jnp.where(low, near, other), jnp.where(low, other, near)], axis=1
        ).reshape(n_dp, n_dp, pair, block_len, -1)
        found = []
        for j in range(n_dp):
            sender = dp ^ j
            for b in range(block_count):
                slot = small[j][2 * block_count + b][:, None]
                chosen = None
                for e in range(n_dp):
                    for q in range(pair):
                        value = lax.dynamic_index_in_dim(cotangent[e], sender, 0, keepdims=False)[q]
                        at = ((dp ^ e) * pair + q).astype(jnp.float32)
                        chosen = value if chosen is None else jnp.where(slot == at, value, chosen)
                weight = small[j][block_count + b].astype(jnp.bfloat16).astype(jnp.float32)
                key_grad = to_bfloat16(chosen.astype(jnp.float32) * weight[:, None])
                found.append(
                    (key_grad.astype(jnp.float32) * small[j][b][:, None]).astype(jnp.bfloat16)
                )
        return jnp.concatenate(found, axis=0)

    parts = []
    for g in range(n_far):
        near = cotangents
        if g:
            near, _ = lax.optimization_barrier((near, parts[0]))
            near = swap(near, "mp", 2 * g)
        key_grad = key_gradient(near)
        for f in range(feature_blocks):
            part = lax.dot_general(
                rows[f],
                key_grad,
                (((0,), (0,)), ((), ())),
                preferred_element_type=jnp.float32,
            )
            parts.append(to_bfloat16(part))
    shards = n_section * n_dp
    shared = {}
    out = [jnp.zeros((local_width, n_mp * columns), jnp.float32)]
    grad_gain = [None] * (n_dp * feature_blocks)

    def shared_sum(total):
        return [total] + [swap(total, "dp", j) for j in range(1, n_dp)]

    def emit(k, values):
        shared[k] = values
        f = k % feature_blocks
        if k // feature_blocks < n_far - 1:
            return
        groups = [shared[g * feature_blocks + f] for g in range(n_far)]
        for e in range(n_dp):
            start = e * own_width + f * chunk
            by_group = [pick(group, dp ^ e) for group in groups]
            value = jnp.concatenate([pick(by_group, far ^ g) for g in range(n_far)], axis=1)
            value = value.astype(jnp.float32) / shards
            out[0] = lax.dynamic_update_slice(
                out[0], value * gain[start : start + chunk, None], (start, 0)
            )
            weight = key_weight[start : start + chunk].astype(jnp.float32)
            grad_gain[e * feature_blocks + f] = jnp.sum(value * weight, axis=1)

    summed(parts, shared_sum, emit)
    grad_weight = out[0]
    grad_gain = jnp.concatenate(grad_gain)

    inverse, _ = lax.optimization_barrier((inverse, shared[0]))
    normed = policy_input.astype(jnp.float32) * inverse.reshape(-1, 1) * gain[None, :]
    normed = lax.optimization_barrier(normed.astype(jnp.bfloat16))
    partial = jnp.dot(normed, key_weight, preferred_element_type=jnp.float32)
    own_columns = pick([partial[:, i * columns : (i + 1) * columns] for i in range(n_mp)], mp)
    partial = partial.astype(jnp.bfloat16)
    for j in range(1, n_mp):
        piece = pick([partial[:, i * columns : (i + 1) * columns] for i in range(n_mp)], mp ^ j)
        own_columns = own_columns + swap(piece, "mp", j).astype(jnp.float32)
    keys = own_columns.astype(jnp.bfloat16).reshape(block_count, block_len, columns)
    by_slot = []
    for slot in range(block_count):
        chosen = keys[0]
        for b in range(1, block_count):
            chosen = jnp.where(order[b] == slot, keys[b], chosen)
        by_slot.append(chosen)
    by_target = [jnp.stack(by_slot[e * pair : (e + 1) * pair]) for e in range(n_dp)]
    arrived = [pick(by_target, dp)]
    arrived += [swap(pick(by_target, dp ^ j), "dp", j) for j in range(1, n_dp)]
    learner_keys = jnp.concatenate([pick(arrived, dp ^ a) for a in range(n_dp)], axis=0)
    return learner_keys.reshape(tokens, columns), grad_weight, grad_gain


def solution(mesh):
    placed = (
        P(("section", "dp")),
        P(("section", "dp"), None),
        P(),
        P(),
        P(("section", "dp"), "mp"),
        P(("section", "dp"), None),
        P("mp"),
        P("mp", None),
        P(("section", "dp"), "mp"),
    )
    return jax.shard_map(
        body,
        mesh=mesh,
        in_specs=placed,
        out_specs=(P(("section", "dp"), "mp"), P("mp", None), P("mp")),
        check_vma=False,
    )
```

```python
import functools

import jax
import jax.numpy as jnp
from jax import lax
from jax.experimental import pallas as pl
from jax.experimental.pallas import tpu as pltpu
from jax.sharding import PartitionSpec as P

EPSILON = 1e-06
CHUNK_ROWS = 256
LAG = 3


def swap(value, axis, bit):
    return lax.ppermute(value, axis, [(i, i ^ bit) for i in range(lax.axis_size(axis))])


def pick(values, index):
    chosen = values[0]
    for i in range(1, len(values)):
        chosen = jnp.where(index == i, values[i], chosen)
    return chosen


def to_bfloat16(value):
    return lax.reduce_precision(value, 8, 7).astype(jnp.bfloat16)


def add(left, right):
    return to_bfloat16(left.astype(jnp.float32) + right.astype(jnp.float32))


def summed(parts, shared_sum, emit, side):
    count = len(parts)
    if lax.axis_size("section") != 4:
        for k, part in enumerate(parts):
            emit(k, shared_sum(to_bfloat16(lax.psum(part.astype(jnp.float32), "section"))))
        pending = ()
        while pending is not None:
            pending = side(pending)
        return
    index = lax.axis_index("section")
    inner = (index == 1) | (index == 2)

    def outer_swap(value):
        return lax.ppermute(value, "section", [(0, 1), (1, 0), (2, 3), (3, 2)])

    def middle_swap(value):
        return lax.ppermute(value, "section", [(1, 2), (2, 1), (0, 0), (3, 3)])

    arriving = {k: outer_swap(parts[k]) for k in range(min(LAG, count))}
    halves, others, totals, shares = {}, {}, {}, {}
    done, pending = (), ()
    for k in range(count + LAG):
        got, done = lax.optimization_barrier((arriving[k], done))
        tied = ()
        if k < count:
            halves[k] = add(parts[k], got)
            others[k] = middle_swap(halves[k])
            tied += (halves[k],)
        if k >= LAG:
            full = jnp.where(inner, totals[k - LAG], got)
            shares[k - LAG] = shared_sum(full)
            tied += (full,)
        waited = {"tied": tied, "side": pending}
        if k - 1 in others:
            waited["other"] = others[k - 1]
        if k - 1 - LAG in shares:
            waited["share"] = shares[k - 1 - LAG]
        waited = lax.optimization_barrier(waited)
        if k < count:
            halves[k] = waited["tied"][0]
        if "other" in waited:
            totals[k - 1] = add(halves[k - 1], waited["other"])
        following = k - 1 + LAG
        if LAG <= following < count + LAG:
            value = totals[following - LAG]
            if following < count:
                value = jnp.where(inner, value, parts[following])
            arriving[following] = outer_swap(value)
        done = ()
        if k >= LAG and pending is not None:
            pending = side(waited["side"])
            done += () if pending is None else pending[:1]
        if "share" in waited:
            done += (emit(k - 1 - LAG, waited["share"]),)
    emit(count - 1, shares[count - 1])
    while pending is not None:
        pending = side(pending)


def prepare(n_dp, block_len, send_width, *refs):
    sources, refs = refs[:6], refs[6:]
    n_pieces = len(refs) - 9
    squares, rest, *pieces = refs[: 2 + n_pieces]
    buffers, semaphores = refs[2 + n_pieces : -1], refs[-1]
    copies = [
        pltpu.make_async_copy(source, buffer, semaphores.at[i])
        for i, (source, buffer) in enumerate(zip(sources, buffers))
    ]
    for copy in copies:
        copy.start()
    for copy in copies:
        copy.wait()
    lengths, order, hidden, gain, head, rows = buffers
    block_count = lengths.shape[0]
    dp = lax.axis_index("dp")
    own_width = rows.shape[1] // n_dp
    per_owner = own_width // send_width
    for j in range(n_dp):
        for e in range(n_dp):

            @pl.when((dp ^ j) == e)
            def _(j=j, e=e):
                for i in range(per_owner):
                    start = e * own_width + i * send_width
                    pieces[j * per_owner + i][...] = rows[:, start : start + send_width]

    lane = lax.broadcasted_iota(jnp.int32, (block_len, block_len), 1)
    diagonal = lane == lax.broadcasted_iota(jnp.int32, (block_len, block_len), 0)
    position = lax.broadcasted_iota(jnp.int32, (1, block_len), 1)
    values = hidden[...].astype(jnp.float32)
    coefficient = (gain[...].astype(jnp.float32) * head[...].astype(jnp.float32)).reshape(1, -1)
    inverse = lax.rsqrt(jnp.mean(values * values, axis=1, keepdims=True) + EPSILON)
    scores = jnp.sum(values * coefficient, axis=1, keepdims=True) * inverse
    for b in range(block_count):
        total = jnp.zeros((block_len, 128), jnp.float32)
        for start in range(0, rows.shape[1], 128):
            value = rows[b * block_len : (b + 1) * block_len, start : start + 128]
            value = value.astype(jnp.float32)
            total = total + value * value
        total = jnp.sum(total, axis=1, keepdims=True)
        squares[b : b + 1, :] = jnp.sum(jnp.where(diagonal, total, 0.0), axis=0, keepdims=True)
        weight = jnp.where(position < lengths[b], scores[b : b + 1], 0.0)
        rest[b : b + 1, :] = weight
        rest[block_count + b : block_count + b + 1, :] = jnp.full(
            (1, block_len), order[0, b].astype(jnp.float32)
        )


def store(n_dp, g, first, shards, *refs):
    values = refs[:n_dp]
    gain, weight = refs[n_dp : n_dp + 2]
    out, sums, weights, results, semaphores = refs[-5:]
    chunk, width = values[0].shape
    dp, far = lax.axis_index("dp"), lax.axis_index("mp") >> 1
    own_width = weight.shape[0] // n_dp
    column = pl.multiple_of((far ^ g) * width, 128)
    starts = [pl.multiple_of((dp ^ j) * own_width + first, 16) for j in range(n_dp)]
    loads = [
        pltpu.make_async_copy(
            weight.at[pl.ds(starts[j], chunk), pl.ds(column, width)],
            weights.at[j],
            semaphores.at[0, j],
        )
        for j in range(n_dp)
    ]
    stores = [
        pltpu.make_async_copy(
            results.at[j],
            out.at[pl.ds(starts[j], chunk), pl.ds(column, width)],
            semaphores.at[1, j],
        )
        for j in range(n_dp)
    ]
    for load in loads:
        load.start()
    lane = lax.broadcasted_iota(jnp.int32, (128, 128), 1)
    diagonal = lane == lax.broadcasted_iota(jnp.int32, (128, 128), 0)
    for j in range(n_dp):
        loads[j].wait()
        for at in range(0, chunk, 128):
            gains = gain[:, pl.ds(pl.multiple_of((dp ^ j) * own_width + first + at, 128), 128)]
            gains = jnp.sum(jnp.where(diagonal, gains, 0.0), axis=1, keepdims=True)
            total = values[j][at : at + 128, :].astype(jnp.float32) * (1.0 / shards)
            results[j, at : at + 128, :] = total * gains
            total = total * weights[j, at : at + 128, :].astype(jnp.float32)
            total = jnp.sum(total, axis=1, keepdims=True)
            total = jnp.sum(jnp.where(diagonal, total, 0.0), axis=0, keepdims=True)
            sums[j : j + 1, at : at + 128] = total
        stores[j].start()
    for copy in stores:
        copy.wait()


def body(
    lengths,
    final_hidden,
    score_gain,
    score_head,
    policy_input,
    block_order,
    norm_gain,
    key_weight,
    key_cotangent,
):
    n_section, n_dp, n_mp = (lax.axis_size(name) for name in ("section", "dp", "mp"))
    dp, mp = lax.axis_index("dp"), lax.axis_index("mp")
    block_count = lengths.shape[0]
    tokens, local_width = policy_input.shape
    block_len = tokens // block_count
    pair = block_count // n_dp
    columns = key_cotangent.shape[1]
    own_width = local_width // n_dp
    chunk = min(CHUNK_ROWS, own_width)
    feature_blocks = own_width // chunk
    n_far = n_mp // 2
    far, core = mp >> 1, mp & 1

    cotangents = [key_cotangent] + [swap(key_cotangent, "dp", j) for j in range(1, n_dp)]
    cotangents = jnp.concatenate(cotangents, axis=0)

    per_owner = feature_blocks
    given = (lengths, block_order, final_hidden, score_gain, score_head, policy_input)
    vmem, hbm = pl.BlockSpec(memory_space=pltpu.VMEM), pl.BlockSpec(memory_space=pl.ANY)
    squares, rest, *pieces = pl.pallas_call(
        functools.partial(prepare, n_dp, block_len, chunk),
        out_shape=[
            jax.ShapeDtypeStruct((block_count, block_len), jnp.float32),
            jax.ShapeDtypeStruct((2 * block_count, block_len), jnp.float32),
        ]
        + [jax.ShapeDtypeStruct((tokens, chunk), jnp.bfloat16)] * (n_dp * per_owner),
        in_specs=[hbm] * 6,
        out_specs=[vmem] * (2 + n_dp * per_owner),
        scratch_shapes=[pltpu.SMEM(value.shape, value.dtype) for value in given[:2]]
        + [pltpu.VMEM(value.shape, value.dtype) for value in given[2:]]
        + [pltpu.SemaphoreType.DMA((6,))],
        compiler_params=pltpu.CompilerParams(vmem_limit_bytes=32 * 2**20),
        name="prepare",
    )(*given)
    squares = squares + sum(swap(squares, "mp", j) for j in range(1, n_mp))
    inverse = lax.rsqrt(squares / (local_width * n_mp) + EPSILON)
    small = jnp.concatenate([inverse, rest], axis=0)
    small = [small] + [swap(small, "dp", j) for j in range(1, n_dp)]

    parts = []

    def rows(f):
        got = [pieces[f]]
        for j in range(1, n_dp):
            piece = pieces[j * per_owner + f]
            if f:
                piece, _ = lax.optimization_barrier((piece, parts[0]))
            piece = swap(piece, "dp", j)
            if f:
                piece, _ = lax.optimization_barrier((piece, parts[f - 1]))
            got.append(piece)
        return jnp.concatenate(got, axis=0)

    gathered = []

    def key_gradient(near):
        other = swap(near, "mp", 1)
        low = core == 0
        cotangent = jnp.concatenate(
            [jnp.where(low, near, other), jnp.where(low, other, near)], axis=1
        ).reshape(n_dp, n_dp, pair, block_len, -1)
        found = []
        for j in range(n_dp):
            sender = dp ^ j
            for b in range(block_count):
                slot = small[j][2 * block_count + b][:, None]
                chosen = None
                for e in range(n_dp):
                    for q in range(pair):
                        value = lax.dynamic_index_in_dim(cotangent[e], sender, 0, keepdims=False)[q]
                        at = ((dp ^ e) * pair + q).astype(jnp.float32)
                        chosen = value if chosen is None else jnp.where(slot == at, value, chosen)
                weight = small[j][block_count + b].astype(jnp.bfloat16).astype(jnp.float32)
                key_grad = to_bfloat16(chosen.astype(jnp.float32) * weight[:, None])
                found.append(
                    (key_grad.astype(jnp.float32) * small[j][b][:, None]).astype(jnp.bfloat16)
                )
        return jnp.concatenate(found, axis=0)

    for g in range(n_far):
        near = cotangents
        if g:
            near, _ = lax.optimization_barrier((near, parts[0]))
            near = swap(near, "mp", 2 * g)
        key_grad = key_gradient(near)
        for f in range(feature_blocks):
            if not g:
                gathered.append(rows(f))
            part = lax.dot_general(
                gathered[f],
                key_grad,
                (((0,), (0,)), ((), ())),
                preferred_element_type=jnp.float32,
            )
            parts.append(to_bfloat16(part))
    late_gain, _ = lax.optimization_barrier((norm_gain, parts[0]))
    gain = late_gain.astype(jnp.float32)[None, :]
    shards = n_section * n_dp
    out = []
    sums = []

    def shared_sum(total):
        return [total] + [swap(total, "dp", j) for j in range(1, n_dp)]

    def emit(k, values):
        g, f = divmod(k, feature_blocks)
        before = tuple(out)
        result, total = pl.pallas_call(
            functools.partial(store, n_dp, g, f * chunk, shards),
            out_shape=[
                jax.ShapeDtypeStruct((local_width, n_mp * columns), jnp.float32),
                jax.ShapeDtypeStruct((n_dp, chunk), jnp.float32),
            ],
            in_specs=[vmem] * (n_dp + 1) + [hbm] * (1 + len(before)),
            out_specs=[hbm, vmem],
            input_output_aliases={n_dp + 2: 0} if before else {},
            scratch_shapes=[
                pltpu.VMEM((n_dp, chunk, 2 * columns), jnp.bfloat16),
                pltpu.VMEM((n_dp, chunk, 2 * columns), jnp.float32),
                pltpu.SemaphoreType.DMA((2, n_dp)),
            ],
            compiler_params=pltpu.CompilerParams(vmem_limit_bytes=32 * 2**20),
            name="store",
        )(*values, gain, key_weight, *before)
        out[:] = [result]
        sums.append(total)
        return total

    def key_steps():
        yield (inverse,)
        (late_inverse,) = side_values[0]
        normed = policy_input.astype(jnp.float32) * late_inverse.reshape(-1, 1) * gain
        normed = lax.optimization_barrier(normed.astype(jnp.bfloat16))
        partial = jnp.dot(normed, key_weight, preferred_element_type=jnp.float32)
        cut = [partial[:, i * columns : (i + 1) * columns] for i in range(n_mp)]
        yield (partial,)
        (partial,) = side_values[0]
        cut = [partial[:, i * columns : (i + 1) * columns] for i in range(n_mp)]
        own = pick(cut, mp)
        yield (own,) + tuple(
            swap(pick(cut, mp ^ j).astype(jnp.bfloat16), "mp", j) for j in range(1, n_mp)
        )
        own, *others = side_values[0]
        keys = own + sum(other.astype(jnp.float32) for other in others)
        keys = keys.astype(jnp.bfloat16).reshape(block_count, block_len, columns)
        by_slot = []
        for slot in range(block_count):
            chosen = keys[0]
            for b in range(1, block_count):
                chosen = jnp.where(rest[block_count + b][:, None] == slot, keys[b], chosen)
            by_slot.append(chosen)
        by_target = [jnp.concatenate(by_slot[e * pair : (e + 1) * pair]) for e in range(n_dp)]
        yield (pick(by_target, dp),) + tuple(
            swap(pick(by_target, dp ^ j), "dp", j) for j in range(1, n_dp)
        )
        arrived = side_values[0]
        learner_keys.append(jnp.concatenate([pick(arrived, dp ^ a) for a in range(n_dp)], axis=0))

    side_values, learner_keys = [()], []
    steps = key_steps()

    def side(waited):
        side_values[0] = waited
        return next(steps, None)

    summed(parts, shared_sum, emit, side)
    grad_gain = [
        sum(sums[g * feature_blocks + f] for g in range(n_far)) for f in range(feature_blocks)
    ]
    grad_gain = jnp.concatenate(grad_gain, axis=1)
    grad_gain = jnp.concatenate([pick([grad_gain[j] for j in range(n_dp)], dp ^ e) for e in range(n_dp)])
    return learner_keys[0], out[0], grad_gain


def solution(mesh):
    placed = (
        P(("section", "dp")),
        P(("section", "dp"), None),
        P(),
        P(),
        P(("section", "dp"), "mp"),
        P(("section", "dp"), None),
        P("mp"),
        P("mp", None),
        P(("section", "dp"), "mp"),
    )
    return jax.shard_map(
        body,
        mesh=mesh,
        in_specs=placed,
        out_specs=(P(("section", "dp"), "mp"), P("mp", None), P("mp")),
        check_vma=False,
    )
```

```python
import functools

import jax
import jax.numpy as jnp
from jax import lax
from jax.experimental import pallas as pl
from jax.experimental.pallas import tpu as pltpu
from jax.sharding import PartitionSpec as P

EPSILON = 1e-06
CHUNK_ROWS = 256
LAG = 3


def swap(value, axis, bit):
    return lax.ppermute(value, axis, [(i, i ^ bit) for i in range(lax.axis_size(axis))])


def pick(values, index):
    chosen = values[0]
    for i in range(1, len(values)):
        chosen = jnp.where(index == i, values[i], chosen)
    return chosen


def to_bfloat16(value):
    return lax.reduce_precision(value, 8, 7).astype(jnp.bfloat16)


def add(left, right):
    return to_bfloat16(left.astype(jnp.float32) + right.astype(jnp.float32))


def summed(parts, shared_sum, emit, side):
    count = len(parts)
    if lax.axis_size("section") != 4:
        for k, part in enumerate(parts):
            emit(k, shared_sum(to_bfloat16(lax.psum(part.astype(jnp.float32), "section"))))
        pending = ()
        while pending is not None:
            pending = side(pending)
        return
    index = lax.axis_index("section")
    inner = (index == 1) | (index == 2)

    def outer_swap(value):
        return lax.ppermute(value, "section", [(0, 1), (1, 0), (2, 3), (3, 2)])

    def middle_swap(value):
        return lax.ppermute(value, "section", [(1, 2), (2, 1), (0, 0), (3, 3)])

    arriving = {k: outer_swap(parts[k]) for k in range(min(LAG, count))}
    halves, others, totals, shares = {}, {}, {}, {}
    done, pending = (), ()
    for k in range(count + LAG):
        got, _ = lax.optimization_barrier((arriving[k], done))
        done = ()
        tied = ()
        if k < count:
            halves[k] = add(parts[k], got)
            others[k] = middle_swap(halves[k])
            tied += (halves[k],)
        if k >= LAG:
            tied += (jnp.where(inner, totals[k - LAG], got),)
        waited = {"tied": tied, "side": pending}
        if k - 1 in others:
            waited["other"] = others[k - 1]
        if k - 1 - LAG in shares:
            waited["share"] = shares[k - 1 - LAG]
        waited = lax.optimization_barrier(waited)
        if k < count:
            halves[k] = waited["tied"][0]
        if "other" in waited:
            totals[k - 1] = add(halves[k - 1], waited["other"])
        following = k - 1 + LAG
        if LAG <= following < count + LAG:
            value = totals[following - LAG]
            if following < count:
                value = jnp.where(inner, value, parts[following])
            value, waited["tied"] = lax.optimization_barrier((value, waited["tied"]))
            arriving[following] = outer_swap(value)
            done = (value,)
        if k >= LAG:
            shares[k - LAG] = shared_sum(waited["tied"][-1])
        if k >= LAG and pending is not None:
            pending = side(waited["side"])
            done += () if pending is None else pending[:1]
        if "share" in waited:
            done += (emit(k - 1 - LAG, waited["share"]),)
    emit(count - 1, shares[count - 1])
    while pending is not None:
        pending = side(pending)


def prepare(n_dp, block_len, send_width, *refs):
    sources, refs = refs[:6], refs[6:]
    n_pieces = len(refs) - 9
    squares, rest, *pieces = refs[: 2 + n_pieces]
    buffers, semaphores = refs[2 + n_pieces : -1], refs[-1]
    copies = [
        pltpu.make_async_copy(source, buffer, semaphores.at[i])
        for i, (source, buffer) in enumerate(zip(sources, buffers))
    ]
    for copy in copies:
        copy.start()
    for copy in copies:
        copy.wait()
    lengths, order, hidden, gain, head, rows = buffers
    block_count = lengths.shape[0]
    dp = lax.axis_index("dp")
    own_width = rows.shape[1] // n_dp
    per_owner = own_width // send_width
    for j in range(n_dp):
        for e in range(n_dp):

            @pl.when((dp ^ j) == e)
            def _(j=j, e=e):
                for i in range(per_owner):
                    start = e * own_width + i * send_width
                    pieces[j * per_owner + i][...] = rows[:, start : start + send_width]

    lane = lax.broadcasted_iota(jnp.int32, (block_len, block_len), 1)
    diagonal = lane == lax.broadcasted_iota(jnp.int32, (block_len, block_len), 0)
    position = lax.broadcasted_iota(jnp.int32, (1, block_len), 1)
    values = hidden[...].astype(jnp.float32)
    coefficient = (gain[...].astype(jnp.float32) * head[...].astype(jnp.float32)).reshape(1, -1)
    inverse = lax.rsqrt(jnp.mean(values * values, axis=1, keepdims=True) + EPSILON)
    scores = jnp.sum(values * coefficient, axis=1, keepdims=True) * inverse
    for b in range(block_count):
        total = jnp.zeros((block_len, 128), jnp.float32)
        for start in range(0, rows.shape[1], 128):
            value = rows[b * block_len : (b + 1) * block_len, start : start + 128]
            value = value.astype(jnp.float32)
            total = total + value * value
        total = jnp.sum(total, axis=1, keepdims=True)
        squares[b : b + 1, :] = jnp.sum(jnp.where(diagonal, total, 0.0), axis=0, keepdims=True)
        weight = jnp.where(position < lengths[b], scores[b : b + 1], 0.0)
        rest[b : b + 1, :] = weight
        rest[block_count + b : block_count + b + 1, :] = jnp.full(
            (1, block_len), order[0, b].astype(jnp.float32)
        )


def store(n_dp, g, first, shards, *refs):
    values = refs[:n_dp]
    gain, weight = refs[n_dp : n_dp + 2]
    out, sums, weights, results, semaphores = refs[-5:]
    chunk, width = values[0].shape
    dp, far = lax.axis_index("dp"), lax.axis_index("mp") >> 1
    own_width = weight.shape[0] // n_dp
    column = pl.multiple_of((far ^ g) * width, 128)
    starts = [pl.multiple_of((dp ^ j) * own_width + first, 16) for j in range(n_dp)]
    loads = [
        pltpu.make_async_copy(
            weight.at[pl.ds(starts[j], chunk), pl.ds(column, width)],
            weights.at[j],
            semaphores.at[0, j],
        )
        for j in range(n_dp)
    ]
    stores = [
        pltpu.make_async_copy(
            results.at[j],
            out.at[pl.ds(starts[j], chunk), pl.ds(column, width)],
            semaphores.at[1, j],
        )
        for j in range(n_dp)
    ]
    for load in loads:
        load.start()
    lane = lax.broadcasted_iota(jnp.int32, (128, 128), 1)
    diagonal = lane == lax.broadcasted_iota(jnp.int32, (128, 128), 0)
    for j in range(n_dp):
        loads[j].wait()
        for at in range(0, chunk, 128):
            gains = gain[:, pl.ds(pl.multiple_of((dp ^ j) * own_width + first + at, 128), 128)]
            gains = jnp.sum(jnp.where(diagonal, gains, 0.0), axis=1, keepdims=True)
            total = values[j][at : at + 128, :].astype(jnp.float32) * (1.0 / shards)
            results[j, at : at + 128, :] = total * gains
            total = total * weights[j, at : at + 128, :].astype(jnp.float32)
            total = jnp.sum(total, axis=1, keepdims=True)
            total = jnp.sum(jnp.where(diagonal, total, 0.0), axis=0, keepdims=True)
            sums[j : j + 1, at : at + 128] = total
        stores[j].start()
    for copy in stores:
        copy.wait()


def body(
    lengths,
    final_hidden,
    score_gain,
    score_head,
    policy_input,
    block_order,
    norm_gain,
    key_weight,
    key_cotangent,
):
    n_section, n_dp, n_mp = (lax.axis_size(name) for name in ("section", "dp", "mp"))
    dp, mp = lax.axis_index("dp"), lax.axis_index("mp")
    block_count = lengths.shape[0]
    tokens, local_width = policy_input.shape
    block_len = tokens // block_count
    pair = block_count // n_dp
    columns = key_cotangent.shape[1]
    own_width = local_width // n_dp
    chunk = min(CHUNK_ROWS, own_width)
    feature_blocks = own_width // chunk
    n_far = n_mp // 2
    far, core = mp >> 1, mp & 1

    cotangents = [key_cotangent] + [swap(key_cotangent, "dp", j) for j in range(1, n_dp)]
    cotangents = jnp.concatenate(cotangents, axis=0)

    per_owner = feature_blocks
    given = (lengths, block_order, final_hidden, score_gain, score_head, policy_input)
    vmem, hbm = pl.BlockSpec(memory_space=pltpu.VMEM), pl.BlockSpec(memory_space=pltpu.MemorySpace.HBM)
    squares, rest, *pieces = pl.pallas_call(
        functools.partial(prepare, n_dp, block_len, chunk),
        out_shape=[
            jax.ShapeDtypeStruct((block_count, block_len), jnp.float32),
            jax.ShapeDtypeStruct((2 * block_count, block_len), jnp.float32),
        ]
        + [jax.ShapeDtypeStruct((tokens, chunk), jnp.bfloat16)] * (n_dp * per_owner),
        in_specs=[hbm] * 6,
        out_specs=[vmem] * (2 + n_dp * per_owner),
        scratch_shapes=[pltpu.SMEM(value.shape, value.dtype) for value in given[:2]]
        + [pltpu.VMEM(value.shape, value.dtype) for value in given[2:]]
        + [pltpu.SemaphoreType.DMA((6,))],
        compiler_params=pltpu.CompilerParams(vmem_limit_bytes=32 * 2**20),
        name="prepare",
    )(*given)
    squares = squares + sum(swap(squares, "mp", j) for j in range(1, n_mp))
    inverse = lax.rsqrt(squares / (local_width * n_mp) + EPSILON)
    small = jnp.concatenate([inverse, rest], axis=0)
    small = [small] + [swap(small, "dp", j) for j in range(1, n_dp)]

    parts = []

    def rows(f):
        got = [pieces[f]]
        for j in range(1, n_dp):
            piece = pieces[j * per_owner + f]
            piece, _ = lax.optimization_barrier((piece, parts[0] if f else small[0]))
            piece = swap(piece, "dp", j)
            if f:
                piece, _ = lax.optimization_barrier((piece, parts[f - 1]))
            got.append(piece)
        return jnp.concatenate(got, axis=0)

    gathered = []

    def key_gradient(near):
        other = swap(near, "mp", 1)
        low = core == 0
        cotangent = jnp.concatenate(
            [jnp.where(low, near, other), jnp.where(low, other, near)], axis=1
        ).reshape(n_dp, n_dp, pair, block_len, -1)
        found = []
        for j in range(n_dp):
            sender = dp ^ j
            for b in range(block_count):
                slot = small[j][2 * block_count + b][:, None]
                chosen = None
                for e in range(n_dp):
                    for q in range(pair):
                        value = lax.dynamic_index_in_dim(cotangent[e], sender, 0, keepdims=False)[q]
                        at = ((dp ^ e) * pair + q).astype(jnp.float32)
                        chosen = value if chosen is None else jnp.where(slot == at, value, chosen)
                weight = small[j][block_count + b].astype(jnp.bfloat16).astype(jnp.float32)
                key_grad = to_bfloat16(chosen.astype(jnp.float32) * weight[:, None])
                found.append(
                    (key_grad.astype(jnp.float32) * small[j][b][:, None]).astype(jnp.bfloat16)
                )
        return jnp.concatenate(found, axis=0)

    for g in range(n_far):
        near = cotangents
        if g:
            near, _ = lax.optimization_barrier((near, parts[0]))
            near = swap(near, "mp", 2 * g)
        key_grad = key_gradient(near)
        for f in range(feature_blocks):
            if not g:
                gathered.append(rows(f))
            part = lax.dot_general(
                gathered[f],
                key_grad,
                (((0,), (0,)), ((), ())),
                preferred_element_type=jnp.float32,
            )
            parts.append(to_bfloat16(part))
    late_gain, _ = lax.optimization_barrier((norm_gain, parts[0]))
    gain = late_gain.astype(jnp.float32)[None, :]
    shards = n_section * n_dp
    out = []
    sums = []

    def shared_sum(total):
        return [total] + [swap(total, "dp", j) for j in range(1, n_dp)]

    def emit(k, values):
        g, f = divmod(k, feature_blocks)
        before = tuple(out)
        result, total = pl.pallas_call(
            functools.partial(store, n_dp, g, f * chunk, shards),
            out_shape=[
                jax.ShapeDtypeStruct((local_width, n_mp * columns), jnp.float32),
                jax.ShapeDtypeStruct((n_dp, chunk), jnp.float32),
            ],
            in_specs=[vmem] * (n_dp + 1) + [hbm] * (1 + len(before)),
            out_specs=[hbm, vmem],
            input_output_aliases={n_dp + 2: 0} if before else {},
            scratch_shapes=[
                pltpu.VMEM((n_dp, chunk, 2 * columns), jnp.bfloat16),
                pltpu.VMEM((n_dp, chunk, 2 * columns), jnp.float32),
                pltpu.SemaphoreType.DMA((2, n_dp)),
            ],
            compiler_params=pltpu.CompilerParams(vmem_limit_bytes=32 * 2**20),
            name="store",
        )(*values, gain, key_weight, *before)
        out[:] = [result]
        sums.append(total)
        return total

    def key_steps():
        yield (inverse,)
        (late_inverse,) = side_values[0]
        normed = policy_input.astype(jnp.float32) * late_inverse.reshape(-1, 1) * gain
        normed = lax.optimization_barrier(normed.astype(jnp.bfloat16))
        partial = jnp.dot(normed, key_weight, preferred_element_type=jnp.float32)
        cut = [partial[:, i * columns : (i + 1) * columns] for i in range(n_mp)]
        yield (partial,)
        (partial,) = side_values[0]
        cut = [partial[:, i * columns : (i + 1) * columns] for i in range(n_mp)]
        own = pick(cut, mp)
        yield (own,) + tuple(
            swap(pick(cut, mp ^ j).astype(jnp.bfloat16), "mp", j) for j in range(1, n_mp)
        )
        own, *others = side_values[0]
        keys = own + sum(other.astype(jnp.float32) for other in others)
        keys = keys.astype(jnp.bfloat16).reshape(block_count, block_len, columns)
        by_slot = []
        for slot in range(block_count):
            chosen = keys[0]
            for b in range(1, block_count):
                chosen = jnp.where(rest[block_count + b][:, None] == slot, keys[b], chosen)
            by_slot.append(chosen)
        by_target = [jnp.concatenate(by_slot[e * pair : (e + 1) * pair]) for e in range(n_dp)]
        yield (pick(by_target, dp),) + tuple(
            swap(pick(by_target, dp ^ j), "dp", j) for j in range(1, n_dp)
        )
        arrived = side_values[0]
        learner_keys.append(jnp.concatenate([pick(arrived, dp ^ a) for a in range(n_dp)], axis=0))

    side_values, learner_keys = [()], []
    steps = key_steps()

    def side(waited):
        side_values[0] = waited
        return next(steps, None)

    summed(parts, shared_sum, emit, side)
    grad_gain = [
        sum(sums[g * feature_blocks + f] for g in range(n_far)) for f in range(feature_blocks)
    ]
    grad_gain = jnp.concatenate(grad_gain, axis=1)
    grad_gain = jnp.concatenate([pick([grad_gain[j] for j in range(n_dp)], dp ^ e) for e in range(n_dp)])
    return learner_keys[0], out[0], grad_gain


def solution(mesh):
    placed = (
        P(("section", "dp")),
        P(("section", "dp"), None),
        P(),
        P(),
        P(("section", "dp"), "mp"),
        P(("section", "dp"), None),
        P("mp"),
        P("mp", None),
        P(("section", "dp"), "mp"),
    )
    return jax.shard_map(
        body,
        mesh=mesh,
        in_specs=placed,
        out_specs=(P(("section", "dp"), "mp"), P("mp", None), P("mp")),
        check_vma=False,
    )
```

```python
import functools

import jax
import jax.numpy as jnp
from jax import lax
from jax.experimental import pallas as pl
from jax.experimental.pallas import tpu as pltpu
from jax.sharding import PartitionSpec as P

EPSILON = 1e-06
CHUNK_ROWS = 256
LAG = 3


def swap(value, axis, bit):
    return lax.ppermute(value, axis, [(i, i ^ bit) for i in range(lax.axis_size(axis))])


def pick(values, index):
    chosen = values[0]
    for i in range(1, len(values)):
        chosen = jnp.where(index == i, values[i], chosen)
    return chosen


def to_bfloat16(value):
    return lax.reduce_precision(value, 8, 7).astype(jnp.bfloat16)


def add(left, right):
    return to_bfloat16(left.astype(jnp.float32) + right.astype(jnp.float32))


def summed(parts, sums, share, emit, side):
    count = len(parts)
    groups = [[0]] + [list(range(k, min(k + 2, count))) for k in range(1, count - 1, 2)]
    groups += [[count - 1]] if count > 1 and groups[-1][-1] != count - 1 else []
    pending = ()
    if lax.axis_size("section") != 4:
        for group in groups:
            found = [to_bfloat16(lax.psum(parts[k].astype(jnp.float32), "section")) for k in group]
            emit(group, share(found))
        while pending is not None:
            pending = side(pending)
        return
    index = lax.axis_index("section")
    inner = (index == 1) | (index == 2)

    def outer_swap(value):
        return lax.ppermute(value, "section", [(0, 1), (1, 0), (2, 3), (3, 2)])

    def middle_swap(value):
        return lax.ppermute(value, "section", [(1, 2), (2, 1), (0, 0), (3, 3)])

    arriving = {k: outer_swap(parts[k]) for k in range(min(LAG, count))}
    halves, others, totals, results = {}, {}, {}, {}
    shares, recent = [], ()
    for k in range(count + LAG):
        tied = ({i: totals[i] for i in (k - 2,) if i in totals}, {i: sums[i] for i in recent})
        got, tied = lax.optimization_barrier((arriving[k], tied))
        totals.update(tied[0])
        sums.update(tied[1])
        if k < count:
            halves[k] = add(parts[k], got)
            others[k] = middle_swap(halves[k])
        if k >= LAG:
            results[k - LAG] = jnp.where(inner, totals[k - LAG], got)
        if k - 1 in others:
            tied = {i: halves[i] for i in (k - 1, k) if i in halves}
            other, tied = lax.optimization_barrier((others[k - 1], tied))
            halves.update(tied)
            totals[k - 1] = add(halves[k - 1], other)
        following = k - 1 + LAG
        if LAG <= following < count + LAG:
            value = totals[following - LAG]
            if following < count:
                value = jnp.where(inner, value, parts[following])
            arriving[following] = outer_swap(value)
        for group in groups:
            if group[-1] == k - LAG:
                tied = {i: totals[i] for i in (k - 1,) if i in totals}
                ready, tied = lax.optimization_barrier(([results[i] for i in group], tied))
                totals.update(tied)
                shares.append((k + len(group), group, share(ready)))
        now = [entry for entry in shares if entry[0] <= k]
        shares = [entry for entry in shares if entry[0] > k]
        tied = {i: totals[i] for i in (k - 1,) if i in totals}
        waited, pending, tied = lax.optimization_barrier(
            ([entry[2] for entry in now], pending, tied)
        )
        totals.update(tied)
        recent = ()
        for (_, group, _), values in zip(now, waited):
            recent += tuple(group)
            emit(group, values)
        if k >= LAG and pending is not None:
            pending = side(pending)
    for _, group, values in shares:
        values, tied = lax.optimization_barrier((values, {i: sums[i] for i in recent}))
        sums.update(tied)
        recent = tuple(group)
        emit(group, values)
    while pending is not None:
        pending = side(pending)


def prepare(n_dp, block_len, width, rows, squares, *pieces):
    dp = lax.axis_index("dp")
    own_width = rows.shape[1] // n_dp
    per_owner = own_width // width
    for j in range(n_dp):
        for e in range(n_dp):

            @pl.when((dp ^ j) == e)
            def _(j=j, e=e):
                for i in range(per_owner):
                    start = e * own_width + i * width
                    pieces[j * per_owner + i][...] = rows[:, start : start + width]

    lane = lax.broadcasted_iota(jnp.int32, (block_len, block_len), 1)
    diagonal = lane == lax.broadcasted_iota(jnp.int32, (block_len, block_len), 0)
    for b in range(squares.shape[0]):
        total = jnp.zeros((block_len, 128), jnp.float32)
        for start in range(0, rows.shape[1], 128):
            value = rows[b * block_len : (b + 1) * block_len, start : start + 128]
            value = value.astype(jnp.float32)
            total = total + value * value
        total = jnp.sum(total, axis=1, keepdims=True)
        squares[b : b + 1, :] = jnp.sum(jnp.where(diagonal, total, 0.0), axis=0, keepdims=True)


def score(lengths, order, hidden, gain, head, rest):
    block_count, block_len = lengths.shape[0], rest.shape[1]
    position = lax.broadcasted_iota(jnp.int32, (1, block_len), 1)
    values = hidden[...].astype(jnp.float32)
    coefficient = (gain[...].astype(jnp.float32) * head[...].astype(jnp.float32)).reshape(1, -1)
    inverse = lax.rsqrt(jnp.mean(values * values, axis=1, keepdims=True) + EPSILON)
    scores = jnp.sum(values * coefficient, axis=1, keepdims=True) * inverse
    for b in range(block_count):
        rest[b : b + 1, :] = jnp.where(position < lengths[b], scores[b : b + 1], 0.0)
        rest[block_count + b : block_count + b + 1, :] = jnp.full(
            (1, block_len), order[0, b].astype(jnp.float32)
        )


def store(n_dp, g, first, offset, shards, *refs):
    values, gain, weight = refs[0], refs[1], refs[2]
    out, sums, results, semaphores = refs[-4:]
    (_, chunk, width) = results.shape
    far = lax.axis_index("mp") >> 1
    own_width = weight.shape[0] // n_dp
    column = pl.multiple_of((far ^ g) * width, 128)
    stores = []
    lane = lax.broadcasted_iota(jnp.int32, (128, 128), 1)
    diagonal = lane == lax.broadcasted_iota(jnp.int32, (128, 128), 0)
    for e in range(n_dp):
        start = e * own_width + first
        for at in range(0, chunk, 128):
            gains = gain[:, start + at : start + at + 128]
            gains = jnp.sum(jnp.where(diagonal, gains, 0.0), axis=1, keepdims=True)
            total = values[e, offset + at : offset + at + 128, :].astype(jnp.float32) * (1.0 / shards)
            results[e, at : at + 128, :] = total * gains
            weights = weight[start + at : start + at + 128, pl.ds(column, width)]
            total = total * weights.astype(jnp.float32)
            total = jnp.sum(total, axis=1, keepdims=True)
            total = jnp.sum(jnp.where(diagonal, total, 0.0), axis=0, keepdims=True)
            sums[e : e + 1, at : at + 128] = total
        copy = pltpu.make_async_copy(
            results.at[e],
            out.at[pl.ds(start, chunk), pl.ds(column, width)],
            semaphores.at[e],
        )
        copy.start()
        stores.append(copy)
    for copy in stores:
        copy.wait()


def body(
    lengths,
    final_hidden,
    score_gain,
    score_head,
    policy_input,
    block_order,
    norm_gain,
    key_weight,
    key_cotangent,
):
    n_section, n_dp, n_mp = (lax.axis_size(name) for name in ("section", "dp", "mp"))
    dp, mp = lax.axis_index("dp"), lax.axis_index("mp")
    block_count = lengths.shape[0]
    tokens, local_width = policy_input.shape
    block_len = tokens // block_count
    pair = block_count // n_dp
    columns = key_cotangent.shape[1]
    own_width = local_width // n_dp
    chunk = min(CHUNK_ROWS, own_width)
    feature_blocks = own_width // chunk
    n_far = n_mp // 2
    far, core = mp >> 1, mp & 1

    cotangents = [key_cotangent] + [swap(key_cotangent, "dp", j) for j in range(1, n_dp)]
    cotangents = jnp.concatenate(cotangents, axis=0)

    per_owner = feature_blocks
    vmem, smem = pl.BlockSpec(memory_space=pltpu.VMEM), pl.BlockSpec(memory_space=pltpu.SMEM)
    hbm = pl.BlockSpec(memory_space=pltpu.MemorySpace.HBM)
    squares, *pieces = pl.pallas_call(
        functools.partial(prepare, n_dp, block_len, chunk),
        out_shape=[jax.ShapeDtypeStruct((block_count, block_len), jnp.float32)]
        + [jax.ShapeDtypeStruct((tokens, chunk), jnp.bfloat16)] * (n_dp * per_owner),
        in_specs=[vmem],
        out_specs=[vmem] * (1 + n_dp * per_owner),
        compiler_params=pltpu.CompilerParams(vmem_limit_bytes=32 * 2**20),
        name="prepare",
    )(policy_input)
    rest = pl.pallas_call(
        score,
        out_shape=jax.ShapeDtypeStruct((2 * block_count, block_len), jnp.float32),
        in_specs=[smem, smem, vmem, vmem, vmem],
        out_specs=vmem,
        name="score",
    )(lengths, block_order, final_hidden, score_gain, score_head)
    squares = squares + sum(swap(squares, "mp", j) for j in range(1, n_mp))
    inverse = lax.rsqrt(squares / (local_width * n_mp) + EPSILON)
    small = jnp.concatenate([inverse, rest], axis=0)
    small = [small] + [swap(small, "dp", j) for j in range(1, n_dp)]

    parts = []

    def rows(f):
        got = [pieces[f]]
        for j in range(1, n_dp):
            piece = pieces[j * per_owner + f]
            tied = parts if f else small
            piece, tied[0] = lax.optimization_barrier((piece, tied[0]))
            got.append(swap(piece, "dp", j))
        return jnp.concatenate(got, axis=0)

    gathered = []

    def key_gradient(near):
        other = swap(near, "mp", 1)
        low = core == 0
        cotangent = jnp.concatenate(
            [jnp.where(low, near, other), jnp.where(low, other, near)], axis=1
        ).reshape(n_dp, n_dp, pair, block_len, -1)
        found = []
        for j in range(n_dp):
            sender = dp ^ j
            for b in range(block_count):
                slot = small[j][2 * block_count + b][:, None]
                chosen = None
                for e in range(n_dp):
                    for q in range(pair):
                        value = lax.dynamic_index_in_dim(cotangent[e], sender, 0, keepdims=False)[q]
                        at = ((dp ^ e) * pair + q).astype(jnp.float32)
                        chosen = value if chosen is None else jnp.where(slot == at, value, chosen)
                weight = small[j][block_count + b].astype(jnp.bfloat16).astype(jnp.float32)
                key_grad = to_bfloat16(chosen.astype(jnp.float32) * weight[:, None])
                found.append(
                    (key_grad.astype(jnp.float32) * small[j][b][:, None]).astype(jnp.bfloat16)
                )
        return jnp.concatenate(found, axis=0)

    for g in range(n_far):
        near = cotangents
        if g:
            near, parts[0] = lax.optimization_barrier((near, parts[0]))
            near = swap(near, "mp", 2 * g)
        key_grad = key_gradient(near)
        for f in range(feature_blocks):
            if not g:
                gathered.append(rows(f))
            part = lax.dot_general(
                gathered[f],
                key_grad,
                (((0,), (0,)), ((), ())),
                preferred_element_type=jnp.float32,
            )
            parts.append(to_bfloat16(part))
    late_gain, parts[0] = lax.optimization_barrier((norm_gain, parts[0]))
    gain = late_gain.astype(jnp.float32)[None, :]
    shards = n_section * n_dp
    out = []
    sums = {}

    def share(values):
        if n_dp == 2 and len(values) == 1:
            return (values[0], swap(values[0], "dp", 1))
        return (lax.all_gather(jnp.concatenate(values, axis=0), "dp"),)

    def emit(group, values):
        if len(values) == 2:
            values = jnp.stack([pick(values, dp), pick(values, 1 - dp)])
        else:
            (values,) = values
        for i, k in enumerate(group):
            g, f = divmod(k, feature_blocks)
            before = tuple(out)
            result, total = pl.pallas_call(
                functools.partial(store, n_dp, g, f * chunk, i * chunk, shards),
                out_shape=[
                    jax.ShapeDtypeStruct((local_width, n_mp * columns), jnp.float32),
                    jax.ShapeDtypeStruct((n_dp, chunk), jnp.float32),
                ],
                in_specs=[vmem] * 3 + [hbm] * len(before),
                out_specs=[hbm, vmem],
                input_output_aliases={3: 0} if before else {},
                scratch_shapes=[
                    pltpu.VMEM((n_dp, chunk, 2 * columns), jnp.float32),
                    pltpu.SemaphoreType.DMA((n_dp,)),
                ],
                compiler_params=pltpu.CompilerParams(vmem_limit_bytes=32 * 2**20),
                name="store",
            )(values, gain, key_weight, *before)
            out[:] = [result]
            sums[k] = total

    def key_steps():
        yield (inverse,)
        (late_inverse,) = side_values[0]
        normed = policy_input.astype(jnp.float32) * late_inverse.reshape(-1, 1) * gain
        normed = lax.optimization_barrier(normed.astype(jnp.bfloat16))
        partial = jnp.dot(normed, key_weight, preferred_element_type=jnp.float32)
        cut = [partial[:, i * columns : (i + 1) * columns] for i in range(n_mp)]
        yield (partial,)
        (partial,) = side_values[0]
        cut = [partial[:, i * columns : (i + 1) * columns] for i in range(n_mp)]
        own = pick(cut, mp)
        yield (own,) + tuple(
            swap(pick(cut, mp ^ j).astype(jnp.bfloat16), "mp", j) for j in range(1, n_mp)
        )
        own, *others = side_values[0]
        keys = own + sum(other.astype(jnp.float32) for other in others)
        keys = keys.astype(jnp.bfloat16).reshape(block_count, block_len, columns)
        by_slot = []
        for slot in range(block_count):
            chosen = keys[0]
            for b in range(1, block_count):
                chosen = jnp.where(rest[block_count + b][:, None] == slot, keys[b], chosen)
            by_slot.append(chosen)
        by_target = [jnp.concatenate(by_slot[e * pair : (e + 1) * pair]) for e in range(n_dp)]
        yield (pick(by_target, dp),) + tuple(
            swap(pick(by_target, dp ^ j), "dp", j) for j in range(1, n_dp)
        )
        arrived = side_values[0]
        learner_keys.append(jnp.concatenate([pick(arrived, dp ^ a) for a in range(n_dp)], axis=0))

    side_values, learner_keys = [()], []
    steps = key_steps()

    def side(waited):
        side_values[0] = waited
        return next(steps, None)

    summed(parts, sums, share, emit, side)
    grad_gain = [
        sum(sums[g * feature_blocks + f] for g in range(n_far)) for f in range(feature_blocks)
    ]
    grad_gain = jnp.concatenate(grad_gain, axis=1)
    grad_gain = grad_gain.reshape(-1)
    return learner_keys[0], out[0], grad_gain


def solution(mesh):
    placed = (
        P(("section", "dp")),
        P(("section", "dp"), None),
        P(),
        P(),
        P(("section", "dp"), "mp"),
        P(("section", "dp"), None),
        P("mp"),
        P("mp", None),
        P(("section", "dp"), "mp"),
    )
    return jax.shard_map(
        body,
        mesh=mesh,
        in_specs=placed,
        out_specs=(P(("section", "dp"), "mp"), P("mp", None), P("mp")),
        check_vma=False,
    )
```

```python
import functools

import jax
import jax.numpy as jnp
from jax import lax
from jax.experimental import pallas as pl
from jax.experimental.pallas import tpu as pltpu
from jax.sharding import PartitionSpec as P

EPSILON = 1e-06
CHUNK_ROWS = 256
LAG = 3


def swap(value, axis, bit):
    return lax.ppermute(value, axis, [(i, i ^ bit) for i in range(lax.axis_size(axis))])


def pick(values, index):
    chosen = values[0]
    for i in range(1, len(values)):
        chosen = jnp.where(index == i, values[i], chosen)
    return chosen


def to_bfloat16(value):
    return lax.reduce_precision(value, 8, 7).astype(jnp.bfloat16)


def add(left, right):
    return to_bfloat16(left.astype(jnp.float32) + right.astype(jnp.float32))


def end_swap(value):
    return lax.ppermute(value, "section", [(0, 1), (1, 0), (2, 3), (3, 2)])


def middle_swap(value):
    return lax.ppermute(value, "section", [(1, 2), (2, 1), (0, 0), (3, 3)])


def summed(parts, arriving, sums, share, emit, side):
    count = len(parts)
    groups = [[0]] + [list(range(k, min(k + 2, count))) for k in range(1, count - 1, 2)]
    groups += [[count - 1]] if count > 1 and groups[-1][-1] != count - 1 else []
    pending = ()
    if lax.axis_size("section") != 4:
        for group in groups:
            found = [to_bfloat16(lax.psum(parts[k].astype(jnp.float32), "section")) for k in group]
            emit(group, share(found))
        while pending is not None:
            pending = side(pending)
        return
    index = lax.axis_index("section")
    inner = (index == 1) | (index == 2)

    halves, others, totals, results = {}, {}, {}, {}
    shares, recent = [], ()
    for k in range(count + LAG):
        tied = ({i: totals[i] for i in (k - 2,) if i in totals}, {i: sums[i] for i in recent})
        got, tied = lax.optimization_barrier((arriving[k], tied))
        totals.update(tied[0])
        sums.update(tied[1])
        if k < count:
            halves[k] = add(parts[k], got)
            others[k] = middle_swap(halves[k])
        if k >= LAG:
            results[k - LAG] = jnp.where(inner, totals[k - LAG], got)
        if k - 1 in others:
            tied = {i: halves[i] for i in (k - 1, k) if i in halves}
            other, tied = lax.optimization_barrier((others[k - 1], tied))
            halves.update(tied)
            totals[k - 1] = add(halves[k - 1], other)
        following = k - 1 + LAG
        if LAG <= following < count + LAG:
            value = totals[following - LAG]
            if following < count:
                value = jnp.where(inner, value, parts[following])
            arriving[following] = end_swap(value)
        for group in groups:
            if group[-1] == k - LAG:
                tied = {i: totals[i] for i in (k - 1,) if i in totals}
                ready, tied = lax.optimization_barrier(([results[i] for i in group], tied))
                totals.update(tied)
                shares.append((k + len(group), group, share(ready)))
        now = [entry for entry in shares if entry[0] <= k]
        shares = [entry for entry in shares if entry[0] > k]
        tied = {i: totals[i] for i in (k - 1,) if i in totals}
        waited, pending, tied = lax.optimization_barrier(
            ([entry[2] for entry in now], pending, tied)
        )
        totals.update(tied)
        recent = ()
        for (_, group, _), values in zip(now, waited):
            recent += tuple(group)
            emit(group, values)
        if k >= LAG and pending is not None:
            pending = side(pending)
    for _, group, values in shares:
        values, tied = lax.optimization_barrier((values, {i: sums[i] for i in recent}))
        sums.update(tied)
        recent = tuple(group)
        emit(group, values)
    while pending is not None:
        pending = side(pending)


def square(block_len, rows, squares):
    lane = lax.broadcasted_iota(jnp.int32, (block_len, block_len), 1)
    diagonal = lane == lax.broadcasted_iota(jnp.int32, (block_len, block_len), 0)
    for b in range(squares.shape[0]):
        total = jnp.zeros((block_len, 128), jnp.float32)
        for start in range(0, rows.shape[1], 128):
            value = rows[b * block_len : (b + 1) * block_len, start : start + 128]
            value = value.astype(jnp.float32)
            total = total + value * value
        total = jnp.sum(total, axis=1, keepdims=True)
        squares[b : b + 1, :] = jnp.sum(jnp.where(diagonal, total, 0.0), axis=0, keepdims=True)


def score(lengths, order, hidden, gain, head, rest):
    block_count, block_len = lengths.shape[0], rest.shape[1]
    position = lax.broadcasted_iota(jnp.int32, (1, block_len), 1)
    values = hidden[...].astype(jnp.float32)
    coefficient = (gain[...].astype(jnp.float32) * head[...].astype(jnp.float32)).reshape(1, -1)
    inverse = lax.rsqrt(jnp.mean(values * values, axis=1, keepdims=True) + EPSILON)
    scores = jnp.sum(values * coefficient, axis=1, keepdims=True) * inverse
    for b in range(block_count):
        weight = jnp.where(position < lengths[b], scores[b : b + 1], 0.0)
        rest[b : b + 1, :] = weight.astype(jnp.bfloat16).astype(jnp.float32)
        rest[block_count + b : block_count + b + 1, :] = jnp.full(
            (1, block_len), order[0, b].astype(jnp.float32)
        )


def scale(n_dp, n_mp, width, order, rest, rows, *refs):
    squares, inverse, pieces = refs[:n_mp], refs[n_mp], refs[n_mp + 1 :]
    block_count, block_len = inverse.shape
    dp = lax.axis_index("dp")
    own_width = rows.shape[1] // n_dp
    per_owner = own_width // width
    total = squares[0][...]
    for other in squares[1:]:
        total = total + other[...]
    inverse[...] = lax.rsqrt(total / (rows.shape[1] * n_mp) + EPSILON)
    factors = inverse[...] * rest[:block_count, :]
    lane = lax.broadcasted_iota(jnp.int32, (block_len, block_len), 1)
    diagonal = lane == lax.broadcasted_iota(jnp.int32, (block_len, block_len), 0)
    sources = []
    for slot in range(block_count):
        source, factor = 0, factors[0:1]
        for b in range(1, block_count):
            here = order[0, b] == slot
            source = jnp.where(here, b, source)
            factor = jnp.where(here, factors[b : b + 1], factor)
        factor = jnp.sum(jnp.where(diagonal, factor, 0.0), axis=1, keepdims=True)
        sources.append((pl.multiple_of(source * block_len, block_len), factor))
    for j in range(n_dp):
        for e in range(n_dp):

            @pl.when((dp ^ j) == e)
            def _(j=j, e=e):
                for i in range(per_owner):
                    start = e * own_width + i * width
                    for slot, (source, factor) in enumerate(sources):
                        value = rows[pl.ds(source, block_len), start : start + width]
                        value = value.astype(jnp.float32) * factor
                        place = slice(slot * block_len, (slot + 1) * block_len)
                        pieces[j * per_owner + i][place, :] = value.astype(jnp.bfloat16)


def store(n_dp, g, first, offset, shards, *refs):
    values, gain, weight = refs[0], refs[1], refs[2]
    out, sums, results, semaphores = refs[-4:]
    (_, chunk, width) = results.shape
    far = lax.axis_index("mp") >> 1
    own_width = weight.shape[0] // n_dp
    column = pl.multiple_of((far ^ g) * width, 128)
    stores = []
    lane = lax.broadcasted_iota(jnp.int32, (128, 128), 1)
    diagonal = lane == lax.broadcasted_iota(jnp.int32, (128, 128), 0)
    for e in range(n_dp):
        start = e * own_width + first
        for at in range(0, chunk, 128):
            gains = gain[:, start + at : start + at + 128]
            gains = jnp.sum(jnp.where(diagonal, gains, 0.0), axis=1, keepdims=True)
            total = values[e, offset + at : offset + at + 128, :].astype(jnp.float32) * (1.0 / shards)
            results[e, at : at + 128, :] = total * gains
            weights = weight[start + at : start + at + 128, pl.ds(column, width)]
            total = total * weights.astype(jnp.float32)
            total = jnp.sum(total, axis=1, keepdims=True)
            total = jnp.sum(jnp.where(diagonal, total, 0.0), axis=0, keepdims=True)
            sums[e : e + 1, at : at + 128] = total
        copy = pltpu.make_async_copy(
            results.at[e],
            out.at[pl.ds(start, chunk), pl.ds(column, width)],
            semaphores.at[e],
        )
        copy.start()
        stores.append(copy)
    for copy in stores:
        copy.wait()


def body(
    lengths,
    final_hidden,
    score_gain,
    score_head,
    policy_input,
    block_order,
    norm_gain,
    key_weight,
    key_cotangent,
):
    n_section, n_dp, n_mp = (lax.axis_size(name) for name in ("section", "dp", "mp"))
    dp, mp = lax.axis_index("dp"), lax.axis_index("mp")
    block_count = lengths.shape[0]
    tokens, local_width = policy_input.shape
    block_len = tokens // block_count
    pair = block_count // n_dp
    columns = key_cotangent.shape[1]
    own_width = local_width // n_dp
    chunk = min(CHUNK_ROWS, own_width)
    feature_blocks = own_width // chunk
    n_far = n_mp // 2
    far, core = mp >> 1, mp & 1

    def in_order(values):
        return [pick(values, dp ^ e) for e in range(n_dp)]

    cotangents = [key_cotangent] + [swap(key_cotangent, "dp", j) for j in range(1, n_dp)]

    vmem, smem = pl.BlockSpec(memory_space=pltpu.VMEM), pl.BlockSpec(memory_space=pltpu.SMEM)
    hbm = pl.BlockSpec(memory_space=pltpu.MemorySpace.HBM)
    squares = pl.pallas_call(
        functools.partial(square, block_len),
        out_shape=jax.ShapeDtypeStruct((block_count, block_len), jnp.float32),
        in_specs=[vmem],
        out_specs=vmem,
        compiler_params=pltpu.CompilerParams(vmem_limit_bytes=32 * 2**20),
        name="square",
    )(policy_input)
    squares = [squares] + [swap(squares, "mp", j) for j in range(1, n_mp)]
    rest = pl.pallas_call(
        score,
        out_shape=jax.ShapeDtypeStruct((2 * block_count, block_len), jnp.float32),
        in_specs=[smem, smem, vmem, vmem, vmem],
        out_specs=vmem,
        name="score",
    )(lengths, block_order, final_hidden, score_gain, score_head)
    inverse, *pieces = pl.pallas_call(
        functools.partial(scale, n_dp, n_mp, chunk),
        out_shape=[jax.ShapeDtypeStruct((block_count, block_len), jnp.float32)]
        + [jax.ShapeDtypeStruct((tokens, chunk), jnp.bfloat16)] * (n_dp * feature_blocks),
        in_specs=[smem] + [vmem] * (2 + n_mp),
        out_specs=[vmem] * (1 + n_dp * feature_blocks),
        compiler_params=pltpu.CompilerParams(vmem_limit_bytes=32 * 2**20),
        name="scale",
    )(block_order, rest, policy_input, *squares)

    cotangents, inverse = lax.optimization_barrier((cotangents, inverse))
    cotangents = jnp.concatenate(in_order(cotangents), axis=0)
    parts, arriving = [], {}

    def rows(f):
        got = [pieces[f]]
        for j in range(1, n_dp):
            piece = pieces[j * feature_blocks + f]
            if f > 1:
                piece, parts[1] = lax.optimization_barrier((piece, parts[1]))
            piece = swap(piece, "dp", j)
            if f:
                piece, parts[f - 1] = lax.optimization_barrier((piece, parts[f - 1]))
            got.append(piece)
        return jnp.concatenate(in_order(got), axis=0)

    gathered = []

    def both_cores(near):
        other = swap(near, "mp", 1)
        cotangent = jnp.concatenate([pick([near, other], core), pick([other, near], core)], axis=1)
        cotangent = cotangent.reshape(n_dp, n_dp, tokens // n_dp, 2 * columns)
        return cotangent.transpose(1, 0, 2, 3).reshape(n_dp * tokens, 2 * columns)

    for g in range(n_far):
        near = cotangents
        if g:
            tied = min(1, len(parts) - 1)
            near, parts[tied] = lax.optimization_barrier((near, parts[tied]))
            near = swap(near, "mp", 2 * g)
        cotangent = both_cores(near)
        for f in range(feature_blocks):
            if not g:
                gathered.append(rows(f))
            part = lax.dot_general(
                gathered[f],
                cotangent,
                (((0,), (0,)), ((), ())),
                preferred_element_type=jnp.float32,
            )
            parts.append(to_bfloat16(part))
            if len(parts) <= LAG and n_section == 4:
                arriving[len(parts) - 1] = end_swap(parts[-1])
    late_gain, parts[1] = lax.optimization_barrier((norm_gain, parts[1]))
    gain = late_gain.astype(jnp.float32)[None, :]
    shards = n_section * n_dp
    out = []
    sums = {}

    def share(values):
        values = jnp.concatenate(values, axis=0)
        if n_dp == 2:
            return (values, swap(values, "dp", 1))
        return (lax.all_gather(values, "dp"),)

    def emit(group, values):
        if len(values) == 2:
            values = jnp.stack(in_order(values))
        else:
            (values,) = values
        for i, k in enumerate(group):
            g, f = divmod(k, feature_blocks)
            before = tuple(out)
            result, total = pl.pallas_call(
                functools.partial(store, n_dp, g, f * chunk, i * chunk, shards),
                out_shape=[
                    jax.ShapeDtypeStruct((local_width, n_mp * columns), jnp.float32),
                    jax.ShapeDtypeStruct((n_dp, chunk), jnp.float32),
                ],
                in_specs=[vmem] * 3 + [hbm] * len(before),
                out_specs=[hbm, vmem],
                input_output_aliases={3: 0} if before else {},
                scratch_shapes=[
                    pltpu.VMEM((n_dp, chunk, 2 * columns), jnp.float32),
                    pltpu.SemaphoreType.DMA((n_dp,)),
                ],
                compiler_params=pltpu.CompilerParams(vmem_limit_bytes=32 * 2**20),
                name="store",
            )(values, gain, key_weight, *before)
            out[:] = [result]
            sums[k] = total

    def key_steps():
        yield (inverse,)
        (late_inverse,) = side_values[0]
        normed = policy_input.astype(jnp.float32) * late_inverse.reshape(-1, 1) * gain
        normed = lax.optimization_barrier(normed.astype(jnp.bfloat16))
        partial = jnp.dot(normed, key_weight, preferred_element_type=jnp.float32)
        cut = [partial[:, i * columns : (i + 1) * columns] for i in range(n_mp)]
        yield (partial,)
        (partial,) = side_values[0]
        cut = [partial[:, i * columns : (i + 1) * columns] for i in range(n_mp)]
        own = pick(cut, mp)
        yield (own,) + tuple(
            swap(pick(cut, mp ^ j).astype(jnp.bfloat16), "mp", j) for j in range(1, n_mp)
        )
        own, *others = side_values[0]
        keys = own + sum(other.astype(jnp.float32) for other in others)
        keys = keys.astype(jnp.bfloat16).reshape(block_count, block_len, columns)
        by_slot = []
        for slot in range(block_count):
            chosen = keys[0]
            for b in range(1, block_count):
                chosen = jnp.where(rest[block_count + b][:, None] == slot, keys[b], chosen)
            by_slot.append(chosen)
        by_target = [jnp.concatenate(by_slot[e * pair : (e + 1) * pair]) for e in range(n_dp)]
        yield (pick(by_target, dp),) + tuple(
            swap(pick(by_target, dp ^ j), "dp", j) for j in range(1, n_dp)
        )
        arrived = side_values[0]
        learner_keys.append(jnp.concatenate(in_order(arrived), axis=0))

    side_values, learner_keys = [()], []
    steps = key_steps()

    def side(waited):
        side_values[0] = waited
        return next(steps, None)

    summed(parts, arriving, sums, share, emit, side)
    grad_gain = [
        sum(sums[g * feature_blocks + f] for g in range(n_far)) for f in range(feature_blocks)
    ]
    grad_gain = jnp.concatenate(grad_gain, axis=1)
    grad_gain = grad_gain.reshape(-1)
    return learner_keys[0], out[0], grad_gain


def solution(mesh):
    placed = (
        P(("section", "dp")),
        P(("section", "dp"), None),
        P(),
        P(),
        P(("section", "dp"), "mp"),
        P(("section", "dp"), None),
        P("mp"),
        P("mp", None),
        P(("section", "dp"), "mp"),
    )
    return jax.shard_map(
        body,
        mesh=mesh,
        in_specs=placed,
        out_specs=(P(("section", "dp"), "mp"), P("mp", None), P("mp")),
        check_vma=False,
    )
```

```python
import functools

import jax
import jax.numpy as jnp
from jax import lax
from jax.experimental import pallas as pl
from jax.experimental.pallas import tpu as pltpu
from jax.sharding import PartitionSpec as P

EPSILON = 1e-06
CHUNK_ROWS = 256
LAG = 3


def swap(value, axis, bit):
    return lax.ppermute(value, axis, [(i, i ^ bit) for i in range(lax.axis_size(axis))])


def pick(values, index):
    chosen = values[0]
    for i in range(1, len(values)):
        chosen = jnp.where(index == i, values[i], chosen)
    return chosen


def to_bfloat16(value):
    return lax.reduce_precision(value, 8, 7).astype(jnp.bfloat16)


def add(left, right):
    return to_bfloat16(left.astype(jnp.float32) + right.astype(jnp.float32))


def end_swap(value):
    return lax.ppermute(value, "section", [(0, 1), (1, 0), (2, 3), (3, 2)])


def middle_swap(value):
    return lax.ppermute(value, "section", [(1, 2), (2, 1), (0, 0), (3, 3)])


def summed(parts, arriving, sums, share, emit, side):
    count = len(parts)
    pending = ()
    if lax.axis_size("section") != 4:
        for k, part in enumerate(parts):
            emit(k, share(to_bfloat16(lax.psum(part.astype(jnp.float32), "section"))))
        while pending is not None:
            pending = side(pending)
        return
    index = lax.axis_index("section")
    inner = (index == 1) | (index == 2)

    halves, others, totals, shares = {}, {}, {}, {}
    recent = ()
    for k in range(count + LAG):
        before = k - 1 - LAG
        tied = ({i: totals[i] for i in (k - 2,) if i in totals}, {i: sums[i] for i in recent})
        got, shared, tied = lax.optimization_barrier((arriving[k], shares.get(before, ()), tied))
        totals.update(tied[0])
        sums.update(tied[1])
        if k >= LAG:
            shares[k - LAG] = share(jnp.where(inner, totals[k - LAG], got))
        if k < count:
            halves[k] = add(parts[k], got)
            others[k] = middle_swap(halves[k])
        if k - 1 in others:
            tied = {i: halves[i] for i in (k - 1, k) if i in halves}
            other, tied = lax.optimization_barrier((others[k - 1], tied))
            halves.update(tied)
            totals[k - 1] = add(halves[k - 1], other)
        following = k - 1 + LAG
        if LAG <= following < count + LAG:
            value = totals[following - LAG]
            if following < count:
                value = jnp.where(inner, value, parts[following])
            arriving[following] = end_swap(value)
        tied = {i: totals[i] for i in (k - 1,) if i in totals}
        shared, pending, tied = lax.optimization_barrier((shared, pending, tied))
        totals.update(tied)
        recent = ()
        if before >= 0:
            recent = (before,)
            emit(before, shared)
        if k >= LAG and pending is not None:
            pending = side(pending)
    tied = {i: sums[i] for i in recent}
    shared, tied = lax.optimization_barrier((shares[count - 1], tied))
    sums.update(tied)
    emit(count - 1, shared)
    while pending is not None:
        pending = side(pending)


def square(block_len, rows, squares, held):
    held[...] = rows[...]
    lane = lax.broadcasted_iota(jnp.int32, (block_len, block_len), 1)
    diagonal = lane == lax.broadcasted_iota(jnp.int32, (block_len, block_len), 0)
    for b in range(squares.shape[0]):
        total = jnp.zeros((block_len, 128), jnp.float32)
        for start in range(0, rows.shape[1], 128):
            value = rows[b * block_len : (b + 1) * block_len, start : start + 128]
            value = value.astype(jnp.float32)
            total = total + value * value
        total = jnp.sum(total, axis=1, keepdims=True)
        squares[b : b + 1, :] = jnp.sum(jnp.where(diagonal, total, 0.0), axis=0, keepdims=True)


def score(lengths, order, hidden, gain, head, rest):
    block_count, block_len = lengths.shape[0], rest.shape[1]
    position = lax.broadcasted_iota(jnp.int32, (1, block_len), 1)
    values = hidden[...].astype(jnp.float32)
    coefficient = (gain[...].astype(jnp.float32) * head[...].astype(jnp.float32)).reshape(1, -1)
    inverse = lax.rsqrt(jnp.mean(values * values, axis=1, keepdims=True) + EPSILON)
    scores = jnp.sum(values * coefficient, axis=1, keepdims=True) * inverse
    for b in range(block_count):
        weight = jnp.where(position < lengths[b], scores[b : b + 1], 0.0)
        rest[b : b + 1, :] = weight.astype(jnp.bfloat16).astype(jnp.float32)
        rest[block_count + b : block_count + b + 1, :] = jnp.full(
            (1, block_len), order[0, b].astype(jnp.float32)
        )


def scale(n_dp, n_mp, width, rest, rows, *refs):
    squares, inverse, pieces = refs[:n_mp], refs[n_mp], refs[n_mp + 1 :]
    block_count, block_len = inverse.shape
    dp = lax.axis_index("dp")
    own_width = rows.shape[1] // n_dp
    per_owner = own_width // width
    total = squares[0][...]
    for other in squares[1:]:
        total = total + other[...]
    inverse[...] = lax.rsqrt(total / (rows.shape[1] * n_mp) + EPSILON)
    factors = inverse[...] * rest[:block_count, :]
    lane = lax.broadcasted_iota(jnp.int32, (block_len, block_len), 1)
    diagonal = lane == lax.broadcasted_iota(jnp.int32, (block_len, block_len), 0)
    order = [jnp.max(rest[block_count + b : block_count + b + 1, :]) for b in range(block_count)]
    sources = []
    for slot in range(block_count):
        source, factor = 0, factors[0:1]
        for b in range(1, block_count):
            here = order[b] == slot
            source = jnp.where(here, b, source)
            factor = jnp.where(here, factors[b : b + 1], factor)
        factor = jnp.sum(jnp.where(diagonal, factor, 0.0), axis=1, keepdims=True)
        sources.append((pl.multiple_of(source * block_len, block_len), factor))
    for j in range(n_dp):
        for e in range(n_dp):

            @pl.when((dp ^ j) == e)
            def _(j=j, e=e):
                for i in range(per_owner):
                    start = e * own_width + i * width
                    for slot, (source, factor) in enumerate(sources):
                        value = rows[pl.ds(source, block_len), start : start + width]
                        value = value.astype(jnp.float32) * factor
                        place = slice(slot * block_len, (slot + 1) * block_len)
                        pieces[j * per_owner + i][place, :] = value.astype(jnp.bfloat16)


def store(n_dp, g, first, shards, *refs):
    values, gain, weight = refs[0], refs[1], refs[2]
    out, sums, results, semaphores = refs[-4:]
    _, chunk, width = results.shape
    far = lax.axis_index("mp") >> 1
    own_width = weight.shape[0] // n_dp
    column = pl.multiple_of((far ^ g) * width, 128)
    stores = []
    lane = lax.broadcasted_iota(jnp.int32, (128, 128), 1)
    diagonal = lane == lax.broadcasted_iota(jnp.int32, (128, 128), 0)
    for e in range(n_dp):
        start = e * own_width + first
        for at in range(0, chunk, 128):
            gains = gain[:, start + at : start + at + 128]
            gains = jnp.sum(jnp.where(diagonal, gains, 0.0), axis=1, keepdims=True)
            total = values[e, at : at + 128, :].astype(jnp.float32) * (1.0 / shards)
            results[e, at : at + 128, :] = total * gains
            weights = weight[start + at : start + at + 128, pl.ds(column, width)]
            total = total * weights.astype(jnp.float32)
            total = jnp.sum(total, axis=1, keepdims=True)
            total = jnp.sum(jnp.where(diagonal, total, 0.0), axis=0, keepdims=True)
            sums[e : e + 1, at : at + 128] = total
        copy = pltpu.make_async_copy(
            results.at[e],
            out.at[pl.ds(start, chunk), pl.ds(column, width)],
            semaphores.at[e],
        )
        copy.start()
        stores.append(copy)
    for copy in stores:
        copy.wait()


def body(
    lengths,
    final_hidden,
    score_gain,
    score_head,
    policy_input,
    block_order,
    norm_gain,
    key_weight,
    key_cotangent,
):
    n_section, n_dp, n_mp = (lax.axis_size(name) for name in ("section", "dp", "mp"))
    dp, mp = lax.axis_index("dp"), lax.axis_index("mp")
    block_count = lengths.shape[0]
    tokens, local_width = policy_input.shape
    block_len = tokens // block_count
    pair = block_count // n_dp
    columns = key_cotangent.shape[1]
    own_width = local_width // n_dp
    chunk = min(CHUNK_ROWS, own_width)
    feature_blocks = own_width // chunk
    n_far = n_mp // 2
    far, core = mp >> 1, mp & 1

    def in_order(values):
        return [pick(values, dp ^ e) for e in range(n_dp)]

    cotangents = [key_cotangent] + [swap(key_cotangent, "dp", j) for j in range(1, n_dp)]

    vmem, smem = pl.BlockSpec(memory_space=pltpu.VMEM), pl.BlockSpec(memory_space=pltpu.SMEM)
    hbm = pl.BlockSpec(memory_space=pltpu.MemorySpace.HBM)
    squares, held = pl.pallas_call(
        functools.partial(square, block_len),
        out_shape=[
            jax.ShapeDtypeStruct((block_count, block_len), jnp.float32),
            jax.ShapeDtypeStruct(policy_input.shape, policy_input.dtype),
        ],
        in_specs=[vmem],
        out_specs=[vmem] * 2,
        compiler_params=pltpu.CompilerParams(vmem_limit_bytes=32 * 2**20),
        name="square",
    )(policy_input)
    squares = [squares] + [swap(squares, "mp", j) for j in range(1, n_mp)]
    rest = pl.pallas_call(
        score,
        out_shape=jax.ShapeDtypeStruct((2 * block_count, block_len), jnp.float32),
        in_specs=[smem, smem, vmem, vmem, vmem],
        out_specs=vmem,
        name="score",
    )(lengths, block_order, final_hidden, score_gain, score_head)
    inverse, *pieces = pl.pallas_call(
        functools.partial(scale, n_dp, n_mp, chunk),
        out_shape=[jax.ShapeDtypeStruct((block_count, block_len), jnp.float32)]
        + [jax.ShapeDtypeStruct((tokens, chunk), jnp.bfloat16)] * (n_dp * feature_blocks),
        in_specs=[vmem] * (2 + n_mp),
        out_specs=[vmem] * (1 + n_dp * feature_blocks),
        compiler_params=pltpu.CompilerParams(vmem_limit_bytes=32 * 2**20),
        name="scale",
    )(rest, held, *squares)

    cotangents, inverse = lax.optimization_barrier((cotangents, inverse))
    cotangents = jnp.concatenate(in_order(cotangents), axis=0)
    parts, arriving, ready = [], {}, []

    def rows(f):
        got = [pieces[f]]
        for j in range(1, n_dp):
            piece = pieces[j * feature_blocks + f]
            if f:
                tied = min(f - 1, 1)
                piece, parts[tied] = lax.optimization_barrier((piece, parts[tied]))
            piece = swap(piece, "dp", j)
            tied, i = (parts, f - 1) if f else (ready, 0)
            piece, tied[i] = lax.optimization_barrier((piece, tied[i]))
            got.append(piece)
        return jnp.concatenate(in_order(got), axis=0)

    gathered = []

    def both_cores(near):
        other = swap(near, "mp", 1)
        cotangent = jnp.concatenate([pick([near, other], core), pick([other, near], core)], axis=1)
        cotangent = cotangent.reshape(n_dp, n_dp, tokens // n_dp, 2 * columns)
        return cotangent.transpose(1, 0, 2, 3).reshape(n_dp * tokens, 2 * columns)

    for g in range(n_far):
        near = cotangents
        if g:
            tied = min(1, len(parts) - 1)
            near, parts[tied] = lax.optimization_barrier((near, parts[tied]))
            near = swap(near, "mp", 2 * g)
        ready[:] = [both_cores(near)]
        for f in range(feature_blocks):
            if not g:
                gathered.append(rows(f))
            part = lax.dot_general(
                gathered[f],
                ready[0],
                (((0,), (0,)), ((), ())),
                preferred_element_type=jnp.float32,
            )
            parts.append(to_bfloat16(part))
            if len(parts) <= LAG and n_section == 4:
                arriving[len(parts) - 1] = end_swap(parts[-1])
    late_gain, parts[1] = lax.optimization_barrier((norm_gain, parts[1]))
    gain = late_gain.astype(jnp.float32)[None, :]
    shards = n_section * n_dp
    out = []
    sums = {}

    def share(value):
        return [value] + [swap(value, "dp", j) for j in range(1, n_dp)]

    def emit(k, values):
        g, f = divmod(k, feature_blocks)
        before = tuple(out)
        result, sums[k] = pl.pallas_call(
            functools.partial(store, n_dp, g, f * chunk, shards),
            out_shape=[
                jax.ShapeDtypeStruct((local_width, n_mp * columns), jnp.float32),
                jax.ShapeDtypeStruct((n_dp, chunk), jnp.float32),
            ],
            in_specs=[vmem] * 3 + [hbm] * len(before),
            out_specs=[hbm, vmem],
            input_output_aliases={3: 0} if before else {},
            scratch_shapes=[
                pltpu.VMEM((n_dp, chunk, 2 * columns), jnp.float32),
                pltpu.SemaphoreType.DMA((n_dp,)),
            ],
            compiler_params=pltpu.CompilerParams(vmem_limit_bytes=32 * 2**20),
            name="store",
        )(jnp.stack(in_order(values)), gain, key_weight, *before)
        out[:] = [result]

    def key_steps():
        yield (inverse,)
        (late_inverse,) = side_values[0]
        normed = held.astype(jnp.float32) * late_inverse.reshape(-1, 1) * gain
        normed = lax.optimization_barrier(normed.astype(jnp.bfloat16))
        partial = jnp.dot(normed, key_weight, preferred_element_type=jnp.float32)
        cut = [partial[:, i * columns : (i + 1) * columns] for i in range(n_mp)]
        yield (partial,)
        (partial,) = side_values[0]
        cut = [partial[:, i * columns : (i + 1) * columns] for i in range(n_mp)]
        own = pick(cut, mp)
        yield (own,) + tuple(
            swap(pick(cut, mp ^ j).astype(jnp.bfloat16), "mp", j) for j in range(1, n_mp)
        )
        own, *others = side_values[0]
        keys = own + sum(other.astype(jnp.float32) for other in others)
        keys = keys.astype(jnp.bfloat16).reshape(block_count, block_len, columns)
        by_slot = []
        for slot in range(block_count):
            chosen = keys[0]
            for b in range(1, block_count):
                chosen = jnp.where(rest[block_count + b][:, None] == slot, keys[b], chosen)
            by_slot.append(chosen)
        by_target = [jnp.concatenate(by_slot[e * pair : (e + 1) * pair]) for e in range(n_dp)]
        yield (pick(by_target, dp),) + tuple(
            swap(pick(by_target, dp ^ j), "dp", j) for j in range(1, n_dp)
        )
        arrived = side_values[0]
        learner_keys.append(jnp.concatenate(in_order(arrived), axis=0))

    side_values, learner_keys = [()], []
    steps = key_steps()

    def side(waited):
        side_values[0] = waited
        return next(steps, None)

    summed(parts, arriving, sums, share, emit, side)
    grad_gain = [
        sum(sums[g * feature_blocks + f] for g in range(n_far)) for f in range(feature_blocks)
    ]
    grad_gain = jnp.concatenate(grad_gain, axis=1)
    grad_gain = grad_gain.reshape(-1)
    return learner_keys[0], out[0], grad_gain


def solution(mesh):
    placed = (
        P(("section", "dp")),
        P(("section", "dp"), None),
        P(),
        P(),
        P(("section", "dp"), "mp"),
        P(("section", "dp"), None),
        P("mp"),
        P("mp", None),
        P(("section", "dp"), "mp"),
    )
    return jax.shard_map(
        body,
        mesh=mesh,
        in_specs=placed,
        out_specs=(P(("section", "dp"), "mp"), P("mp", None), P("mp")),
        check_vma=False,
    )
```

```python
import functools

import jax
import jax.numpy as jnp
from jax import lax
from jax.experimental import pallas as pl
from jax.experimental.pallas import tpu as pltpu
from jax.sharding import PartitionSpec as P

EPSILON = 1e-06
CHUNK_ROWS = 256
LAG = 3
KN = {"groups": (lambda c: [[0], [1, 2], [3, 4], [5], [6], [7]] if c == 8 else [[k] for k in range(c)]), "due": len, "xser": 0, "t1": 0, "t2": 0, "t3": 1, "tA": 0, "tail": 1, "keys": 3, "rpay": (None, 0, 1, 1), "rrecv": (0, 0, 0, 1), "ypay": 0, "yrecv": 0, "ptie": 1}


def swap(value, axis, bit):
    return lax.ppermute(value, axis, [(i, i ^ bit) for i in range(lax.axis_size(axis))])


def pick(values, index):
    chosen = values[0]
    for i in range(1, len(values)):
        chosen = jnp.where(index == i, values[i], chosen)
    return chosen


def to_bfloat16(value):
    return lax.reduce_precision(value, 8, 7).astype(jnp.bfloat16)


def add(left, right):
    return to_bfloat16(left.astype(jnp.float32) + right.astype(jnp.float32))


def end_swap(value):
    return lax.ppermute(value, "section", [(0, 1), (1, 0), (2, 3), (3, 2)])


def middle_swap(value):
    return lax.ppermute(value, "section", [(1, 2), (2, 1), (0, 0), (3, 3)])


def summed(part, count, sums, share, emit, side):
    groups = KN["groups"](count)
    pending = ()
    if lax.axis_size("section") != 4:
        for group in groups:
            found = []
            for k in group:
                value, _ = part(k, None)
                found.append(to_bfloat16(lax.psum(value.astype(jnp.float32), "section")))
            emit(group, share(found))
        while pending is not None:
            pending = side(pending)
        return
    index = lax.axis_index("section")
    inner = (index == 1) | (index == 2)

    parts, arriving, halves, others, totals, results = {}, {}, {}, {}, {}, {}
    for k in range(min(LAG, count)):
        last = parts.get(k - 1)
        parts[k], last = part(k, last)
        if k and KN["ptie"] and last is not None:
            parts[k - 1] = last
        arriving[k] = end_swap(parts[k])
    shares = []
    for k in range(count + LAG):
        tied = {i: totals[i] for i in (k - 2,) if i in totals and KN["t1"]}
        got, tied = lax.optimization_barrier((arriving[k], tied))
        totals.update(tied)
        if k < count:
            halves[k] = add(parts[k], got)
            others[k] = middle_swap(halves[k])
        if LAG + k < count:
            parts[LAG + k], value = part(LAG + k, halves[k])
            if value is not None:
                halves[k] = value
        if k - 1 in others:
            tied = {i: halves[i] for i in (k - 1, k) if i in halves and (i < k or KN["t2"])}
            if KN["tail"] and k >= count:
                other, tied, got = lax.optimization_barrier((others[k - 1], tied, got))
            else:
                other, tied = lax.optimization_barrier((others[k - 1], tied))
            halves.update(tied)
            totals[k - 1] = add(halves[k - 1], other)
        following = k - 1 + LAG
        if LAG <= following < count + LAG:
            value = totals[following - LAG]
            if following < count:
                value = jnp.where(inner, value, parts[following])
            arriving[following] = end_swap(value)
        if k >= LAG:
            results[k - LAG] = jnp.where(inner, totals[k - LAG], got)
            for group in groups:
                if group[-1] == k - LAG:
                    found = [results[i] for i in group]
                    if KN["tA"] and k - 1 in totals:
                        found, totals[k - 1] = lax.optimization_barrier((found, totals[k - 1]))
                    back = KN["xser"]
                    if back and len(shares) >= back and shares[-back] is not None:
                        due, last, values = shares[-back]
                        found, values = lax.optimization_barrier((found, values))
                        shares[-back] = (due, last, values)
                    shares.append((k + KN["due"](group), group, share(found)))
        now = [i for i, entry in enumerate(shares) if entry is not None and entry[0] <= k]
        tied = {i: totals[i] for i in (k - 1,) if i in totals and KN["t3"]}
        if now or (pending is not None and k >= KN["keys"]):
            waited, held, tied = lax.optimization_barrier(
                ([shares[i][2] for i in now], pending if k >= KN["keys"] else (), tied)
            )
            totals.update(tied)
            for i, values in zip(now, waited):
                emit(shares[i][1], values)
                shares[i] = None
            if k >= KN["keys"] and pending is not None:
                pending = side(held)
    for entry in shares:
        if entry is not None:
            emit(entry[1], entry[2])
    while pending is not None:
        pending = side(pending)


def square(block_len, rows, squares, held):
    held[...] = rows[...]
    lane = lax.broadcasted_iota(jnp.int32, (block_len, block_len), 1)
    diagonal = lane == lax.broadcasted_iota(jnp.int32, (block_len, block_len), 0)
    for b in range(squares.shape[0]):
        total = jnp.zeros((block_len, 128), jnp.float32)
        for start in range(0, rows.shape[1], 128):
            value = rows[b * block_len : (b + 1) * block_len, start : start + 128]
            value = value.astype(jnp.float32)
            total = total + value * value
        total = jnp.sum(total, axis=1, keepdims=True)
        squares[b : b + 1, :] = jnp.sum(jnp.where(diagonal, total, 0.0), axis=0, keepdims=True)


def score(lengths, order, hidden, gain, head, rest):
    block_count, block_len = lengths.shape[0], rest.shape[1]
    position = lax.broadcasted_iota(jnp.int32, (1, block_len), 1)
    values = hidden[...].astype(jnp.float32)
    coefficient = (gain[...].astype(jnp.float32) * head[...].astype(jnp.float32)).reshape(1, -1)
    inverse = lax.rsqrt(jnp.mean(values * values, axis=1, keepdims=True) + EPSILON)
    scores = jnp.sum(values * coefficient, axis=1, keepdims=True) * inverse
    for b in range(block_count):
        weight = jnp.where(position < lengths[b], scores[b : b + 1], 0.0)
        rest[b : b + 1, :] = weight.astype(jnp.bfloat16).astype(jnp.float32)
        rest[block_count + b : block_count + b + 1, :] = jnp.full(
            (1, block_len), order[0, b].astype(jnp.float32)
        )


def scale(n_dp, n_mp, width, rest, rows, *refs):
    squares, inverse, pieces = refs[:n_mp], refs[n_mp], refs[n_mp + 1 :]
    block_count, block_len = inverse.shape
    dp = lax.axis_index("dp")
    own_width = rows.shape[1] // n_dp
    per_owner = own_width // width
    total = squares[0][...]
    for other in squares[1:]:
        total = total + other[...]
    inverse[...] = lax.rsqrt(total / (rows.shape[1] * n_mp) + EPSILON)
    factors = inverse[...] * rest[:block_count, :]
    lane = lax.broadcasted_iota(jnp.int32, (block_len, block_len), 1)
    diagonal = lane == lax.broadcasted_iota(jnp.int32, (block_len, block_len), 0)
    order = [jnp.max(rest[block_count + b : block_count + b + 1, :]) for b in range(block_count)]
    sources = []
    for slot in range(block_count):
        source, factor = 0, factors[0:1]
        for b in range(1, block_count):
            here = order[b] == slot
            source = jnp.where(here, b, source)
            factor = jnp.where(here, factors[b : b + 1], factor)
        factor = jnp.sum(jnp.where(diagonal, factor, 0.0), axis=1, keepdims=True)
        sources.append((pl.multiple_of(source * block_len, block_len), factor))
    for j in range(n_dp):
        for e in range(n_dp):

            @pl.when((dp ^ j) == e)
            def _(j=j, e=e):
                for i in range(per_owner):
                    start = e * own_width + i * width
                    for slot, (source, factor) in enumerate(sources):
                        value = rows[pl.ds(source, block_len), start : start + width]
                        value = value.astype(jnp.float32) * factor
                        place = slice(slot * block_len, (slot + 1) * block_len)
                        pieces[j * per_owner + i][place, :] = value.astype(jnp.bfloat16)


def store(n_dp, g, first, offset, shards, *refs):
    values, gain, weight = refs[0], refs[1], refs[2]
    out, sums, results, semaphores = refs[-4:]
    _, chunk, width = results.shape
    far = lax.axis_index("mp") >> 1
    own_width = weight.shape[0] // n_dp
    column = pl.multiple_of((far ^ g) * width, 128)
    stores = []
    lane = lax.broadcasted_iota(jnp.int32, (128, 128), 1)
    diagonal = lane == lax.broadcasted_iota(jnp.int32, (128, 128), 0)
    for e in range(n_dp):
        start = e * own_width + first
        for at in range(0, chunk, 128):
            gains = gain[:, start + at : start + at + 128]
            gains = jnp.sum(jnp.where(diagonal, gains, 0.0), axis=1, keepdims=True)
            total = values[e, offset + at : offset + at + 128, :].astype(jnp.float32) * (1.0 / shards)
            results[e, at : at + 128, :] = total * gains
            weights = weight[start + at : start + at + 128, pl.ds(column, width)]
            total = total * weights.astype(jnp.float32)
            total = jnp.sum(total, axis=1, keepdims=True)
            total = jnp.sum(jnp.where(diagonal, total, 0.0), axis=0, keepdims=True)
            sums[e : e + 1, at : at + 128] = total
        copy = pltpu.make_async_copy(
            results.at[e],
            out.at[pl.ds(start, chunk), pl.ds(column, width)],
            semaphores.at[e],
        )
        copy.start()
        stores.append(copy)
    for copy in stores:
        copy.wait()


def body(
    lengths,
    final_hidden,
    score_gain,
    score_head,
    policy_input,
    block_order,
    norm_gain,
    key_weight,
    key_cotangent,
):
    n_section, n_dp, n_mp = (lax.axis_size(name) for name in ("section", "dp", "mp"))
    dp, mp = lax.axis_index("dp"), lax.axis_index("mp")
    block_count = lengths.shape[0]
    tokens, local_width = policy_input.shape
    block_len = tokens // block_count
    pair = block_count // n_dp
    columns = key_cotangent.shape[1]
    own_width = local_width // n_dp
    chunk = min(CHUNK_ROWS, own_width)
    feature_blocks = own_width // chunk
    n_far = n_mp // 2
    far, core = mp >> 1, mp & 1

    def in_order(values):
        return [pick(values, dp ^ e) for e in range(n_dp)]

    vmem, smem = pl.BlockSpec(memory_space=pltpu.VMEM), pl.BlockSpec(memory_space=pltpu.SMEM)
    hbm = pl.BlockSpec(memory_space=pltpu.MemorySpace.HBM)
    squares, held = pl.pallas_call(
        functools.partial(square, block_len),
        out_shape=[
            jax.ShapeDtypeStruct((block_count, block_len), jnp.float32),
            jax.ShapeDtypeStruct(policy_input.shape, policy_input.dtype),
        ],
        in_specs=[vmem],
        out_specs=[vmem] * 2,
        compiler_params=pltpu.CompilerParams(vmem_limit_bytes=32 * 2**20),
        name="square",
    )(policy_input)
    squares = [squares] + [swap(squares, "mp", j) for j in range(1, n_mp)]
    cotangents, squares[0] = lax.optimization_barrier((key_cotangent, squares[0]))
    cotangents = [cotangents] + [swap(cotangents, "dp", j) for j in range(1, n_dp)]
    rest = pl.pallas_call(
        score,
        out_shape=jax.ShapeDtypeStruct((2 * block_count, block_len), jnp.float32),
        in_specs=[smem, smem, vmem, vmem, vmem],
        out_specs=vmem,
        name="score",
    )(lengths, block_order, final_hidden, score_gain, score_head)
    inverse, *pieces = pl.pallas_call(
        functools.partial(scale, n_dp, n_mp, chunk),
        out_shape=[jax.ShapeDtypeStruct((block_count, block_len), jnp.float32)]
        + [jax.ShapeDtypeStruct((tokens, chunk), jnp.bfloat16)] * (n_dp * feature_blocks),
        in_specs=[vmem] * (2 + n_mp),
        out_specs=[vmem] * (1 + n_dp * feature_blocks),
        compiler_params=pltpu.CompilerParams(vmem_limit_bytes=32 * 2**20),
        name="scale",
    )(rest, held, *squares)

    cotangents, inverse = lax.optimization_barrier((cotangents, inverse))
    cotangents = jnp.concatenate(in_order(cotangents), axis=0)
    def both_cores(near):
        other = swap(near, "mp", 1)
        cotangent = jnp.concatenate([pick([near, other], core), pick([other, near], core)], axis=1)
        cotangent = cotangent.reshape(n_dp, n_dp, tokens // n_dp, 2 * columns)
        return cotangent.transpose(1, 0, 2, 3).reshape(n_dp * tokens, 2 * columns)

    ready, moved, first = {}, {}, {}

    def send(f):
        got = [pieces[f]]
        for j in range(1, n_dp):
            piece = pieces[j * feature_blocks + f]
            tie = KN["rpay"][f] if n_dp == 2 else None
            if tie is not None:
                piece, first[tie] = lax.optimization_barrier((piece, first[tie]))
            got.append(swap(piece, "dp", j))
        return got

    def columns_of(g, value):
        near = cotangents
        if g:
            if KN["ypay"] is not None:
                near, first[KN["ypay"]] = lax.optimization_barrier((near, first[KN["ypay"]]))
            near = swap(near, "mp", 2 * g)
            if KN["yrecv"] and value is not None:
                near, value = lax.optimization_barrier((near, value))
        return both_cores(near), value

    def part(k, value):
        g, f = divmod(k, feature_blocks)
        if g not in ready:
            ready[g], value = columns_of(g, value)
        if f not in moved:
            got = send(f)
            if not f:
                got, ready[0] = lax.optimization_barrier((got, ready[0]))
            elif KN["rrecv"][f] and value is not None:
                got, value = lax.optimization_barrier((got, value))
            moved[f] = jnp.concatenate(in_order(got), axis=0)
        found = to_bfloat16(
            lax.dot_general(
                moved[f], ready[g], (((0,), (0,)), ((), ())), preferred_element_type=jnp.float32
            )
        )
        if k < 2:
            first[k] = found
        return found, value

    late_gain = norm_gain
    gain = late_gain.astype(jnp.float32)[None, :]
    shards = n_section * n_dp
    out = []
    sums = {}

    def share(values):
        values = jnp.concatenate(values, axis=0)
        if n_dp == 2:
            return (values, swap(values, "dp", 1))
        return (lax.all_gather(values, "dp"),)

    def emit(group, values):
        if len(values) == 2:
            values = jnp.stack(in_order(values))
        else:
            (values,) = values
        for i, k in enumerate(group):
            g, f = divmod(k, feature_blocks)
            before = tuple(out)
            result, total = pl.pallas_call(
                functools.partial(store, n_dp, g, f * chunk, i * chunk, shards),
                out_shape=[
                    jax.ShapeDtypeStruct((local_width, n_mp * columns), jnp.float32),
                    jax.ShapeDtypeStruct((n_dp, chunk), jnp.float32),
                ],
                in_specs=[vmem] * 3 + [hbm] * len(before),
                out_specs=[hbm, vmem],
                input_output_aliases={3: 0} if before else {},
                scratch_shapes=[
                    pltpu.VMEM((n_dp, chunk, 2 * columns), jnp.float32),
                    pltpu.SemaphoreType.DMA((n_dp,)),
                ],
                compiler_params=pltpu.CompilerParams(vmem_limit_bytes=32 * 2**20),
                name="store",
            )(values, gain, key_weight, *before)
            out[:] = [result]
            sums[k] = total

    def key_steps():
        yield (inverse,)
        (late_inverse,) = side_values[0]
        normed = held.astype(jnp.float32) * late_inverse.reshape(-1, 1) * gain
        normed = lax.optimization_barrier(normed.astype(jnp.bfloat16))
        partial = jnp.dot(normed, key_weight, preferred_element_type=jnp.float32)
        yield (partial,)
        (partial,) = side_values[0]
        cut = [partial[:, i * columns : (i + 1) * columns] for i in range(n_mp)]
        own = pick(cut, mp)
        yield (own,) + tuple(
            swap(pick(cut, mp ^ j).astype(jnp.bfloat16), "mp", j) for j in range(1, n_mp)
        )
        own, *others = side_values[0]
        keys = own + sum(other.astype(jnp.float32) for other in others)
        keys = keys.astype(jnp.bfloat16).reshape(block_count, block_len, columns)
        by_slot = []
        for slot in range(block_count):
            chosen = keys[0]
            for b in range(1, block_count):
                chosen = jnp.where(rest[block_count + b][:, None] == slot, keys[b], chosen)
            by_slot.append(chosen)
        by_target = [jnp.concatenate(by_slot[e * pair : (e + 1) * pair]) for e in range(n_dp)]
        yield (pick(by_target, dp),) + tuple(
            swap(pick(by_target, dp ^ j), "dp", j) for j in range(1, n_dp)
        )
        arrived = side_values[0]
        learner_keys.append(jnp.concatenate(in_order(arrived), axis=0))

    side_values, learner_keys = [()], []
    steps = key_steps()

    def side(waited):
        side_values[0] = waited
        return next(steps, None)

    summed(part, n_far * feature_blocks, sums, share, emit, side)
    grad_gain = [
        sum(sums[g * feature_blocks + f] for g in range(n_far)) for f in range(feature_blocks)
    ]
    grad_gain = jnp.concatenate(grad_gain, axis=1)
    grad_gain = grad_gain.reshape(-1)
    return learner_keys[0], out[0], grad_gain


def solution(mesh):
    placed = (
        P(("section", "dp")),
        P(("section", "dp"), None),
        P(),
        P(),
        P(("section", "dp"), "mp"),
        P(("section", "dp"), None),
        P("mp"),
        P("mp", None),
        P(("section", "dp"), "mp"),
    )
    return jax.shard_map(
        body,
        mesh=mesh,
        in_specs=placed,
        out_specs=(P(("section", "dp"), "mp"), P("mp", None), P("mp")),
        check_vma=False,
    )
```

```python
import functools

import jax
import jax.numpy as jnp
from jax import lax
from jax.experimental import pallas as pl
from jax.experimental.pallas import tpu as pltpu
from jax.sharding import PartitionSpec as P

EPSILON = 1e-06
CHUNK_ROWS = 256
LAG = 3
KN = {"groups": (lambda c: [[k] for k in range(c)]), "due": (lambda g: 1), "xser": 0, "t1": 0, "t2": 1, "t3": 1, "tA": 0, "tail": 1, "keys": 4, "rpay": (0, 1, 2, 2), "rrecv": (0, 0, 1, 1), "ypay": 1, "yrecv": 1, "ptie": 0, "lead": 2, "kpre": 0}


def swap(value, axis, bit):
    return lax.ppermute(value, axis, [(i, i ^ bit) for i in range(lax.axis_size(axis))])


def pick(values, index):
    chosen = values[0]
    for i in range(1, len(values)):
        chosen = jnp.where(index == i, values[i], chosen)
    return chosen


def to_bfloat16(value):
    return lax.reduce_precision(value, 8, 7).astype(jnp.bfloat16)


def add(left, right):
    return to_bfloat16(left.astype(jnp.float32) + right.astype(jnp.float32))


def end_swap(value):
    return lax.ppermute(value, "section", [(0, 1), (1, 0), (2, 3), (3, 2)])


def middle_swap(value):
    return lax.ppermute(value, "section", [(1, 2), (2, 1), (0, 0), (3, 3)])


def summed(part, count, sums, share, emit, side):
    groups = KN["groups"](count)
    pending = ()
    if lax.axis_size("section") != 4:
        for group in groups:
            found = []
            for k in group:
                value, _ = part(k, None)
                found.append(to_bfloat16(lax.psum(value.astype(jnp.float32), "section")))
            emit(group, share(found))
        while pending is not None:
            pending = side(pending)
        return
    index = lax.axis_index("section")
    inner = (index == 1) | (index == 2)

    parts, arriving, halves, others, totals, results = {}, {}, {}, {}, {}, {}
    for k in range(min(KN["lead"], count)):
        last = parts.get(k - 1)
        parts[k], last = part(k, last)
        if k and KN["ptie"] and last is not None:
            parts[k - 1] = last
        arriving[k] = end_swap(parts[k])
    shares = []
    if KN["kpre"]:
        pending, parts[1] = lax.optimization_barrier((side(()), parts[1]))
        pending = side(pending)
        if KN["kpre"] == 2:
            pending, parts[1] = lax.optimization_barrier((pending, parts[1]))
            pending = side(pending)
    for k in range(count + LAG):
        tied = {i: totals[i] for i in (k - 2,) if i in totals and KN["t1"]}
        got, tied = lax.optimization_barrier((arriving[k], tied))
        totals.update(tied)
        if k < count:
            halves[k] = add(parts[k], got)
            others[k] = middle_swap(halves[k])
        for i in range(LAG + k if k else KN["lead"], min(LAG + k + 1, count)):
            parts[i], value = part(i, halves[k])
            if value is not None:
                halves[k] = value
            if i < LAG:
                arriving[i] = end_swap(parts[i])
        if k - 1 in others:
            tied = {i: halves[i] for i in (k - 1, k) if i in halves and (i < k or KN["t2"])}
            if KN["tail"] and k >= count:
                other, tied, got = lax.optimization_barrier((others[k - 1], tied, got))
            else:
                other, tied = lax.optimization_barrier((others[k - 1], tied))
            halves.update(tied)
            totals[k - 1] = add(halves[k - 1], other)
        following = k - 1 + LAG
        if LAG <= following < count + LAG:
            value = totals[following - LAG]
            if following < count:
                value = jnp.where(inner, value, parts[following])
            arriving[following] = end_swap(value)
        if k >= LAG:
            results[k - LAG] = jnp.where(inner, totals[k - LAG], got)
            for group in groups:
                if group[-1] == k - LAG:
                    found = [results[i] for i in group]
                    if KN["tA"] and k - 1 in totals:
                        found, totals[k - 1] = lax.optimization_barrier((found, totals[k - 1]))
                    back = KN["xser"]
                    if back and len(shares) >= back and shares[-back] is not None:
                        due, last, values = shares[-back]
                        found, values = lax.optimization_barrier((found, values))
                        shares[-back] = (due, last, values)
                    shares.append((k + KN["due"](group), group, share(found)))
        now = [i for i, entry in enumerate(shares) if entry is not None and entry[0] <= k]
        tied = {i: totals[i] for i in (k - 1,) if i in totals and KN["t3"]}
        if now or (pending is not None and k >= KN["keys"]):
            waited, held, tied = lax.optimization_barrier(
                ([shares[i][2] for i in now], pending if k >= KN["keys"] else (), tied)
            )
            totals.update(tied)
            for i, values in zip(now, waited):
                emit(shares[i][1], values)
                shares[i] = None
            if k >= KN["keys"] and pending is not None:
                pending = side(held)
    for entry in shares:
        if entry is not None:
            emit(entry[1], entry[2])
    while pending is not None:
        pending = side(pending)


def square(block_len, rows, squares, held):
    held[...] = rows[...]
    lane = lax.broadcasted_iota(jnp.int32, (block_len, block_len), 1)
    diagonal = lane == lax.broadcasted_iota(jnp.int32, (block_len, block_len), 0)
    for b in range(squares.shape[0]):
        total = jnp.zeros((block_len, 128), jnp.float32)
        for start in range(0, rows.shape[1], 128):
            value = rows[b * block_len : (b + 1) * block_len, start : start + 128]
            value = value.astype(jnp.float32)
            total = total + value * value
        total = jnp.sum(total, axis=1, keepdims=True)
        squares[b : b + 1, :] = jnp.sum(jnp.where(diagonal, total, 0.0), axis=0, keepdims=True)


def score(lengths, order, hidden, gain, head, rest):
    block_count, block_len = lengths.shape[0], rest.shape[1]
    position = lax.broadcasted_iota(jnp.int32, (1, block_len), 1)
    values = hidden[...].astype(jnp.float32)
    coefficient = (gain[...].astype(jnp.float32) * head[...].astype(jnp.float32)).reshape(1, -1)
    inverse = lax.rsqrt(jnp.mean(values * values, axis=1, keepdims=True) + EPSILON)
    scores = jnp.sum(values * coefficient, axis=1, keepdims=True) * inverse
    for b in range(block_count):
        weight = jnp.where(position < lengths[b], scores[b : b + 1], 0.0)
        rest[b : b + 1, :] = weight.astype(jnp.bfloat16).astype(jnp.float32)
        rest[block_count + b : block_count + b + 1, :] = jnp.full(
            (1, block_len), order[0, b].astype(jnp.float32)
        )


def scale(n_dp, n_mp, width, rest, rows, *refs):
    squares, (inverse, places), pieces = refs[:n_mp], refs[n_mp : n_mp + 2], refs[n_mp + 2 :]
    block_count, block_len = inverse.shape
    dp = lax.axis_index("dp")
    own_width = rows.shape[1] // n_dp
    per_owner = own_width // width
    total = squares[0][...]
    for other in squares[1:]:
        total = total + other[...]
    inverse[...] = lax.rsqrt(total / (rows.shape[1] * n_mp) + EPSILON)
    places[...] = rest[block_count:, :]
    factors = inverse[...] * rest[:block_count, :]
    lane = lax.broadcasted_iota(jnp.int32, (block_len, block_len), 1)
    diagonal = lane == lax.broadcasted_iota(jnp.int32, (block_len, block_len), 0)
    order = [jnp.max(rest[block_count + b : block_count + b + 1, :]) for b in range(block_count)]
    sources = []
    for slot in range(block_count):
        source, factor = 0, factors[0:1]
        for b in range(1, block_count):
            here = order[b] == slot
            source = jnp.where(here, b, source)
            factor = jnp.where(here, factors[b : b + 1], factor)
        factor = jnp.sum(jnp.where(diagonal, factor, 0.0), axis=1, keepdims=True)
        sources.append((pl.multiple_of(source * block_len, block_len), factor))
    for j in range(n_dp):
        for e in range(n_dp):

            @pl.when((dp ^ j) == e)
            def _(j=j, e=e):
                for i in range(per_owner):
                    start = e * own_width + i * width
                    for slot, (source, factor) in enumerate(sources):
                        value = rows[pl.ds(source, block_len), start : start + width]
                        value = value.astype(jnp.float32) * factor
                        place = slice(slot * block_len, (slot + 1) * block_len)
                        pieces[j * per_owner + i][place, :] = value.astype(jnp.bfloat16)


def store(n_dp, g, first, offset, shards, *refs):
    values, gain, weight = refs[0], refs[1], refs[2]
    out, sums, results, semaphores = refs[-4:]
    _, chunk, width = results.shape
    far = lax.axis_index("mp") >> 1
    own_width = weight.shape[0] // n_dp
    column = pl.multiple_of((far ^ g) * width, 128)
    stores = []
    lane = lax.broadcasted_iota(jnp.int32, (128, 128), 1)
    diagonal = lane == lax.broadcasted_iota(jnp.int32, (128, 128), 0)
    for e in range(n_dp):
        start = e * own_width + first
        for at in range(0, chunk, 128):
            gains = gain[:, start + at : start + at + 128]
            gains = jnp.sum(jnp.where(diagonal, gains, 0.0), axis=1, keepdims=True)
            total = values[e, offset + at : offset + at + 128, :].astype(jnp.float32) * (1.0 / shards)
            results[e, at : at + 128, :] = total * gains
            weights = weight[start + at : start + at + 128, pl.ds(column, width)]
            total = total * weights.astype(jnp.float32)
            total = jnp.sum(total, axis=1, keepdims=True)
            total = jnp.sum(jnp.where(diagonal, total, 0.0), axis=0, keepdims=True)
            sums[e : e + 1, at : at + 128] = total
        copy = pltpu.make_async_copy(
            results.at[e],
            out.at[pl.ds(start, chunk), pl.ds(column, width)],
            semaphores.at[e],
        )
        copy.start()
        stores.append(copy)
    for copy in stores:
        copy.wait()


def body(
    lengths,
    final_hidden,
    score_gain,
    score_head,
    policy_input,
    block_order,
    norm_gain,
    key_weight,
    key_cotangent,
):
    n_section, n_dp, n_mp = (lax.axis_size(name) for name in ("section", "dp", "mp"))
    dp, mp = lax.axis_index("dp"), lax.axis_index("mp")
    block_count = lengths.shape[0]
    tokens, local_width = policy_input.shape
    block_len = tokens // block_count
    pair = block_count // n_dp
    columns = key_cotangent.shape[1]
    own_width = local_width // n_dp
    chunk = min(CHUNK_ROWS, own_width)
    feature_blocks = own_width // chunk
    n_far = n_mp // 2
    far, core = mp >> 1, mp & 1

    def in_order(values):
        return [pick(values, dp ^ e) for e in range(n_dp)]

    vmem, smem = pl.BlockSpec(memory_space=pltpu.VMEM), pl.BlockSpec(memory_space=pltpu.SMEM)
    hbm = pl.BlockSpec(memory_space=pltpu.MemorySpace.HBM)
    squares, held = pl.pallas_call(
        functools.partial(square, block_len),
        out_shape=[
            jax.ShapeDtypeStruct((block_count, block_len), jnp.float32),
            jax.ShapeDtypeStruct(policy_input.shape, policy_input.dtype),
        ],
        in_specs=[vmem],
        out_specs=[vmem] * 2,
        compiler_params=pltpu.CompilerParams(vmem_limit_bytes=32 * 2**20),
        name="square",
    )(policy_input)
    squares = [squares] + [swap(squares, "mp", j) for j in range(1, n_mp)]
    cotangents, squares[0] = lax.optimization_barrier((key_cotangent, squares[0]))
    cotangents = [cotangents] + [swap(cotangents, "dp", j) for j in range(1, n_dp)]
    rest = pl.pallas_call(
        score,
        out_shape=jax.ShapeDtypeStruct((2 * block_count, block_len), jnp.float32),
        in_specs=[smem, smem, vmem, vmem, vmem],
        out_specs=vmem,
        name="score",
    )(lengths, block_order, final_hidden, score_gain, score_head)
    inverse, places, *pieces = pl.pallas_call(
        functools.partial(scale, n_dp, n_mp, chunk),
        out_shape=[jax.ShapeDtypeStruct((block_count, block_len), jnp.float32)] * 2
        + [jax.ShapeDtypeStruct((tokens, chunk), jnp.bfloat16)] * (n_dp * feature_blocks),
        in_specs=[vmem] * (2 + n_mp),
        out_specs=[vmem] * (2 + n_dp * feature_blocks),
        compiler_params=pltpu.CompilerParams(vmem_limit_bytes=32 * 2**20),
        name="scale",
    )(rest, held, *squares)

    cotangents, inverse = lax.optimization_barrier((cotangents, inverse))
    cotangents = jnp.concatenate(in_order(cotangents), axis=0)
    def both_cores(near):
        other = swap(near, "mp", 1)
        cotangent = jnp.concatenate([pick([near, other], core), pick([other, near], core)], axis=1)
        cotangent = cotangent.reshape(n_dp, n_dp, tokens // n_dp, 2 * columns)
        return cotangent.transpose(1, 0, 2, 3).reshape(n_dp * tokens, 2 * columns)

    ready, moved = {}, {}

    def send(f, value):
        got = [pieces[f]]
        for j in range(1, n_dp):
            piece = pieces[j * feature_blocks + f]
            if n_dp == 2 and KN["rpay"][f] == 1:
                piece, ready[0] = lax.optimization_barrier((piece, ready[0]))
            elif n_dp == 2 and KN["rpay"][f] == 2 and value is not None:
                piece, value = lax.optimization_barrier((piece, value))
            got.append(swap(piece, "dp", j))
        return got, value

    def columns_of(g, value):
        near = cotangents
        if g:
            if KN["ypay"] == 1:
                near, ready[0] = lax.optimization_barrier((near, ready[0]))
            elif KN["ypay"] == 2 and value is not None:
                near, value = lax.optimization_barrier((near, value))
            near = swap(near, "mp", 2 * g)
            if KN["yrecv"] and value is not None:
                near, value = lax.optimization_barrier((near, value))
        return both_cores(near), value

    def part(k, value):
        g, f = divmod(k, feature_blocks)
        if g not in ready:
            ready[g], value = columns_of(g, value)
        if f not in moved:
            got, value = send(f, value)
            if not f:
                got, ready[0] = lax.optimization_barrier((got, ready[0]))
            elif KN["rrecv"][f] and value is not None:
                got, value = lax.optimization_barrier((got, value))
            moved[f] = jnp.concatenate(in_order(got), axis=0)
        found = to_bfloat16(
            lax.dot_general(
                moved[f], ready[g], (((0,), (0,)), ((), ())), preferred_element_type=jnp.float32
            )
        )
        return found, value

    shards = n_section * n_dp
    out = []
    sums = {}

    def share(values):
        values = jnp.concatenate(values, axis=0)
        if n_dp == 2:
            return (values, swap(values, "dp", 1))
        return (lax.all_gather(values, "dp"),)

    def emit(group, values):
        values, late_gain = lax.optimization_barrier((values, norm_gain))
        gain = late_gain.astype(jnp.float32)[None, :]
        if len(values) == 2:
            values = jnp.stack(in_order(values))
        else:
            (values,) = values
        for i, k in enumerate(group):
            g, f = divmod(k, feature_blocks)
            before = tuple(out)
            result, total = pl.pallas_call(
                functools.partial(store, n_dp, g, f * chunk, i * chunk, shards),
                out_shape=[
                    jax.ShapeDtypeStruct((local_width, n_mp * columns), jnp.float32),
                    jax.ShapeDtypeStruct((n_dp, chunk), jnp.float32),
                ],
                in_specs=[vmem] * 3 + [hbm] * len(before),
                out_specs=[hbm, vmem],
                input_output_aliases={3: 0} if before else {},
                scratch_shapes=[
                    pltpu.VMEM((n_dp, chunk, 2 * columns), jnp.float32),
                    pltpu.SemaphoreType.DMA((n_dp,)),
                ],
                compiler_params=pltpu.CompilerParams(vmem_limit_bytes=32 * 2**20),
                name="store",
            )(values, gain, key_weight, *before)
            out[:] = [result]
            sums[k] = total

    def key_steps():
        yield (inverse, places, norm_gain)
        late_inverse, late_places, late_gain = side_values[0]
        gain = late_gain.astype(jnp.float32)[None, :]
        normed = held.astype(jnp.float32) * late_inverse.reshape(-1, 1) * gain
        normed = lax.optimization_barrier(normed.astype(jnp.bfloat16))
        partial = jnp.dot(normed, key_weight, preferred_element_type=jnp.float32)
        yield (partial,)
        (partial,) = side_values[0]
        cut = [partial[:, i * columns : (i + 1) * columns] for i in range(n_mp)]
        own = pick(cut, mp)
        yield (own,) + tuple(
            swap(pick(cut, mp ^ j).astype(jnp.bfloat16), "mp", j) for j in range(1, n_mp)
        )
        own, *others = side_values[0]
        keys = own + sum(other.astype(jnp.float32) for other in others)
        keys = keys.astype(jnp.bfloat16).reshape(block_count, block_len, columns)
        by_slot = []
        for slot in range(block_count):
            chosen = keys[0]
            for b in range(1, block_count):
                chosen = jnp.where(late_places[b][:, None] == slot, keys[b], chosen)
            by_slot.append(chosen)
        by_target = [jnp.concatenate(by_slot[e * pair : (e + 1) * pair]) for e in range(n_dp)]
        yield (pick(by_target, dp),) + tuple(
            swap(pick(by_target, dp ^ j), "dp", j) for j in range(1, n_dp)
        )
        arrived = side_values[0]
        learner_keys.append(jnp.concatenate(in_order(arrived), axis=0))

    side_values, learner_keys = [()], []
    steps = key_steps()

    def side(waited):
        side_values[0] = waited
        return next(steps, None)

    summed(part, n_far * feature_blocks, sums, share, emit, side)
    grad_gain = [
        sum(sums[g * feature_blocks + f] for g in range(n_far)) for f in range(feature_blocks)
    ]
    grad_gain = jnp.concatenate(grad_gain, axis=1)
    grad_gain = grad_gain.reshape(-1)
    return learner_keys[0], out[0], grad_gain


def solution(mesh):
    placed = (
        P(("section", "dp")),
        P(("section", "dp"), None),
        P(),
        P(),
        P(("section", "dp"), "mp"),
        P(("section", "dp"), None),
        P("mp"),
        P("mp", None),
        P(("section", "dp"), "mp"),
    )
    return jax.shard_map(
        body,
        mesh=mesh,
        in_specs=placed,
        out_specs=(P(("section", "dp"), "mp"), P("mp", None), P("mp")),
        check_vma=False,
    )
```

```python
import functools

import jax
import jax.numpy as jnp
from jax import lax
from jax.experimental import pallas as pl
from jax.experimental.pallas import tpu as pltpu
from jax.sharding import PartitionSpec as P

EPSILON = 1e-06
CHUNK_ROWS = 256
LAG = 3
KN = {"groups": (lambda c: [[0], [1, 2], [3, 4], [5], [6], [7]] if c == 8 else [[k] for k in range(c)]), "due": len, "xser": 0, "t1": 0, "t2": 0, "t3": 1, "tA": 0, "tail": 1, "keys": 3, "rpay": (None, 0, 1, 1), "rrecv": (0, 0, 0, 1), "ypay": 0, "yrecv": 0, "ptie": 1}


def swap(value, axis, bit):
    return lax.ppermute(value, axis, [(i, i ^ bit) for i in range(lax.axis_size(axis))])


def pick(values, index):
    chosen = values[0]
    for i in range(1, len(values)):
        chosen = jnp.where(index == i, values[i], chosen)
    return chosen


def to_bfloat16(value):
    return lax.reduce_precision(value, 8, 7).astype(jnp.bfloat16)


def add(left, right):
    return to_bfloat16(left.astype(jnp.float32) + right.astype(jnp.float32))


def end_swap(value):
    return lax.ppermute(value, "section", [(0, 1), (1, 0), (2, 3), (3, 2)])


def middle_swap(value):
    return lax.ppermute(value, "section", [(1, 2), (2, 1), (0, 0), (3, 3)])


def summed(part, count, sums, share, emit, side):
    groups = KN["groups"](count)
    pending = ()
    if lax.axis_size("section") != 4:
        for group in groups:
            found = []
            for k in group:
                value, _ = part(k, None)
                found.append(to_bfloat16(lax.psum(value.astype(jnp.float32), "section")))
            emit(group, share(found))
        while pending is not None:
            pending = side(pending)
        return
    index = lax.axis_index("section")
    inner = (index == 1) | (index == 2)

    parts, arriving, halves, others, totals, results = {}, {}, {}, {}, {}, {}
    for k in range(min(LAG, count)):
        last = parts.get(k - 1)
        parts[k], last = part(k, last)
        if k and KN["ptie"] and last is not None:
            parts[k - 1] = last
        arriving[k] = end_swap(parts[k])
    shares = []
    for k in range(count + LAG):
        tied = {i: totals[i] for i in (k - 2,) if i in totals and KN["t1"]}
        got, tied = lax.optimization_barrier((arriving[k], tied))
        totals.update(tied)
        if k < count:
            halves[k] = add(parts[k], got)
            others[k] = middle_swap(halves[k])
        if LAG + k < count:
            parts[LAG + k], value = part(LAG + k, halves[k])
            if value is not None:
                halves[k] = value
        if k - 1 in others:
            tied = {i: halves[i] for i in (k - 1, k) if i in halves and (i < k or KN["t2"])}
            if KN["tail"] and k >= count:
                other, tied, got = lax.optimization_barrier((others[k - 1], tied, got))
            else:
                other, tied = lax.optimization_barrier((others[k - 1], tied))
            halves.update(tied)
            totals[k - 1] = add(halves[k - 1], other)
        following = k - 1 + LAG
        if LAG <= following < count + LAG:
            value = totals[following - LAG]
            if following < count:
                value = jnp.where(inner, value, parts[following])
            arriving[following] = end_swap(value)
        if k >= LAG:
            results[k - LAG] = jnp.where(inner, totals[k - LAG], got)
            for group in groups:
                if group[-1] == k - LAG:
                    found = [results[i] for i in group]
                    if KN["tA"] and k - 1 in totals:
                        found, totals[k - 1] = lax.optimization_barrier((found, totals[k - 1]))
                    back = KN["xser"]
                    if back and len(shares) >= back and shares[-back] is not None:
                        due, last, values = shares[-back]
                        found, values = lax.optimization_barrier((found, values))
                        shares[-back] = (due, last, values)
                    shares.append((k + KN["due"](group), group, share(found)))
        now = [i for i, entry in enumerate(shares) if entry is not None and entry[0] <= k]
        tied = {i: totals[i] for i in (k - 1,) if i in totals and KN["t3"]}
        if now or (pending is not None and k >= KN["keys"]):
            waited, held, tied = lax.optimization_barrier(
                ([shares[i][2] for i in now], pending if k >= KN["keys"] else (), tied)
            )
            totals.update(tied)
            for i, values in zip(now, waited):
                emit(shares[i][1], values)
                shares[i] = None
            if k >= KN["keys"] and pending is not None:
                pending = side(held)
    for entry in shares:
        if entry is not None:
            emit(entry[1], entry[2])
    while pending is not None:
        pending = side(pending)


def square(block_len, rows, squares, held):
    held[...] = rows[...]
    lane = lax.broadcasted_iota(jnp.int32, (block_len, block_len), 1)
    diagonal = lane == lax.broadcasted_iota(jnp.int32, (block_len, block_len), 0)
    for b in range(squares.shape[0]):
        total = jnp.zeros((block_len, 128), jnp.float32)
        for start in range(0, rows.shape[1], 128):
            value = rows[b * block_len : (b + 1) * block_len, start : start + 128]
            value = value.astype(jnp.float32)
            total = total + value * value
        total = jnp.sum(total, axis=1, keepdims=True)
        squares[b : b + 1, :] = jnp.sum(jnp.where(diagonal, total, 0.0), axis=0, keepdims=True)


def score(lengths, order, hidden, gain, head, rest):
    block_count, block_len = lengths.shape[0], rest.shape[1]
    position = lax.broadcasted_iota(jnp.int32, (1, block_len), 1)
    values = hidden[...].astype(jnp.float32)
    coefficient = (gain[...].astype(jnp.float32) * head[...].astype(jnp.float32)).reshape(1, -1)
    inverse = lax.rsqrt(jnp.mean(values * values, axis=1, keepdims=True) + EPSILON)
    scores = jnp.sum(values * coefficient, axis=1, keepdims=True) * inverse
    for b in range(block_count):
        weight = jnp.where(position < lengths[b], scores[b : b + 1], 0.0)
        rest[b : b + 1, :] = weight.astype(jnp.bfloat16).astype(jnp.float32)
        rest[block_count + b : block_count + b + 1, :] = jnp.full(
            (1, block_len), order[0, b].astype(jnp.float32)
        )


def scale(n_dp, n_mp, width, rest, rows, *refs):
    squares, (inverse, places), pieces = refs[:n_mp], refs[n_mp : n_mp + 2], refs[n_mp + 2 :]
    block_count, block_len = inverse.shape
    dp = lax.axis_index("dp")
    own_width = rows.shape[1] // n_dp
    per_owner = own_width // width
    total = squares[0][...]
    for other in squares[1:]:
        total = total + other[...]
    inverse[...] = lax.rsqrt(total / (rows.shape[1] * n_mp) + EPSILON)
    places[...] = rest[block_count:, :]
    factors = inverse[...] * rest[:block_count, :]
    lane = lax.broadcasted_iota(jnp.int32, (block_len, block_len), 1)
    diagonal = lane == lax.broadcasted_iota(jnp.int32, (block_len, block_len), 0)
    order = [jnp.max(rest[block_count + b : block_count + b + 1, :]) for b in range(block_count)]
    sources = []
    for slot in range(block_count):
        source, factor = 0, factors[0:1]
        for b in range(1, block_count):
            here = order[b] == slot
            source = jnp.where(here, b, source)
            factor = jnp.where(here, factors[b : b + 1], factor)
        factor = jnp.sum(jnp.where(diagonal, factor, 0.0), axis=1, keepdims=True)
        sources.append((pl.multiple_of(source * block_len, block_len), factor))
    for j in range(n_dp):
        for e in range(n_dp):

            @pl.when((dp ^ j) == e)
            def _(j=j, e=e):
                for i in range(per_owner):
                    start = e * own_width + i * width
                    for slot, (source, factor) in enumerate(sources):
                        value = rows[pl.ds(source, block_len), start : start + width]
                        value = value.astype(jnp.float32) * factor
                        place = slice(slot * block_len, (slot + 1) * block_len)
                        pieces[j * per_owner + i][place, :] = value.astype(jnp.bfloat16)


def store(n_dp, g, first, offset, shards, *refs):
    values, gain, weight = refs[0], refs[1], refs[2]
    out, sums, results, semaphores = refs[-4:]
    _, chunk, width = results.shape
    far = lax.axis_index("mp") >> 1
    own_width = weight.shape[0] // n_dp
    column = pl.multiple_of((far ^ g) * width, 128)
    stores = []
    lane = lax.broadcasted_iota(jnp.int32, (128, 128), 1)
    diagonal = lane == lax.broadcasted_iota(jnp.int32, (128, 128), 0)
    for e in range(n_dp):
        start = e * own_width + first
        for at in range(0, chunk, 128):
            gains = gain[:, start + at : start + at + 128]
            gains = jnp.sum(jnp.where(diagonal, gains, 0.0), axis=1, keepdims=True)
            total = values[e, offset + at : offset + at + 128, :].astype(jnp.float32) * (1.0 / shards)
            results[e, at : at + 128, :] = total * gains
            weights = weight[start + at : start + at + 128, pl.ds(column, width)]
            total = total * weights.astype(jnp.float32)
            total = jnp.sum(total, axis=1, keepdims=True)
            total = jnp.sum(jnp.where(diagonal, total, 0.0), axis=0, keepdims=True)
            sums[e : e + 1, at : at + 128] = total
            copy = pltpu.make_async_copy(
                results.at[e, pl.ds(at, 128)],
                out.at[pl.ds(start + at, 128), pl.ds(column, width)],
                semaphores.at[e, at // 128],
            )
            copy.start()
            stores.append(copy)
    for copy in stores:
        copy.wait()


def body(
    lengths,
    final_hidden,
    score_gain,
    score_head,
    policy_input,
    block_order,
    norm_gain,
    key_weight,
    key_cotangent,
):
    n_section, n_dp, n_mp = (lax.axis_size(name) for name in ("section", "dp", "mp"))
    dp, mp = lax.axis_index("dp"), lax.axis_index("mp")
    block_count = lengths.shape[0]
    tokens, local_width = policy_input.shape
    block_len = tokens // block_count
    pair = block_count // n_dp
    columns = key_cotangent.shape[1]
    own_width = local_width // n_dp
    chunk = min(CHUNK_ROWS, own_width)
    feature_blocks = own_width // chunk
    n_far = n_mp // 2
    far, core = mp >> 1, mp & 1

    def in_order(values):
        return [pick(values, dp ^ e) for e in range(n_dp)]

    vmem, smem = pl.BlockSpec(memory_space=pltpu.VMEM), pl.BlockSpec(memory_space=pltpu.SMEM)
    hbm = pl.BlockSpec(memory_space=pltpu.MemorySpace.HBM)
    squares, held = pl.pallas_call(
        functools.partial(square, block_len),
        out_shape=[
            jax.ShapeDtypeStruct((block_count, block_len), jnp.float32),
            jax.ShapeDtypeStruct(policy_input.shape, policy_input.dtype),
        ],
        in_specs=[vmem],
        out_specs=[vmem] * 2,
        compiler_params=pltpu.CompilerParams(vmem_limit_bytes=32 * 2**20),
        name="square",
    )(policy_input)
    squares = [squares] + [swap(squares, "mp", j) for j in range(1, n_mp)]
    cotangents, squares[0] = lax.optimization_barrier((key_cotangent, squares[0]))
    cotangents = [cotangents] + [swap(cotangents, "dp", j) for j in range(1, n_dp)]
    rest = pl.pallas_call(
        score,
        out_shape=jax.ShapeDtypeStruct((2 * block_count, block_len), jnp.float32),
        in_specs=[smem, smem, vmem, vmem, vmem],
        out_specs=vmem,
        name="score",
    )(lengths, block_order, final_hidden, score_gain, score_head)
    inverse, places, *pieces = pl.pallas_call(
        functools.partial(scale, n_dp, n_mp, chunk),
        out_shape=[jax.ShapeDtypeStruct((block_count, block_len), jnp.float32)] * 2
        + [jax.ShapeDtypeStruct((tokens, chunk), jnp.bfloat16)] * (n_dp * feature_blocks),
        in_specs=[vmem] * (2 + n_mp),
        out_specs=[vmem] * (2 + n_dp * feature_blocks),
        compiler_params=pltpu.CompilerParams(vmem_limit_bytes=32 * 2**20),
        name="scale",
    )(rest, held, *squares)

    cotangents, inverse = lax.optimization_barrier((cotangents, inverse))
    cotangents = jnp.concatenate(in_order(cotangents), axis=0)
    def both_cores(near):
        other = swap(near, "mp", 1)
        cotangent = jnp.concatenate([pick([near, other], core), pick([other, near], core)], axis=1)
        cotangent = cotangent.reshape(n_dp, n_dp, tokens // n_dp, 2 * columns)
        return cotangent.transpose(1, 0, 2, 3).reshape(n_dp * tokens, 2 * columns)

    ready, moved, first = {}, {}, {}

    def send(f):
        got = [pieces[f]]
        for j in range(1, n_dp):
            piece = pieces[j * feature_blocks + f]
            tie = KN["rpay"][f] if n_dp == 2 else None
            if tie is not None:
                piece, first[tie] = lax.optimization_barrier((piece, first[tie]))
            got.append(swap(piece, "dp", j))
        return got

    def columns_of(g, value):
        near = cotangents
        if g:
            if KN["ypay"] is not None:
                near, first[KN["ypay"]] = lax.optimization_barrier((near, first[KN["ypay"]]))
            near = swap(near, "mp", 2 * g)
            if KN["yrecv"] and value is not None:
                near, value = lax.optimization_barrier((near, value))
        return both_cores(near), value

    def part(k, value):
        g, f = divmod(k, feature_blocks)
        if g not in ready:
            ready[g], value = columns_of(g, value)
        if f not in moved:
            got = send(f)
            if not f:
                got, ready[0] = lax.optimization_barrier((got, ready[0]))
            elif KN["rrecv"][f] and value is not None:
                got, value = lax.optimization_barrier((got, value))
            moved[f] = jnp.concatenate(in_order(got), axis=0)
        found = to_bfloat16(
            lax.dot_general(
                moved[f], ready[g], (((0,), (0,)), ((), ())), preferred_element_type=jnp.float32
            )
        )
        if k < 2:
            first[k] = found
        return found, value

    shards = n_section * n_dp
    out = []
    sums = {}

    def share(values):
        values = jnp.concatenate(values, axis=0)
        if n_dp == 2:
            return (values, swap(values, "dp", 1))
        return (lax.all_gather(values, "dp"),)

    def emit(group, values):
        values, late_gain = lax.optimization_barrier((values, norm_gain))
        gain = late_gain.astype(jnp.float32)[None, :]
        if len(values) == 2:
            values = jnp.stack(in_order(values))
        else:
            (values,) = values
        for i, k in enumerate(group):
            g, f = divmod(k, feature_blocks)
            before = tuple(out)
            result, total = pl.pallas_call(
                functools.partial(store, n_dp, g, f * chunk, i * chunk, shards),
                out_shape=[
                    jax.ShapeDtypeStruct((local_width, n_mp * columns), jnp.float32),
                    jax.ShapeDtypeStruct((n_dp, chunk), jnp.float32),
                ],
                in_specs=[vmem] * 3 + [hbm] * len(before),
                out_specs=[hbm, vmem],
                input_output_aliases={3: 0} if before else {},
                scratch_shapes=[
                    pltpu.VMEM((n_dp, chunk, 2 * columns), jnp.float32),
                    pltpu.SemaphoreType.DMA((n_dp, chunk // 128)),
                ],
                compiler_params=pltpu.CompilerParams(vmem_limit_bytes=32 * 2**20),
                name="store",
            )(values, gain, key_weight, *before)
            out[:] = [result]
            sums[k] = total

    def key_steps():
        yield (inverse, norm_gain)
        late_inverse, late_gain = side_values[0]
        gain = late_gain.astype(jnp.float32)[None, :]
        normed = held.astype(jnp.float32) * late_inverse.reshape(-1, 1) * gain
        normed = lax.optimization_barrier(normed.astype(jnp.bfloat16))
        partial = jnp.dot(normed, key_weight, preferred_element_type=jnp.float32)
        yield (partial,)
        (partial,) = side_values[0]
        cut = [partial[:, i * columns : (i + 1) * columns] for i in range(n_mp)]
        own = pick(cut, mp)
        yield (own,) + tuple(
            swap(pick(cut, mp ^ j).astype(jnp.bfloat16), "mp", j) for j in range(1, n_mp)
        )
        own, *others = side_values[0]
        keys = own + sum(other.astype(jnp.float32) for other in others)
        keys = keys.astype(jnp.bfloat16).reshape(block_count, block_len, columns)
        by_slot = []
        for slot in range(block_count):
            chosen = keys[0]
            for b in range(1, block_count):
                chosen = jnp.where(places[b][:, None] == slot, keys[b], chosen)
            by_slot.append(chosen)
        by_target = [jnp.concatenate(by_slot[e * pair : (e + 1) * pair]) for e in range(n_dp)]
        yield (pick(by_target, dp),) + tuple(
            swap(pick(by_target, dp ^ j), "dp", j) for j in range(1, n_dp)
        )
        arrived = side_values[0]
        learner_keys.append(jnp.concatenate(in_order(arrived), axis=0))

    side_values, learner_keys = [()], []
    steps = key_steps()

    def side(waited):
        side_values[0] = waited
        return next(steps, None)

    summed(part, n_far * feature_blocks, sums, share, emit, side)
    grad_gain = [
        sum(sums[g * feature_blocks + f] for g in range(n_far)) for f in range(feature_blocks)
    ]
    grad_gain = jnp.concatenate(grad_gain, axis=1)
    grad_gain = grad_gain.reshape(-1)
    return learner_keys[0], out[0], grad_gain


def solution(mesh):
    placed = (
        P(("section", "dp")),
        P(("section", "dp"), None),
        P(),
        P(),
        P(("section", "dp"), "mp"),
        P(("section", "dp"), None),
        P("mp"),
        P("mp", None),
        P(("section", "dp"), "mp"),
    )
    return jax.shard_map(
        body,
        mesh=mesh,
        in_specs=placed,
        out_specs=(P(("section", "dp"), "mp"), P("mp", None), P("mp")),
        check_vma=False,
    )
```

```python
import functools

import jax
import jax.numpy as jnp
from jax import lax
from jax.experimental import pallas as pl
from jax.experimental.pallas import tpu as pltpu
from jax.sharding import PartitionSpec as P

EPSILON = 1e-06
CHUNK_ROWS = 256
LAG = 3
KEYS_STEP = 3


def swap(value, axis, bit):
    return lax.ppermute(value, axis, [(i, i ^ bit) for i in range(lax.axis_size(axis))])


def pick(values, index):
    chosen = values[0]
    for i in range(1, len(values)):
        chosen = jnp.where(index == i, values[i], chosen)
    return chosen


def to_bfloat16(value):
    return lax.reduce_precision(value, 8, 7).astype(jnp.bfloat16)


def add(left, right):
    return to_bfloat16(left.astype(jnp.float32) + right.astype(jnp.float32))


def end_swap(value):
    return lax.ppermute(value, "section", [(0, 1), (1, 0), (2, 3), (3, 2)])


def middle_swap(value):
    return lax.ppermute(value, "section", [(1, 2), (2, 1), (0, 0), (3, 3)])


def summed(part, count, sums, share, emit, side):
    groups = [[k] for k in range(count)]
    if count == 8:
        groups = [[0], [1, 2], [3, 4], [5], [6], [7]]
    pending = ()
    if lax.axis_size("section") != 4:
        for group in groups:
            found = []
            for k in group:
                value, _ = part(k, None)
                found.append(to_bfloat16(lax.psum(value.astype(jnp.float32), "section")))
            emit(group, share(found))
        while pending is not None:
            pending = side(pending)
        return
    index = lax.axis_index("section")
    inner = (index == 1) | (index == 2)

    parts, arriving, halves, others, totals, results = {}, {}, {}, {}, {}, {}
    for k in range(min(LAG, count)):
        last = parts.get(k - 1)
        parts[k], last = part(k, last)
        if last is not None:
            parts[k - 1] = last
        arriving[k] = end_swap(parts[k])
    shares = []
    for k in range(count + LAG):
        got = lax.optimization_barrier(arriving[k])
        if k < count:
            halves[k] = add(parts[k], got)
            others[k] = middle_swap(halves[k])
        if LAG + k < count:
            parts[LAG + k], value = part(LAG + k, halves[k])
            if value is not None:
                halves[k] = value
        if k - 1 in others:
            tied = (others[k - 1], halves[k - 1])
            if k >= count:
                other, half, got = lax.optimization_barrier(tied + (got,))
            else:
                other, half = lax.optimization_barrier(tied)
            totals[k - 1] = add(half, other)
        following = k - 1 + LAG
        if LAG <= following < count + LAG:
            value = totals[following - LAG]
            if following < count:
                value = jnp.where(inner, value, parts[following])
            arriving[following] = end_swap(value)
        if k >= LAG:
            results[k - LAG] = jnp.where(inner, totals[k - LAG], got)
            for group in groups:
                if group[-1] == k - LAG:
                    shares.append((k + 2, group, share([results[i] for i in group])))
        now = [i for i, entry in enumerate(shares) if entry is not None and entry[0] <= k]
        tied = {i: totals[i] for i in (k - 1,) if i in totals}
        if now or (pending is not None and k >= KEYS_STEP):
            waited, held, tied = lax.optimization_barrier(
                ([shares[i][2] for i in now], pending if k >= KEYS_STEP else (), tied)
            )
            totals.update(tied)
            for i, values in zip(now, waited):
                emit(shares[i][1], values)
                shares[i] = None
            if k >= KEYS_STEP and pending is not None:
                pending = side(held)
    for entry in shares:
        if entry is not None:
            emit(entry[1], entry[2])
    while pending is not None:
        pending = side(pending)


def square(block_len, rows, squares, held):
    held[...] = rows[...]
    lane = lax.broadcasted_iota(jnp.int32, (block_len, block_len), 1)
    diagonal = lane == lax.broadcasted_iota(jnp.int32, (block_len, block_len), 0)
    for b in range(squares.shape[0]):
        total = jnp.zeros((block_len, 128), jnp.float32)
        for start in range(0, rows.shape[1], 128):
            value = rows[b * block_len : (b + 1) * block_len, start : start + 128]
            value = value.astype(jnp.float32)
            total = total + value * value
        total = jnp.sum(total, axis=1, keepdims=True)
        squares[b : b + 1, :] = jnp.sum(jnp.where(diagonal, total, 0.0), axis=0, keepdims=True)


def score(lengths, order, hidden, gain, head, rest):
    block_count, block_len = lengths.shape[0], rest.shape[1]
    position = lax.broadcasted_iota(jnp.int32, (1, block_len), 1)
    values = hidden[...].astype(jnp.float32)
    coefficient = (gain[...].astype(jnp.float32) * head[...].astype(jnp.float32)).reshape(1, -1)
    inverse = lax.rsqrt(jnp.mean(values * values, axis=1, keepdims=True) + EPSILON)
    scores = jnp.sum(values * coefficient, axis=1, keepdims=True) * inverse
    for b in range(block_count):
        weight = jnp.where(position < lengths[b], scores[b : b + 1], 0.0)
        rest[b : b + 1, :] = weight.astype(jnp.bfloat16).astype(jnp.float32)
        rest[block_count + b : block_count + b + 1, :] = jnp.full(
            (1, block_len), order[0, b].astype(jnp.float32)
        )


def scale(n_dp, n_mp, width, rest, rows, *refs):
    squares, (inverse, places), pieces = refs[:n_mp], refs[n_mp : n_mp + 2], refs[n_mp + 2 :]
    block_count, block_len = inverse.shape
    dp = lax.axis_index("dp")
    own_width = rows.shape[1] // n_dp
    per_owner = own_width // width
    total = squares[0][...]
    for other in squares[1:]:
        total = total + other[...]
    inverse[...] = lax.rsqrt(total / (rows.shape[1] * n_mp) + EPSILON)
    places[...] = rest[block_count:, :]
    factors = inverse[...] * rest[:block_count, :]
    lane = lax.broadcasted_iota(jnp.int32, (block_len, block_len), 1)
    diagonal = lane == lax.broadcasted_iota(jnp.int32, (block_len, block_len), 0)
    order = [jnp.max(rest[block_count + b : block_count + b + 1, :]) for b in range(block_count)]
    sources = []
    for slot in range(block_count):
        source, factor = 0, factors[0:1]
        for b in range(1, block_count):
            here = order[b] == slot
            source = jnp.where(here, b, source)
            factor = jnp.where(here, factors[b : b + 1], factor)
        factor = jnp.sum(jnp.where(diagonal, factor, 0.0), axis=1, keepdims=True)
        sources.append((pl.multiple_of(source * block_len, block_len), factor))
    for j in range(n_dp):
        for e in range(n_dp):

            @pl.when((dp ^ j) == e)
            def _(j=j, e=e):
                for i in range(per_owner):
                    start = e * own_width + i * width
                    for slot, (source, factor) in enumerate(sources):
                        value = rows[pl.ds(source, block_len), start : start + width]
                        value = value.astype(jnp.float32) * factor
                        place = slice(slot * block_len, (slot + 1) * block_len)
                        pieces[j * per_owner + i][place, :] = value.astype(jnp.bfloat16)


def store(n_dp, g, first, offset, shards, *refs):
    values, gain, weight = refs[0], refs[1], refs[2]
    out, sums, results, semaphores = refs[-4:]
    _, chunk, width = results.shape
    far = lax.axis_index("mp") >> 1
    own_width = weight.shape[0] // n_dp
    column = pl.multiple_of((far ^ g) * width, 128)
    stores = []
    lane = lax.broadcasted_iota(jnp.int32, (128, 128), 1)
    diagonal = lane == lax.broadcasted_iota(jnp.int32, (128, 128), 0)
    for e in range(n_dp):
        start = e * own_width + first
        for at in range(0, chunk, 128):
            gains = gain[:, start + at : start + at + 128]
            gains = jnp.sum(jnp.where(diagonal, gains, 0.0), axis=1, keepdims=True)
            total = values[e, offset + at : offset + at + 128, :].astype(jnp.float32) * (1.0 / shards)
            results[e, at : at + 128, :] = total * gains
            weights = weight[start + at : start + at + 128, pl.ds(column, width)]
            total = total * weights.astype(jnp.float32)
            total = jnp.sum(total, axis=1, keepdims=True)
            total = jnp.sum(jnp.where(diagonal, total, 0.0), axis=0, keepdims=True)
            sums[e : e + 1, at : at + 128] = total
            copy = pltpu.make_async_copy(
                results.at[e, pl.ds(at, 128)],
                out.at[pl.ds(start + at, 128), pl.ds(column, width)],
                semaphores.at[e, at // 128],
            )
            copy.start()
            stores.append(copy)
    for copy in stores:
        copy.wait()


def body(
    lengths,
    final_hidden,
    score_gain,
    score_head,
    policy_input,
    block_order,
    norm_gain,
    key_weight,
    key_cotangent,
):
    n_section, n_dp, n_mp = (lax.axis_size(name) for name in ("section", "dp", "mp"))
    dp, mp = lax.axis_index("dp"), lax.axis_index("mp")
    block_count = lengths.shape[0]
    tokens, local_width = policy_input.shape
    block_len = tokens // block_count
    pair = block_count // n_dp
    columns = key_cotangent.shape[1]
    own_width = local_width // n_dp
    chunk = min(CHUNK_ROWS, own_width)
    feature_blocks = own_width // chunk
    n_far = n_mp // 2
    far, core = mp >> 1, mp & 1

    def in_order(values):
        return [pick(values, dp ^ e) for e in range(n_dp)]

    vmem, smem = pl.BlockSpec(memory_space=pltpu.VMEM), pl.BlockSpec(memory_space=pltpu.SMEM)
    hbm = pl.BlockSpec(memory_space=pltpu.MemorySpace.HBM)
    squares, held = pl.pallas_call(
        functools.partial(square, block_len),
        out_shape=[
            jax.ShapeDtypeStruct((block_count, block_len), jnp.float32),
            jax.ShapeDtypeStruct(policy_input.shape, policy_input.dtype),
        ],
        in_specs=[vmem],
        out_specs=[vmem] * 2,
        compiler_params=pltpu.CompilerParams(vmem_limit_bytes=32 * 2**20),
        name="square",
    )(policy_input)
    squares = [squares] + [swap(squares, "mp", j) for j in range(1, n_mp)]
    cotangents, squares[0] = lax.optimization_barrier((key_cotangent, squares[0]))
    cotangents = [cotangents] + [swap(cotangents, "dp", j) for j in range(1, n_dp)]
    rest = pl.pallas_call(
        score,
        out_shape=jax.ShapeDtypeStruct((2 * block_count, block_len), jnp.float32),
        in_specs=[smem, smem, vmem, vmem, vmem],
        out_specs=vmem,
        name="score",
    )(lengths, block_order, final_hidden, score_gain, score_head)
    inverse, places, *pieces = pl.pallas_call(
        functools.partial(scale, n_dp, n_mp, chunk),
        out_shape=[jax.ShapeDtypeStruct((block_count, block_len), jnp.float32)] * 2
        + [jax.ShapeDtypeStruct((tokens, chunk), jnp.bfloat16)] * (n_dp * feature_blocks),
        in_specs=[vmem] * (2 + n_mp),
        out_specs=[vmem] * (2 + n_dp * feature_blocks),
        compiler_params=pltpu.CompilerParams(vmem_limit_bytes=32 * 2**20),
        name="scale",
    )(rest, held, *squares)

    cotangents, inverse = lax.optimization_barrier((cotangents, inverse))
    cotangents = jnp.concatenate(in_order(cotangents), axis=0)
    def both_cores(near):
        other = swap(near, "mp", 1)
        cotangent = jnp.concatenate([pick([near, other], core), pick([other, near], core)], axis=1)
        cotangent = cotangent.reshape(n_dp, n_dp, tokens // n_dp, 2 * columns)
        return cotangent.transpose(1, 0, 2, 3).reshape(n_dp * tokens, 2 * columns)

    ready, moved, first = {}, {}, {}

    def send(f):
        got = [pieces[f]]
        for j in range(1, n_dp):
            piece = pieces[j * feature_blocks + f]
            tie = min(f - 1, 1)
            if tie in first:
                piece, first[tie] = lax.optimization_barrier((piece, first[tie]))
            got.append(swap(piece, "dp", j))
        return got

    def columns_of(g):
        near = cotangents
        if g:
            near, first[0] = lax.optimization_barrier((near, first[0]))
            near = swap(near, "mp", 2 * g)
        return both_cores(near)

    def part(k, value):
        g, f = divmod(k, feature_blocks)
        if g not in ready:
            ready[g] = columns_of(g)
        if f not in moved:
            got = send(f)
            if not f:
                got, ready[0] = lax.optimization_barrier((got, ready[0]))
            elif f >= LAG and value is not None:
                got, value = lax.optimization_barrier((got, value))
            moved[f] = jnp.concatenate(in_order(got), axis=0)
        found = to_bfloat16(
            lax.dot_general(
                moved[f], ready[g], (((0,), (0,)), ((), ())), preferred_element_type=jnp.float32
            )
        )
        if k < 2:
            first[k] = found
        return found, value

    shards = n_section * n_dp
    out = []
    sums = {}

    def share(values):
        values = jnp.concatenate(values, axis=0)
        if n_dp == 2:
            return (values, swap(values, "dp", 1))
        return (lax.all_gather(values, "dp"),)

    def emit(group, values):
        values, late_gain = lax.optimization_barrier((values, norm_gain))
        gain = late_gain.astype(jnp.float32)[None, :]
        if len(values) == 2:
            values = jnp.stack(in_order(values))
        else:
            (values,) = values
        for i, k in enumerate(group):
            g, f = divmod(k, feature_blocks)
            before = tuple(out)
            result, total = pl.pallas_call(
                functools.partial(store, n_dp, g, f * chunk, i * chunk, shards),
                out_shape=[
                    jax.ShapeDtypeStruct((local_width, n_mp * columns), jnp.float32),
                    jax.ShapeDtypeStruct((n_dp, chunk), jnp.float32),
                ],
                in_specs=[vmem] * 3 + [hbm] * len(before),
                out_specs=[hbm, vmem],
                input_output_aliases={3: 0} if before else {},
                scratch_shapes=[
                    pltpu.VMEM((n_dp, chunk, 2 * columns), jnp.float32),
                    pltpu.SemaphoreType.DMA((n_dp, chunk // 128)),
                ],
                compiler_params=pltpu.CompilerParams(vmem_limit_bytes=32 * 2**20),
                name="store",
            )(values, gain, key_weight, *before)
            out[:] = [result]
            sums[k] = total

    def key_steps():
        yield (inverse, norm_gain)
        late_inverse, late_gain = side_values[0]
        gain = late_gain.astype(jnp.float32)[None, :]
        normed = held.astype(jnp.float32) * late_inverse.reshape(-1, 1) * gain
        normed = lax.optimization_barrier(normed.astype(jnp.bfloat16))
        partial = jnp.dot(normed, key_weight, preferred_element_type=jnp.float32)
        yield (partial,)
        (partial,) = side_values[0]
        cut = [partial[:, i * columns : (i + 1) * columns] for i in range(n_mp)]
        own = pick(cut, mp)
        yield (own,) + tuple(
            swap(pick(cut, mp ^ j).astype(jnp.bfloat16), "mp", j) for j in range(1, n_mp)
        )
        own, *others = side_values[0]
        keys = own + sum(other.astype(jnp.float32) for other in others)
        keys = keys.astype(jnp.bfloat16).reshape(block_count, block_len, columns)
        by_slot = []
        for slot in range(block_count):
            chosen = keys[0]
            for b in range(1, block_count):
                chosen = jnp.where(places[b][:, None] == slot, keys[b], chosen)
            by_slot.append(chosen)
        by_target = [jnp.concatenate(by_slot[e * pair : (e + 1) * pair]) for e in range(n_dp)]
        yield (pick(by_target, dp),) + tuple(
            swap(pick(by_target, dp ^ j), "dp", j) for j in range(1, n_dp)
        )
        arrived = side_values[0]
        learner_keys.append(jnp.concatenate(in_order(arrived), axis=0))

    side_values, learner_keys = [()], []
    steps = key_steps()

    def side(waited):
        side_values[0] = waited
        return next(steps, None)

    summed(part, n_far * feature_blocks, sums, share, emit, side)
    grad_gain = [
        sum(sums[g * feature_blocks + f] for g in range(n_far)) for f in range(feature_blocks)
    ]
    grad_gain = jnp.concatenate(grad_gain, axis=1)
    grad_gain = grad_gain.reshape(-1)
    return learner_keys[0], out[0], grad_gain


def solution(mesh):
    placed = (
        P(("section", "dp")),
        P(("section", "dp"), None),
        P(),
        P(),
        P(("section", "dp"), "mp"),
        P(("section", "dp"), None),
        P("mp"),
        P("mp", None),
        P(("section", "dp"), "mp"),
    )
    return jax.shard_map(
        body,
        mesh=mesh,
        in_specs=placed,
        out_specs=(P(("section", "dp"), "mp"), P("mp", None), P("mp")),
        check_vma=False,
    )
```

```python
import functools

import jax
import jax.numpy as jnp
from jax import lax
from jax.experimental import pallas as pl
from jax.experimental.pallas import tpu as pltpu
from jax.sharding import PartitionSpec as P

EPSILON = 1e-06
CHUNK_ROWS = 256
LAG = 3
KEYS_STEP = 4


def swap(value, axis, bit):
    return lax.ppermute(value, axis, [(i, i ^ bit) for i in range(lax.axis_size(axis))])


def pick(values, index):
    chosen = values[0]
    for i in range(1, len(values)):
        chosen = jnp.where(index == i, values[i], chosen)
    return chosen


def to_bfloat16(value):
    return lax.reduce_precision(value, 8, 7).astype(jnp.bfloat16)


def add(left, right):
    return to_bfloat16(left.astype(jnp.float32) + right.astype(jnp.float32))


def end_swap(value):
    return lax.ppermute(value, "section", [(0, 1), (1, 0), (2, 3), (3, 2)])


def middle_swap(value):
    return lax.ppermute(value, "section", [(1, 2), (2, 1), (0, 0), (3, 3)])


def summed(part, count, sums, share, emit, side):
    groups = [[k] for k in range(count)]
    if count == 8:
        groups = [[0], [1, 2], [3, 4], [5], [6], [7]]
    pending = ()
    if lax.axis_size("section") != 4:
        for group in groups:
            found = []
            for k in group:
                value, _ = part(k, None)
                found.append(to_bfloat16(lax.psum(value.astype(jnp.float32), "section")))
            emit(group, share(found))
        while pending is not None:
            pending = side(pending)
        return
    index = lax.axis_index("section")
    inner = (index == 1) | (index == 2)

    parts, arriving, halves, others, totals, results = {}, {}, {}, {}, {}, {}
    for k in range(min(LAG, count)):
        last = parts.get(k - 1)
        parts[k], last = part(k, last)
        if last is not None:
            parts[k - 1] = last
        arriving[k] = end_swap(parts[k])
    shares = []
    for k in range(count + LAG):
        got = lax.optimization_barrier(arriving[k])
        if k < count:
            halves[k] = add(parts[k], got)
            others[k] = middle_swap(halves[k])
        if LAG + k < count:
            parts[LAG + k], value = part(LAG + k, halves[k])
            if value is not None:
                halves[k] = value
        if k - 1 in others:
            tied = (others[k - 1], halves[k - 1])
            if k >= count:
                other, half, got = lax.optimization_barrier(tied + (got,))
            else:
                other, half = lax.optimization_barrier(tied)
            totals[k - 1] = add(half, other)
        following = k - 1 + LAG
        if LAG <= following < count + LAG:
            value = totals[following - LAG]
            if following < count:
                value = jnp.where(inner, value, parts[following])
            arriving[following] = end_swap(value)
        if k >= LAG:
            results[k - LAG] = jnp.where(inner, totals[k - LAG], got)
            for group in groups:
                if group[-1] == k - LAG:
                    shares.append((k + 2, group, share([results[i] for i in group])))
        now = [i for i, entry in enumerate(shares) if entry is not None and entry[0] <= k]
        tied = {i: totals[i] for i in (k - 1,) if i in totals}
        if now or (pending is not None and k >= KEYS_STEP):
            waited, held, tied = lax.optimization_barrier(
                ([shares[i][2] for i in now], pending if k >= KEYS_STEP else (), tied)
            )
            totals.update(tied)
            for i, values in zip(now, waited):
                emit(shares[i][1], values)
                shares[i] = None
            if k >= KEYS_STEP and pending is not None:
                pending = side(held)
    for entry in shares:
        if entry is not None:
            emit(entry[1], entry[2])
    while pending is not None:
        pending = side(pending)


def square(block_len, rows, squares, held):
    held[...] = rows[...]
    lane = lax.broadcasted_iota(jnp.int32, (block_len, block_len), 1)
    diagonal = lane == lax.broadcasted_iota(jnp.int32, (block_len, block_len), 0)
    for b in range(squares.shape[0]):
        total = jnp.zeros((block_len, 128), jnp.float32)
        for start in range(0, rows.shape[1], 128):
            value = rows[b * block_len : (b + 1) * block_len, start : start + 128]
            value = value.astype(jnp.float32)
            total = total + value * value
        total = jnp.sum(total, axis=1, keepdims=True)
        squares[b : b + 1, :] = jnp.sum(jnp.where(diagonal, total, 0.0), axis=0, keepdims=True)


def score(lengths, order, hidden, gain, head, rest):
    block_count, block_len = lengths.shape[0], rest.shape[1]
    position = lax.broadcasted_iota(jnp.int32, (1, block_len), 1)
    values = hidden[...].astype(jnp.float32)
    coefficient = (gain[...].astype(jnp.float32) * head[...].astype(jnp.float32)).reshape(1, -1)
    inverse = lax.rsqrt(jnp.mean(values * values, axis=1, keepdims=True) + EPSILON)
    scores = jnp.sum(values * coefficient, axis=1, keepdims=True) * inverse
    for b in range(block_count):
        weight = jnp.where(position < lengths[b], scores[b : b + 1], 0.0)
        rest[b : b + 1, :] = weight.astype(jnp.bfloat16).astype(jnp.float32)
        rest[block_count + b : block_count + b + 1, :] = jnp.full(
            (1, block_len), order[0, b].astype(jnp.float32)
        )


def scale(n_dp, n_mp, width, rest, rows, *refs):
    squares, (inverse, places), pieces = refs[:n_mp], refs[n_mp : n_mp + 2], refs[n_mp + 2 :]
    block_count, block_len = inverse.shape
    dp = lax.axis_index("dp")
    own_width = rows.shape[1] // n_dp
    per_owner = own_width // width
    total = squares[0][...]
    for other in squares[1:]:
        total = total + other[...]
    inverse[...] = lax.rsqrt(total / (rows.shape[1] * n_mp) + EPSILON)
    places[...] = rest[block_count:, :]
    factors = inverse[...] * rest[:block_count, :]
    lane = lax.broadcasted_iota(jnp.int32, (block_len, block_len), 1)
    diagonal = lane == lax.broadcasted_iota(jnp.int32, (block_len, block_len), 0)
    order = [jnp.max(rest[block_count + b : block_count + b + 1, :]) for b in range(block_count)]
    sources = []
    for slot in range(block_count):
        source, factor = 0, factors[0:1]
        for b in range(1, block_count):
            here = order[b] == slot
            source = jnp.where(here, b, source)
            factor = jnp.where(here, factors[b : b + 1], factor)
        factor = jnp.sum(jnp.where(diagonal, factor, 0.0), axis=1, keepdims=True)
        sources.append((pl.multiple_of(source * block_len, block_len), factor))
    for j in range(n_dp):
        for e in range(n_dp):

            @pl.when((dp ^ j) == e)
            def _(j=j, e=e):
                for i in range(per_owner):
                    start = e * own_width + i * width
                    for slot, (source, factor) in enumerate(sources):
                        value = rows[pl.ds(source, block_len), start : start + width]
                        value = value.astype(jnp.float32) * factor
                        place = slice(slot * block_len, (slot + 1) * block_len)
                        pieces[j * per_owner + i][place, :] = value.astype(jnp.bfloat16)


def store(n_dp, g, first, offset, shards, *refs):
    values, gain, weight = refs[0], refs[1], refs[2]
    out, sums, results, semaphores = refs[-4:]
    _, chunk, width = results.shape
    far = lax.axis_index("mp") >> 1
    own_width = weight.shape[0] // n_dp
    column = pl.multiple_of((far ^ g) * width, 128)
    stores = []
    lane = lax.broadcasted_iota(jnp.int32, (128, 128), 1)
    diagonal = lane == lax.broadcasted_iota(jnp.int32, (128, 128), 0)
    for e in range(n_dp):
        start = e * own_width + first
        for at in range(0, chunk, 128):
            gains = gain[:, start + at : start + at + 128]
            gains = jnp.sum(jnp.where(diagonal, gains, 0.0), axis=1, keepdims=True)
            total = values[e, offset + at : offset + at + 128, :].astype(jnp.float32) * (1.0 / shards)
            results[e, at : at + 128, :] = total * gains
            weights = weight[start + at : start + at + 128, pl.ds(column, width)]
            total = total * weights.astype(jnp.float32)
            total = jnp.sum(total, axis=1, keepdims=True)
            total = jnp.sum(jnp.where(diagonal, total, 0.0), axis=0, keepdims=True)
            sums[e : e + 1, at : at + 128] = total
            copy = pltpu.make_async_copy(
                results.at[e, pl.ds(at, 128)],
                out.at[pl.ds(start + at, 128), pl.ds(column, width)],
                semaphores.at[e, at // 128],
            )
            copy.start()
            stores.append(copy)
    for copy in stores:
        copy.wait()


def body(
    lengths,
    final_hidden,
    score_gain,
    score_head,
    policy_input,
    block_order,
    norm_gain,
    key_weight,
    key_cotangent,
):
    n_section, n_dp, n_mp = (lax.axis_size(name) for name in ("section", "dp", "mp"))
    dp, mp = lax.axis_index("dp"), lax.axis_index("mp")
    block_count = lengths.shape[0]
    tokens, local_width = policy_input.shape
    block_len = tokens // block_count
    pair = block_count // n_dp
    columns = key_cotangent.shape[1]
    own_width = local_width // n_dp
    chunk = min(CHUNK_ROWS, own_width)
    feature_blocks = own_width // chunk
    n_far = n_mp // 2
    far, core = mp >> 1, mp & 1

    def in_order(values):
        return [pick(values, dp ^ e) for e in range(n_dp)]

    vmem, smem = pl.BlockSpec(memory_space=pltpu.VMEM), pl.BlockSpec(memory_space=pltpu.SMEM)
    hbm = pl.BlockSpec(memory_space=pltpu.MemorySpace.HBM)
    squares, held = pl.pallas_call(
        functools.partial(square, block_len),
        out_shape=[
            jax.ShapeDtypeStruct((block_count, block_len), jnp.float32),
            jax.ShapeDtypeStruct(policy_input.shape, policy_input.dtype),
        ],
        in_specs=[vmem],
        out_specs=[vmem] * 2,
        compiler_params=pltpu.CompilerParams(vmem_limit_bytes=32 * 2**20),
        name="square",
    )(policy_input)
    squares = [squares] + [swap(squares, "mp", j) for j in range(1, n_mp)]
    cotangents, squares[0] = lax.optimization_barrier((key_cotangent, squares[0]))
    cotangents = [cotangents] + [swap(cotangents, "dp", j) for j in range(1, n_dp)]
    rest = pl.pallas_call(
        score,
        out_shape=jax.ShapeDtypeStruct((2 * block_count, block_len), jnp.float32),
        in_specs=[smem, smem, vmem, vmem, vmem],
        out_specs=vmem,
        name="score",
    )(lengths, block_order, final_hidden, score_gain, score_head)
    inverse, places, *pieces = pl.pallas_call(
        functools.partial(scale, n_dp, n_mp, chunk),
        out_shape=[jax.ShapeDtypeStruct((block_count, block_len), jnp.float32)] * 2
        + [jax.ShapeDtypeStruct((tokens, chunk), jnp.bfloat16)] * (n_dp * feature_blocks),
        in_specs=[vmem] * (2 + n_mp),
        out_specs=[vmem] * (2 + n_dp * feature_blocks),
        compiler_params=pltpu.CompilerParams(vmem_limit_bytes=32 * 2**20),
        name="scale",
    )(rest, held, *squares)

    cotangents, inverse = lax.optimization_barrier((cotangents, inverse))
    cotangents = jnp.concatenate(in_order(cotangents), axis=0)
    def both_cores(near):
        other = swap(near, "mp", 1)
        cotangent = jnp.concatenate([pick([near, other], core), pick([other, near], core)], axis=1)
        cotangent = cotangent.reshape(n_dp, n_dp, tokens // n_dp, 2 * columns)
        return cotangent.transpose(1, 0, 2, 3).reshape(n_dp * tokens, 2 * columns)

    ready, moved, first = {}, {}, {}

    def send(f):
        got = [pieces[f]]
        for j in range(1, n_dp):
            piece = pieces[j * feature_blocks + f]
            tie = min(f - 1, 1)
            if tie in first:
                piece, first[tie] = lax.optimization_barrier((piece, first[tie]))
            got.append(swap(piece, "dp", j))
        return got

    def columns_of(g):
        near = cotangents
        if g:
            near, first[0] = lax.optimization_barrier((near, first[0]))
            near = swap(near, "mp", 2 * g)
        return both_cores(near)

    def part(k, value):
        g, f = divmod(k, feature_blocks)
        if g not in ready:
            ready[g] = columns_of(g)
        if f not in moved:
            got = send(f)
            if not f:
                got, ready[0] = lax.optimization_barrier((got, ready[0]))
            elif f >= LAG and value is not None:
                got, value = lax.optimization_barrier((got, value))
            moved[f] = jnp.concatenate(in_order(got), axis=0)
        found = to_bfloat16(
            lax.dot_general(
                moved[f], ready[g], (((0,), (0,)), ((), ())), preferred_element_type=jnp.float32
            )
        )
        if k < 2:
            first[k] = found
        return found, value

    shards = n_section * n_dp
    out = []
    sums = {}

    def share(values):
        values = jnp.concatenate(values, axis=0)
        if n_dp == 2:
            return (values, swap(values, "dp", 1))
        return (lax.all_gather(values, "dp"),)

    def emit(group, values):
        values, late_gain = lax.optimization_barrier((values, norm_gain))
        gain = late_gain.astype(jnp.float32)[None, :]
        if len(values) == 2:
            values = jnp.stack(in_order(values))
        else:
            (values,) = values
        for i, k in enumerate(group):
            g, f = divmod(k, feature_blocks)
            before = tuple(out)
            result, total = pl.pallas_call(
                functools.partial(store, n_dp, g, f * chunk, i * chunk, shards),
                out_shape=[
                    jax.ShapeDtypeStruct((local_width, n_mp * columns), jnp.float32),
                    jax.ShapeDtypeStruct((n_dp, chunk), jnp.float32),
                ],
                in_specs=[vmem] * 3 + [hbm] * len(before),
                out_specs=[hbm, vmem],
                input_output_aliases={3: 0} if before else {},
                scratch_shapes=[
                    pltpu.VMEM((n_dp, chunk, 2 * columns), jnp.float32),
                    pltpu.SemaphoreType.DMA((n_dp, chunk // 128)),
                ],
                compiler_params=pltpu.CompilerParams(vmem_limit_bytes=32 * 2**20),
                name="store",
            )(values, gain, key_weight, *before)
            out[:] = [result]
            sums[k] = total

    def key_steps():
        yield (inverse, norm_gain)
        late_inverse, late_gain = side_values[0]
        gain = late_gain.astype(jnp.float32)[None, :]
        normed = held.astype(jnp.float32) * late_inverse.reshape(-1, 1) * gain
        normed = lax.optimization_barrier(normed.astype(jnp.bfloat16))
        partial = jnp.dot(normed, key_weight, preferred_element_type=jnp.float32)
        yield (partial,)
        (partial,) = side_values[0]
        cut = [partial[:, i * columns : (i + 1) * columns] for i in range(n_mp)]
        own = pick(cut, mp)
        yield (own,) + tuple(
            swap(pick(cut, mp ^ j).astype(jnp.bfloat16), "mp", j) for j in range(1, n_mp)
        )
        own, *others = side_values[0]
        keys = own + sum(other.astype(jnp.float32) for other in others)
        keys = keys.astype(jnp.bfloat16).reshape(block_count, block_len, columns)
        by_slot = []
        for slot in range(block_count):
            chosen = keys[0]
            for b in range(1, block_count):
                chosen = jnp.where(places[b][:, None] == slot, keys[b], chosen)
            by_slot.append(chosen)
        by_target = [jnp.concatenate(by_slot[e * pair : (e + 1) * pair]) for e in range(n_dp)]
        yield (pick(by_target, dp),) + tuple(
            swap(pick(by_target, dp ^ j), "dp", j) for j in range(1, n_dp)
        )
        arrived = side_values[0]
        learner_keys.append(jnp.concatenate(in_order(arrived), axis=0))

    side_values, learner_keys = [()], []
    steps = key_steps()

    def side(waited):
        side_values[0] = waited
        return next(steps, None)

    summed(part, n_far * feature_blocks, sums, share, emit, side)
    grad_gain = [
        sum(sums[g * feature_blocks + f] for g in range(n_far)) for f in range(feature_blocks)
    ]
    grad_gain = jnp.concatenate(grad_gain, axis=1)
    grad_gain = grad_gain.reshape(-1)
    return learner_keys[0], out[0], grad_gain


def solution(mesh):
    placed = (
        P(("section", "dp")),
        P(("section", "dp"), None),
        P(),
        P(),
        P(("section", "dp"), "mp"),
        P(("section", "dp"), None),
        P("mp"),
        P("mp", None),
        P(("section", "dp"), "mp"),
    )
    return jax.shard_map(
        body,
        mesh=mesh,
        in_specs=placed,
        out_specs=(P(("section", "dp"), "mp"), P("mp", None), P("mp")),
        check_vma=False,
    )
```
